32 devices in a mesh: pipe: 4 (over y, x), expert: 8 (over z, core).
Axes of the slice: x: 2, y: 2, z: 4, core: 2. Of those that a mesh axis runs over, the one named last changes fastest.
Arguments:
- hidden_in: bfloat16 [4, 1024, 4096], P('pipe', 'expert'), may hold values from -90 to 90
- out_grad: bfloat16 [4, 1024, 4096], P('pipe', 'expert'), may hold values from -6 to 6
- expert_ids: int32 [4, 1024, 8], P('pipe', 'expert'), may hold values from 0 to 127, as said below
- route_weight: bfloat16 [4, 1024, 8], P('pipe', 'expert'), may hold values from 0.25 to 1
- norm_gain: float32 [4, 4096], P('pipe'), may hold values from 0.25 to 1.75
- w_gate_up: bfloat16 [4, 8, 2, 192, 4096], P('pipe', 'expert'), may hold values from -0.09375 to 0.09375
- w_down: bfloat16 [4, 8, 192, 4096], P('pipe', 'expert'), may hold values from -0.15625 to 0.15625
Outputs:
- handed_grad: bfloat16 [4, 1024, 4096], P('pipe', 'expert')
- grad_gate_up: bfloat16 [4, 8, 2, 192, 4096], P('pipe', 'expert')
- grad_down: bfloat16 [4, 8, 192, 4096], P('pipe', 'expert')
- grad_combine: float32 [4, 1024, 8], P('pipe', 'expert')
The draws below stay inside these ranges and needn't reach their ends.
Inputs may be any that keep to these rules, and one draw needn't show every extreme that they name: `expert_ids`: each token names 8 different experts. In each layer, at most 8 tokens of one aligned block of 128 tokens name any one of the experts 0 to 0, and one of these experts is named by exactly 8 tokens of every block.
All inputs are finite; a program needn't handle non-finite values.
Results may differ from the reference program's by a relative error of at most 0.008.
Values may be sent and summed in bfloat16 or wider, within the bound.
No kernel may reach another device: no remote copies, remote signals or barrier semaphores. Data moves between devices by JAX's collectives and lax.ppermute only.
A program may use at most 128 MiB of HBM per device.

```python
import math
import jax
import jax.numpy as jnp
from jax import lax

D = 4096
FF = 1536
EXPERTS = 128
TOPK = 8
TOK_DEV = 128
F_DEV = 192
EXP_FLY = 1
SLABS = 8
SPECIALIST_CAP = 8
TOKENS = 1024
LAYERS = 4


def draw_hidden_in(key, part):
    key_rows, key_cols, key_base = jax.random.split(key, 3)
    row_scale = jnp.exp(jax.random.uniform(key_rows, (LAYERS, TOKENS, 1), jnp.float32, math.log(0.5), math.log(5.0)))
    col_scale = jnp.exp(jax.random.uniform(key_cols, (LAYERS, 1, D), jnp.float32, math.log(0.3), math.log(3.0)))
    values = jnp.clip(jax.random.normal(key_base, (LAYERS, TOKENS, D), jnp.float32), -6.0, 6.0)
    return (values * row_scale * col_scale).astype(jnp.bfloat16)


def draw_expert_ids(key, part):
    seed_sequence = jax.random.split(key, 6)
    specialist_span = EXP_FLY
    tile_shape_sizes = (LAYERS, SLABS, specialist_span)
    tally_starts = jax.random.randint(seed_sequence[0], tile_shape_sizes, SPECIALIST_CAP // 4, SPECIALIST_CAP // 2 + 1)
    arrival_surges = jax.random.randint(seed_sequence[1], tile_shape_sizes, 0, 8) == 0
    heaviest_specialist = jax.random.randint(seed_sequence[2], (LAYERS, 1, 1), 0, specialist_span)
    specialist_tallies = jnp.where(arrival_surges | (jnp.arange(specialist_span)[None, None, :] == heaviest_specialist), SPECIALIST_CAP, tally_starts)
    scores = jax.random.randint(seed_sequence[3], (LAYERS, SLABS, specialist_span, TOK_DEV), 0, 1 << 20)
    scores = scores * TOK_DEV + jnp.arange(TOK_DEV)
    ranks = jnp.argsort(jnp.argsort(scores, axis=-1), axis=-1)
    member = jnp.swapaxes(ranks < specialist_tallies[..., None], 2, 3)
    marked = jnp.sort(jnp.where(member, jnp.arange(specialist_span), EXPERTS), axis=-1)
    padding = jnp.full((LAYERS, SLABS, TOK_DEV, TOPK - specialist_span), EXPERTS, jnp.int32)
    marked = jnp.concatenate([marked.astype(jnp.int32), padding], axis=-1)
    taken = jnp.sum(member.astype(jnp.int32), axis=-1)[..., None]
    outside_count = EXPERTS - specialist_span
    scores_out = jax.random.randint(seed_sequence[4], (LAYERS, SLABS, TOK_DEV, outside_count), 0, 1 << 20)
    scores_out = scores_out * outside_count + jnp.arange(outside_count)
    outside = jnp.argsort(scores_out, axis=-1)[..., :TOPK] + specialist_span
    slot_range = jnp.arange(TOPK)
    filler = jnp.take_along_axis(outside, jnp.clip(slot_range - taken, 0, TOPK - 1), axis=-1)
    chosen = jnp.where(slot_range < taken, marked, filler)
    scores_slot = jax.random.randint(seed_sequence[5], (LAYERS, SLABS, TOK_DEV, TOPK), 0, 1 << 20) * TOPK + slot_range
    ordering = jnp.argsort(scores_slot, axis=-1)
    chosen = jnp.take_along_axis(chosen, ordering, axis=-1)
    return chosen.reshape(LAYERS, TOKENS, TOPK).astype(jnp.int32)


def level_of(rng, dims, cuts, smallest, largest):
    loudness, own = 1.0, jax.random.fold_in(rng, 6)
    for axis_at, blocks in cuts:
        heights = jnp.exp(jax.random.uniform(jax.random.fold_in(own, axis_at), (blocks,), jnp.float32, smallest / len(cuts), largest / len(cuts)))
        loudness = loudness * jnp.repeat(heights, dims[axis_at] // blocks).reshape([-1 if axis == axis_at else 1 for axis in range(len(dims))])
    return loudness


def bell_draw(own_key, dims, deviation, limit, cuts=(), kind=jnp.bfloat16):
    array = jax.random.normal(own_key, dims, jnp.float32) * deviation
    if len(cuts) > 0:
        array = level_of(own_key, dims, cuts, -0.22, 0.18) * array
    return jnp.clip(array, min=-limit, max=limit).astype(kind)


def setup_inputs(seed: int = 0) -> dict:
    seeds = jax.random.split(jax.random.key(seed), 8)
    return {
        "hidden_in": draw_hidden_in(jax.random.fold_in(seeds[7], 71), 0),
        "out_grad": bell_draw(seeds[1], (LAYERS, TOKENS, D), 1.0, 6.0, ((0, 4), (1, 8))),
        "expert_ids": draw_expert_ids(jax.random.fold_in(seeds[7], 71), 0),
        "route_weight": jnp.clip(0.25 + 0.75 * jax.random.uniform(seeds[3], (LAYERS, TOKENS, TOPK), jnp.float32) ** level_of(seeds[3], (LAYERS, TOKENS, TOPK), ((0, 4), (1, 8)), -0.2, 0.2), 0.25, 1.0).astype(jnp.bfloat16),
        "norm_gain": jnp.clip(1.0 + 0.15 * jax.random.normal(seeds[4], (LAYERS, D), jnp.float32), 0.25, 1.75),
        "w_gate_up": bell_draw(seeds[5], (LAYERS, SLABS, 2, F_DEV, D), D ** -0.5, 0.09375, ((0, 4), (1, 8))),
        "w_down": bell_draw(seeds[6], (LAYERS, SLABS, F_DEV, D), FF ** -0.5, 0.15625, ((0, 4), (1, 8))),
    }


def reference(hidden_in, out_grad, expert_ids, route_weight, norm_gain, w_gate_up, w_down):
    specialist_span = EXP_FLY
    group = SLABS // EXP_FLY
    total_rows = SLABS * SPECIALIST_CAP
    handed_list = []
    gate_up_list = []
    down_list = []
    combine_list = []
    for layer_idx in range(LAYERS):
        tokens_f = hidden_in[layer_idx].astype(jnp.float32)
        rms_value = jnp.sqrt(lax.optimization_barrier(jnp.mean(tokens_f * tokens_f, axis=-1, keepdims=True)) + 1e-06)
        normed = tokens_f / rms_value
        gain_row = norm_gain[layer_idx].astype(jnp.float32)
        normed_in = (normed * gain_row).astype(jnp.bfloat16)
        grad_out = out_grad[layer_idx]
        chosen = expert_ids[layer_idx]
        picked = chosen[:, :, None] == jnp.arange(specialist_span, dtype=jnp.int32)[None, None, :]
        member = jnp.any(picked, axis=1).astype(jnp.int32)
        weight_te = lax.optimization_barrier(jnp.sum(jnp.where(picked, route_weight[layer_idx].astype(jnp.float32)[:, :, None], jnp.float32(0.0)), axis=1))
        blocked = member.reshape(SLABS, TOK_DEV, specialist_span)
        position = (jnp.cumsum(blocked, axis=1) - blocked).reshape(TOKENS, specialist_span).astype(jnp.int32)
        source = (jnp.arange(TOKENS, dtype=jnp.int32) // TOK_DEV).astype(jnp.int32)
        grad_normed = jnp.zeros((TOKENS, D), jnp.float32)
        grad_combine = jnp.zeros((TOKENS, TOPK), jnp.float32)
        gate_up_parts = []
        down_parts = []
        for expert_idx in range(specialist_span):
            target = jnp.where(member[:, expert_idx] == 1, source * SPECIALIST_CAP + position[:, expert_idx], total_rows).astype(jnp.int32)
            rows_in = jnp.zeros((total_rows + 1, D), jnp.float32).at[target].add(normed_in.astype(jnp.float32))[:total_rows].astype(jnp.bfloat16)
            rows_grad = jnp.zeros((total_rows + 1, D), jnp.float32).at[target].add(grad_out.astype(jnp.float32))[:total_rows].astype(jnp.bfloat16)
            rows_weight = jnp.zeros((total_rows + 1,), jnp.float32).at[target].add(weight_te[:, expert_idx])[:total_rows]
            first_slab = expert_idx * group
            gate_up_w = w_gate_up[layer_idx, first_slab:first_slab + group].astype(jnp.float32)
            down_w = w_down[layer_idx, first_slab:first_slab + group].astype(jnp.float32)
            rows_in_f = rows_in.astype(jnp.float32)
            rows_grad_f = rows_grad.astype(jnp.float32)
            weight_col = rows_weight[:, None, None]
            gate_pre = jnp.einsum('rd,sfd->rsf', rows_in_f, gate_up_w[:, 0])
            up_pre = jnp.einsum('rd,sfd->rsf', rows_in_f, gate_up_w[:, 1])
            sigmoid_gate = jax.nn.sigmoid(gate_pre)
            active = gate_pre * sigmoid_gate
            hidden_act = active * up_pre
            back_proj = jnp.einsum('rd,sfd->rsf', rows_grad_f, down_w)
            grad_hidden = weight_col * back_proj
            grad_gate = (grad_hidden * up_pre * sigmoid_gate * (1.0 + gate_pre * (1.0 - sigmoid_gate))).astype(jnp.bfloat16).astype(jnp.float32)
            grad_up = (grad_hidden * active).astype(jnp.bfloat16).astype(jnp.float32)
            scaled_hidden = (weight_col * hidden_act).astype(jnp.bfloat16).astype(jnp.float32)
            gate_grad = jnp.einsum('rsf,rd->sfd', grad_gate, rows_in_f)
            up_grad = jnp.einsum('rsf,rd->sfd', grad_up, rows_in_f)
            gate_up_parts.append(jnp.stack([gate_grad, up_grad], axis=1).astype(jnp.bfloat16))
            down_parts.append(jnp.einsum('rsf,rd->sfd', scaled_hidden, rows_grad_f).astype(jnp.bfloat16))
            input_part = jnp.einsum('rsf,sfd->rsd', grad_gate, gate_up_w[:, 0]) + jnp.einsum('rsf,sfd->rsd', grad_up, gate_up_w[:, 1])
            input_sum = lax.optimization_barrier(jnp.sum(input_part.astype(jnp.bfloat16).astype(jnp.float32), axis=1))
            combine_sum = lax.optimization_barrier(jnp.sum(lax.optimization_barrier(jnp.sum(hidden_act * back_proj, axis=-1)).astype(jnp.bfloat16).astype(jnp.float32), axis=1))
            extended = jnp.concatenate([input_sum, jnp.zeros((1, D), jnp.float32)], axis=0)
            grad_normed = grad_normed + extended[target]
            comb_ext = jnp.concatenate([combine_sum, jnp.zeros((1,), jnp.float32)], axis=0)
            grad_combine = grad_combine + jnp.where(picked[:, :, expert_idx], comb_ext[target][:, None], jnp.float32(0.0))
        scaled = grad_normed * gain_row
        inner_mean = lax.optimization_barrier(jnp.mean(scaled * normed, axis=-1, keepdims=True))
        grad_tokens = (grad_out.astype(jnp.float32) + (scaled - normed * inner_mean) / rms_value).astype(jnp.bfloat16)
        handed_list.append(grad_tokens)
        gate_up_list.append(jnp.concatenate(gate_up_parts, axis=0))
        down_list.append(jnp.concatenate(down_parts, axis=0))
        combine_list.append(grad_combine)
    handed_grad = jnp.roll(jnp.stack(handed_list, axis=0), -1, axis=0)
    return (handed_grad, jnp.stack(gate_up_list, axis=0), jnp.stack(down_list, axis=0), jnp.stack(combine_list, axis=0))
```

```python
import functools

import jax
import jax.numpy as jnp
from jax import lax
from jax.experimental import pallas as pl
from jax.experimental.pallas import tpu as pltpu
from jax.sharding import PartitionSpec as P

SPLIT = 8
SPECIALIST_CAP = 8
LANES = 128
EPS = 1e-06
F32 = jnp.float32
BF16 = jnp.bfloat16


def shifted(block, axis, distance):
    devices = range(lax.axis_size(axis))
    route = [((i - distance) % len(devices), i) for i in devices]
    return lax.ppermute(block, axis, route)


def rows_product(left_rows, right_rows):
    return lax.dot_general(
        left_rows, right_rows, (((1,), (1,)), ((), ())), preferred_element_type=jnp.float32
    )


def column_product(left_rows, right_rows):
    return lax.dot_general(
        left_rows, right_rows, (((0,), (0,)), ((), ())), preferred_element_type=jnp.float32
    )


def on_many(hidden_in, out_grad, expert_ids, route_weight, norm_gain, w_gate_up, w_down):
    tokens_in = hidden_in[0]
    grad_out = out_grad[0]
    chosen = expert_ids[0]
    weights_in = route_weight[0]
    gain_row = norm_gain[0]
    slab_gate_up = w_gate_up[0, 0]
    slab_down = w_down[0, 0]
    devices = lax.axis_size("expert")
    specialist_span = devices // SPLIT
    model_width = tokens_in.shape[1]
    hidden_slab = slab_down.shape[0]
    capacity = SPECIALIST_CAP
    tokens_f = tokens_in.astype(jnp.float32)
    rms_value = jnp.sqrt(jnp.mean(tokens_f * tokens_f, axis=-1, keepdims=True) + 1e-06)
    normed = tokens_f / rms_value
    normed_in = (normed * gain_row).astype(jnp.bfloat16)
    expert_range = jnp.arange(specialist_span, dtype=jnp.int32)
    picked = chosen[:, :, None] == expert_range[None, None, :]
    member = jnp.any(picked, axis=1).astype(jnp.int32)
    weight_te = jnp.sum(jnp.where(picked, weights_in.astype(jnp.float32)[:, :, None], 0.0), axis=1)
    position = jnp.cumsum(member, axis=0) - member
    slot_range = jnp.arange(capacity, dtype=jnp.int32)
    placing = (position.T[:, None, :] == slot_range[None, :, None]) & (member.T[:, None, :] == 1)
    place_bf = placing.astype(jnp.bfloat16)
    place_f = placing.astype(jnp.float32)
    sent_in = jnp.einsum(
        "wst,td->wsd", place_bf, normed_in, preferred_element_type=jnp.float32
    ).astype(jnp.bfloat16)
    sent_grad = jnp.einsum(
        "wst,td->wsd", place_bf, grad_out, preferred_element_type=jnp.float32
    ).astype(jnp.bfloat16)
    sent_weight = jnp.sum(place_f * weight_te.T[:, None, :], axis=-1).astype(jnp.bfloat16)
    rows_in, rows_grad, rows_weight = (
        lax.all_to_all(
            jnp.repeat(sent_in, SPLIT, axis=0), "expert", split_axis=0, concat_axis=0, tiled=True
        ),
        lax.all_to_all(
            jnp.repeat(sent_grad, SPLIT, axis=0), "expert", split_axis=0, concat_axis=0, tiled=True
        ),
        lax.all_to_all(
            jnp.repeat(sent_weight, SPLIT, axis=0),
            "expert",
            split_axis=0,
            concat_axis=0,
            tiled=True,
        ),
    )
    total_rows = devices * capacity
    flat_in = rows_in.reshape(total_rows, model_width)
    flat_grad = rows_grad.reshape(total_rows, model_width)
    flat_weight = rows_weight.reshape(total_rows, 1).astype(jnp.float32)
    joined_slab = slab_gate_up.reshape(2 * hidden_slab, model_width)
    projected = rows_product(flat_in, joined_slab)
    gate_pre = projected[:, :hidden_slab]
    up_pre = projected[:, hidden_slab:]
    sigmoid_gate = jax.nn.sigmoid(gate_pre)
    active = gate_pre * sigmoid_gate
    hidden_act = active * up_pre
    scaled_hidden = (flat_weight * hidden_act).astype(jnp.bfloat16)
    back_proj = rows_product(flat_grad, slab_down)
    grad_hidden = flat_weight * back_proj
    grad_gate = (
        grad_hidden * up_pre * sigmoid_gate * (1.0 + gate_pre * (1.0 - sigmoid_gate))
    ).astype(jnp.bfloat16)
    grad_up = (grad_hidden * active).astype(jnp.bfloat16)
    grad_both = jnp.concatenate([grad_gate, grad_up], axis=1)
    weight_grad = column_product(grad_both, flat_in)
    down_grad = column_product(scaled_hidden, flat_grad)
    input_part = (
        jnp.dot(grad_both, joined_slab, preferred_element_type=jnp.float32)
        .astype(jnp.bfloat16)
        .reshape(devices, capacity, model_width)
    )
    combine_part = (
        jnp.sum(hidden_act * back_proj, axis=-1).astype(jnp.bfloat16).reshape(devices, capacity)
    )
    returned_in, returned_comb = (
        lax.all_to_all(input_part, "expert", split_axis=0, concat_axis=0, tiled=True),
        lax.all_to_all(combine_part, "expert", split_axis=0, concat_axis=0, tiled=True),
    )
    summed_in = jnp.sum(
        returned_in.reshape(specialist_span, SPLIT, capacity, model_width).astype(jnp.float32),
        axis=1,
    )
    summed_comb = jnp.sum(
        returned_comb.reshape(specialist_span, SPLIT, capacity).astype(jnp.float32), axis=1
    )
    grad_normed = jnp.einsum("wst,wsd->td", place_f, summed_in, precision=lax.Precision.HIGHEST)
    comb_te = jnp.sum(place_f * summed_comb[:, :, None], axis=1)
    grad_combine = jnp.sum(jnp.where(picked, comb_te.T[:, None, :], 0.0), axis=-1)
    scaled = grad_normed * gain_row
    inner_mean = jnp.mean(scaled * normed, axis=-1, keepdims=True)
    grad_tokens = (
        grad_out.astype(jnp.float32) + (scaled - normed * inner_mean) / rms_value
    ).astype(jnp.bfloat16)
    handed = shifted(grad_tokens, "pipe", -1)
    gate_up_out = weight_grad.reshape(2, hidden_slab, model_width).astype(jnp.bfloat16)
    return (
        handed[None],
        gate_up_out[None, None],
        down_grad.astype(jnp.bfloat16)[None, None],
        grad_combine[None],
    )


def call(kernel, outs, flops, moved, limit=24, scratch=()):
    return pl.pallas_call(
        kernel,
        out_shape=[jax.ShapeDtypeStruct(shape, kind) for shape, kind in outs],
        scratch_shapes=list(scratch),
        compiler_params=pltpu.CompilerParams(vmem_limit_bytes=limit << 20),
        cost_estimate=pl.CostEstimate(flops=flops, bytes_accessed=moved, transcendentals=0),
    )


def take_rows(place, block):
    return lax.dot_general(place, block, (((1,), (0,)), ((), ())), preferred_element_type=F32)


def normed_rows(rows):
    rms = jnp.sqrt(jnp.mean(rows * rows, axis=-1, keepdims=True) + EPS)
    return rows / rms, rms


def place_kernel(ids_ref, hidden_ref, gain_ref, in_ref, raw_ref, place_ref):
    tokens = ids_ref.shape[1]
    cap = SPECIALIST_CAP
    member = jnp.max((ids_ref[...] == 0).astype(F32), axis=0, keepdims=True)
    member = jnp.broadcast_to(member, (cap, tokens))
    earlier = lax.broadcasted_iota(jnp.int32, (tokens, tokens), 0) < lax.broadcasted_iota(
        jnp.int32, (tokens, tokens), 1
    )
    position = take_rows(member.astype(BF16), earlier.astype(F32).astype(BF16))
    slot = lax.broadcasted_iota(jnp.int32, (cap, tokens), 0).astype(F32)
    place = jnp.where(position == slot, member, 0.0)
    place_ref[...] = place
    rows = take_rows(place.astype(BF16), hidden_ref[...])
    raw_ref[...] = rows.astype(BF16)
    normed, _ = normed_rows(rows)
    in_ref[...] = (normed * gain_ref[...]).astype(BF16)


def grad_rows_kernel(ids_ref, weight_ref, place_ref, grad_ref, out_ref):
    width = grad_ref.shape[1]
    place = place_ref[...]
    out_ref[:, :width] = take_rows(place.astype(BF16), grad_ref[...]).astype(BF16)
    weight = jnp.sum(
        jnp.where(ids_ref[...] == 0, weight_ref[...].astype(F32), 0.0), axis=0, keepdims=True
    )
    taken = jnp.sum(place * weight, axis=1, keepdims=True)
    out_ref[:, width:] = jnp.broadcast_to(taken, (place.shape[0], LANES)).astype(BF16)


def stacked(refs, start, stop):
    return jnp.concatenate([r[:, start:stop].astype(F32) for r in refs], axis=0)


def project_kernel(*refs):
    *blocks, slab_ref, out_ref = refs
    width = slab_ref.shape[1]
    out_ref[...] = rows_product(stacked(blocks, 0, width).astype(BF16), slab_ref[...])


def hidden_kernel(*refs):
    *blocks, pre_ref, down_ref, slab_ref, keep_ref, send_ref, both_ref, act_ref = refs
    hidden, width = down_ref.shape
    half = keep_ref.shape[0]
    grad = stacked(blocks, 0, width).astype(BF16)
    weight = stacked(blocks, width, width + LANES)[:, :1]
    back = rows_product(grad, down_ref[...])
    gate = pre_ref[:, :hidden]
    up = pre_ref[:, hidden:]
    sig = jax.nn.sigmoid(gate)
    active = gate * sig
    act = active * up
    act_ref[...] = (weight * act).T.astype(BF16)
    into = weight * back
    both = jnp.concatenate(
        [into * up * sig * (1.0 + gate * (1.0 - sig)), into * active], axis=1
    )
    both_ref[...] = both.T.astype(BF16)
    part = take_rows(both.astype(BF16), slab_ref[...]).astype(BF16)
    keep_ref[:, :width] = part[:half]
    send_ref[:, :width] = part[half:]
    comb = jnp.sum(act * back, axis=1, keepdims=True)
    comb = jnp.broadcast_to(comb, (2 * half, LANES)).astype(BF16)
    keep_ref[:, width:] = comb[:half]
    send_ref[:, width:] = comb[half:]


def join_kernel(keep_ref, got_ref, *refs):
    *out_refs, comb_ref = refs
    width = out_refs[0].shape[1]
    total = keep_ref[...].astype(F32) + got_ref[...].astype(F32)
    rows = out_refs[0].shape[0]
    for k, out_ref in enumerate(out_refs):
        out_ref[...] = total[k * rows : (k + 1) * rows, :width].astype(BF16)
    comb_ref[...] = total[:, width:]


def weights_kernel(*refs):
    *blocks, both_ref, act_ref, both_out, act_out = refs
    ins, grads = blocks[: len(blocks) // 2], blocks[len(blocks) // 2 :]
    step = both_out.shape[1]
    both_out[...] = take_rows(both_ref[...], stacked(ins, 0, step).astype(BF16)).astype(BF16)
    act_out[...] = take_rows(act_ref[...], stacked(grads, 0, step).astype(BF16)).astype(BF16)


def weight_grads(ins, grads, both, act, width):
    chunk = min(width, 1024)
    rows = ins[0].shape[0]
    block = pl.BlockSpec((rows, chunk), lambda i: (0, i))
    whole = lambda a: pl.BlockSpec(a.shape, lambda i: (0, 0))
    return pl.pallas_call(
        weights_kernel,
        grid=(width // chunk,),
        in_specs=[block] * (len(ins) + len(grads)) + [whole(both), whole(act)],
        out_specs=[
            pl.BlockSpec((both.shape[0], chunk), lambda i: (0, i)),
            pl.BlockSpec((act.shape[0], chunk), lambda i: (0, i)),
        ],
        out_shape=[
            jax.ShapeDtypeStruct((both.shape[0], width), BF16),
            jax.ShapeDtypeStruct((act.shape[0], width), BF16),
        ],
        compiler_params=pltpu.CompilerParams(vmem_limit_bytes=24 << 20),
        cost_estimate=pl.CostEstimate(
            flops=2 * 64 * 576 * width, bytes_accessed=2 * 700 * width, transcendentals=0
        ),
    )(*ins, *grads, both, act)


def finish_kernel(*refs):
    *parts, raw_ref, gain_ref, place_ref, grad_ref, out_ref = refs
    place = place_ref[...]
    normed, rms = normed_rows(raw_ref[...].astype(F32))
    grad = grad_ref[...]
    own = take_rows(place.astype(BF16), grad)
    total = sum(p[...].astype(F32) for p in parts)
    scaled = total * gain_ref[...]
    inner = jnp.mean(scaled * normed, axis=-1, keepdims=True)
    rows = (own + (scaled - normed * inner) / rms).astype(BF16)
    back = place.T
    spread = take_rows(back.astype(BF16), rows)
    named = jnp.sum(back, axis=1, keepdims=True) > 0.0
    out_ref[...] = jnp.where(named, spread, grad.astype(F32)).astype(BF16)


def combine_kernel(*refs):
    *parts, ids_ref, place_ref, out_ref = refs
    total = sum(p[...] for p in parts)
    spread = jnp.sum(place_ref[...] * total, axis=0, keepdims=True)
    out_ref[...] = jnp.where(ids_ref[...] == 0, spread, 0.0)


def on_one(hidden_in, out_grad, expert_ids, route_weight, norm_gain, w_gate_up, w_down):
    sections = lax.axis_size("pipe")
    devices = lax.axis_size("expert")
    chips = devices // 2
    tokens, width = hidden_in.shape[1:]
    hidden = w_down.shape[2]
    cap = SPECIALIST_CAP
    ids = expert_ids[0].T
    weights = route_weight[0].T
    slab = w_gate_up.reshape(2 * hidden, width)
    down = w_down.reshape(hidden, width)
    grad = out_grad[0]
    wide = width + LANES

    def across(block, offset):
        return lax.ppermute(block, "expert", [(i, i ^ (2 * offset)) for i in range(devices)])

    def beside(block):
        return lax.ppermute(block, "expert", [(i, i ^ 1) for i in range(devices)])

    def handed(block, offset):
        route = [
            (((p + 1) % sections) * devices + i, p * devices + (i ^ (2 * offset)))
            for p in range(sections)
            for i in range(devices)
        ]
        return lax.ppermute(block, ("pipe", "expert"), route)

    next_grad = handed(grad, 0)
    row_in, row_raw, place = call(
        place_kernel,
        [((cap, width), BF16), ((cap, width), BF16), ((cap, tokens), F32)],
        2 * tokens * width * cap,
        2 * tokens * width,
    )(ids, hidden_in[0], norm_gain)
    lane_in = [row_in] + [across(row_in, k) for k in range(1, chips)]
    (row_grad,) = call(
        grad_rows_kernel, [((cap, wide), BF16)], 2 * tokens * width * cap, 2 * tokens * width
    )(ids, weights, place, grad)
    lane_grad = [row_grad] + [across(row_grad, k) for k in range(1, chips)]
    next_raw, next_gain, next_place = handed(row_raw, 0), handed(norm_gain, 0), handed(place, 0)
    all_in = lane_in + [beside(b) for b in lane_in]
    all_grad = lane_grad + [beside(b) for b in lane_grad]
    total_rows = devices * cap
    (pre,) = call(
        project_kernel,
        [((total_rows, 2 * hidden), F32)],
        4 * total_rows * hidden * width,
        4 * hidden * width,
    )(*all_in, slab)
    keep, send, both, act = call(
        hidden_kernel,
        [
            ((total_rows // 2, wide), BF16),
            ((total_rows // 2, wide), BF16),
            ((2 * hidden, total_rows), BF16),
            ((hidden, total_rows), BF16),
        ],
        6 * total_rows * hidden * width,
        6 * hidden * width,
    )(*all_grad, pre, down, slab)
    *parts, comb = call(
        join_kernel,
        [((cap, width), BF16)] * chips + [((total_rows // 2, LANES), F32)],
        total_rows * width,
        4 * total_rows * width,
    )(keep, beside(send))
    got = [handed(parts[k], k) for k in range(chips)]
    comb_parts = [comb[k * cap : (k + 1) * cap] for k in range(chips)]
    comb_got = [comb_parts[0]] + [across(comb_parts[k], k) for k in range(1, chips)]
    gate_up_out, down_out = weight_grads(all_in, all_grad, both, act, width)
    (combined,) = call(combine_kernel, [((SPLIT, tokens), F32)], 1000, 1000)(*comb_got, ids, place)
    (out,) = call(finish_kernel, [((tokens, width), BF16)], 4 * tokens * width * cap, 4 * tokens * width)(
        *got, next_raw, next_gain, next_place, next_grad
    )
    return (
        out[None],
        gate_up_out.reshape(1, 1, 2, hidden, width),
        down_out.reshape(1, 1, hidden, width),
        combined.T[None],
    )


def solution(mesh):
    on_device = on_one if mesh.shape["expert"] == SPLIT else on_many
    return jax.shard_map(
        on_device,
        mesh=mesh,
        in_specs=(
            P("pipe", "expert", None),
            P("pipe", "expert", None),
            P("pipe", "expert", None),
            P("pipe", "expert", None),
            P("pipe", None),
            P("pipe", "expert", None, None, None),
            P("pipe", "expert", None, None),
        ),
        out_specs=(
            P("pipe", "expert", None),
            P("pipe", "expert", None, None, None),
            P("pipe", "expert", None, None),
            P("pipe", "expert", None),
        ),
        check_vma=False,
    )
```

```python
import functools

import jax
import jax.numpy as jnp
from jax import lax
from jax.experimental import pallas as pl
from jax.experimental.pallas import tpu as pltpu
from jax.sharding import PartitionSpec as P

SPLIT = 8
SPECIALIST_CAP = 8
LANES = 128
EPS = 1e-06
F32 = jnp.float32
BF16 = jnp.bfloat16


def shifted(block, axis, distance):
    devices = range(lax.axis_size(axis))
    route = [((i - distance) % len(devices), i) for i in devices]
    return lax.ppermute(block, axis, route)


def rows_product(left_rows, right_rows):
    return lax.dot_general(
        left_rows, right_rows, (((1,), (1,)), ((), ())), preferred_element_type=jnp.float32
    )


def column_product(left_rows, right_rows):
    return lax.dot_general(
        left_rows, right_rows, (((0,), (0,)), ((), ())), preferred_element_type=jnp.float32
    )


def on_many(hidden_in, out_grad, expert_ids, route_weight, norm_gain, w_gate_up, w_down):
    tokens_in = hidden_in[0]
    grad_out = out_grad[0]
    chosen = expert_ids[0]
    weights_in = route_weight[0]
    gain_row = norm_gain[0]
    slab_gate_up = w_gate_up[0, 0]
    slab_down = w_down[0, 0]
    devices = lax.axis_size("expert")
    specialist_span = devices // SPLIT
    model_width = tokens_in.shape[1]
    hidden_slab = slab_down.shape[0]
    capacity = SPECIALIST_CAP
    tokens_f = tokens_in.astype(jnp.float32)
    rms_value = jnp.sqrt(jnp.mean(tokens_f * tokens_f, axis=-1, keepdims=True) + 1e-06)
    normed = tokens_f / rms_value
    normed_in = (normed * gain_row).astype(jnp.bfloat16)
    expert_range = jnp.arange(specialist_span, dtype=jnp.int32)
    picked = chosen[:, :, None] == expert_range[None, None, :]
    member = jnp.any(picked, axis=1).astype(jnp.int32)
    weight_te = jnp.sum(jnp.where(picked, weights_in.astype(jnp.float32)[:, :, None], 0.0), axis=1)
    position = jnp.cumsum(member, axis=0) - member
    slot_range = jnp.arange(capacity, dtype=jnp.int32)
    placing = (position.T[:, None, :] == slot_range[None, :, None]) & (member.T[:, None, :] == 1)
    place_bf = placing.astype(jnp.bfloat16)
    place_f = placing.astype(jnp.float32)
    sent_in = jnp.einsum(
        "wst,td->wsd", place_bf, normed_in, preferred_element_type=jnp.float32
    ).astype(jnp.bfloat16)
    sent_grad = jnp.einsum(
        "wst,td->wsd", place_bf, grad_out, preferred_element_type=jnp.float32
    ).astype(jnp.bfloat16)
    sent_weight = jnp.sum(place_f * weight_te.T[:, None, :], axis=-1).astype(jnp.bfloat16)
    rows_in, rows_grad, rows_weight = (
        lax.all_to_all(
            jnp.repeat(sent_in, SPLIT, axis=0), "expert", split_axis=0, concat_axis=0, tiled=True
        ),
        lax.all_to_all(
            jnp.repeat(sent_grad, SPLIT, axis=0), "expert", split_axis=0, concat_axis=0, tiled=True
        ),
        lax.all_to_all(
            jnp.repeat(sent_weight, SPLIT, axis=0),
            "expert",
            split_axis=0,
            concat_axis=0,
            tiled=True,
        ),
    )
    total_rows = devices * capacity
    flat_in = rows_in.reshape(total_rows, model_width)
    flat_grad = rows_grad.reshape(total_rows, model_width)
    flat_weight = rows_weight.reshape(total_rows, 1).astype(jnp.float32)
    joined_slab = slab_gate_up.reshape(2 * hidden_slab, model_width)
    projected = rows_product(flat_in, joined_slab)
    gate_pre = projected[:, :hidden_slab]
    up_pre = projected[:, hidden_slab:]
    sigmoid_gate = jax.nn.sigmoid(gate_pre)
    active = gate_pre * sigmoid_gate
    hidden_act = active * up_pre
    scaled_hidden = (flat_weight * hidden_act).astype(jnp.bfloat16)
    back_proj = rows_product(flat_grad, slab_down)
    grad_hidden = flat_weight * back_proj
    grad_gate = (
        grad_hidden * up_pre * sigmoid_gate * (1.0 + gate_pre * (1.0 - sigmoid_gate))
    ).astype(jnp.bfloat16)
    grad_up = (grad_hidden * active).astype(jnp.bfloat16)
    grad_both = jnp.concatenate([grad_gate, grad_up], axis=1)
    weight_grad = column_product(grad_both, flat_in)
    down_grad = column_product(scaled_hidden, flat_grad)
    input_part = (
        jnp.dot(grad_both, joined_slab, preferred_element_type=jnp.float32)
        .astype(jnp.bfloat16)
        .reshape(devices, capacity, model_width)
    )
    combine_part = (
        jnp.sum(hidden_act * back_proj, axis=-1).astype(jnp.bfloat16).reshape(devices, capacity)
    )
    returned_in, returned_comb = (
        lax.all_to_all(input_part, "expert", split_axis=0, concat_axis=0, tiled=True),
        lax.all_to_all(combine_part, "expert", split_axis=0, concat_axis=0, tiled=True),
    )
    summed_in = jnp.sum(
        returned_in.reshape(specialist_span, SPLIT, capacity, model_width).astype(jnp.float32),
        axis=1,
    )
    summed_comb = jnp.sum(
        returned_comb.reshape(specialist_span, SPLIT, capacity).astype(jnp.float32), axis=1
    )
    grad_normed = jnp.einsum("wst,wsd->td", place_f, summed_in, precision=lax.Precision.HIGHEST)
    comb_te = jnp.sum(place_f * summed_comb[:, :, None], axis=1)
    grad_combine = jnp.sum(jnp.where(picked, comb_te.T[:, None, :], 0.0), axis=-1)
    scaled = grad_normed * gain_row
    inner_mean = jnp.mean(scaled * normed, axis=-1, keepdims=True)
    grad_tokens = (
        grad_out.astype(jnp.float32) + (scaled - normed * inner_mean) / rms_value
    ).astype(jnp.bfloat16)
    handed = shifted(grad_tokens, "pipe", -1)
    gate_up_out = weight_grad.reshape(2, hidden_slab, model_width).astype(jnp.bfloat16)
    return (
        handed[None],
        gate_up_out[None, None],
        down_grad.astype(jnp.bfloat16)[None, None],
        grad_combine[None],
    )


def call(kernel, outs, flops, moved, in_specs=None, scratch=(), limit=24):
    given = {} if in_specs is None else {"in_specs": in_specs}
    return pl.pallas_call(
        kernel,
        **given,
        out_shape=[jax.ShapeDtypeStruct(shape, kind) for shape, kind in outs],
        scratch_shapes=list(scratch),
        compiler_params=pltpu.CompilerParams(vmem_limit_bytes=limit << 20),
        cost_estimate=pl.CostEstimate(flops=flops, bytes_accessed=moved, transcendentals=0),
    )


IN_HBM = pl.BlockSpec(memory_space=pltpu.HBM)
IN_VMEM = pl.BlockSpec(memory_space=pltpu.VMEM)


def take_rows(place, block):
    return lax.dot_general(place, block, (((1,), (0,)), ((), ())), preferred_element_type=F32)


def normed_rows(rows):
    rms = jnp.sqrt(jnp.mean(rows * rows, axis=-1, keepdims=True) + EPS)
    return rows / rms, rms


def rows_kernel(ids_hbm, weight_hbm, gain_hbm, hidden_hbm, grad_hbm, rows_ref, side_ref, place_ref,
                ids_ref, weight_ref, gain_ref, hidden_ref, grad_ref, sems):
    copies = [
        pltpu.make_async_copy(src, dst, sems.at[i])
        for i, (src, dst) in enumerate([
            (ids_hbm, ids_ref),
            (hidden_hbm, hidden_ref),
            (gain_hbm, gain_ref),
            (weight_hbm, weight_ref),
            (grad_hbm, grad_ref),
        ])
    ]
    for copy in copies:
        copy.start()
    width = hidden_ref.shape[1]
    tokens = ids_ref.shape[1]
    cap = SPECIALIST_CAP
    copies[0].wait()
    hit = ids_ref[...] == 0
    member = jnp.max(hit.astype(F32), axis=0, keepdims=True)
    member = jnp.broadcast_to(member, (cap, tokens))
    earlier = lax.broadcasted_iota(jnp.int32, (tokens, tokens), 0) < lax.broadcasted_iota(
        jnp.int32, (tokens, tokens), 1
    )
    position = take_rows(member.astype(BF16), earlier.astype(F32).astype(BF16))
    slot = lax.broadcasted_iota(jnp.int32, (cap, tokens), 0).astype(F32)
    place = jnp.where(position == slot, member, 0.0)
    place_ref[...] = place
    copies[1].wait()
    raw = take_rows(place.astype(BF16), hidden_ref[...])
    normed, _ = normed_rows(raw)
    copies[2].wait()
    gain = gain_ref[...]
    normed_in = normed * gain
    high = gain.astype(BF16).astype(F32)
    middle = (gain - high).astype(BF16).astype(F32)
    low = gain - high - middle
    blank = jnp.zeros((cap - 3, width), F32)
    side_ref[:, :width] = jnp.concatenate([raw, high, middle, low, blank], axis=0).astype(BF16)
    side_ref[:, width:] = jnp.concatenate([place, jnp.zeros((cap, tokens), F32)], axis=0).astype(BF16)
    copies[3].wait()
    weight = jnp.sum(
        jnp.where(hit, weight_ref[...].astype(F32), 0.0), axis=0, keepdims=True
    )
    taken = jnp.sum(place * weight, axis=1, keepdims=True)
    taken = jnp.broadcast_to(taken, (cap, LANES))
    rows_ref[:, width:] = jnp.concatenate([taken, taken], axis=0).astype(BF16)
    copies[4].wait()
    grad = take_rows(place.astype(BF16), grad_ref[...])
    rows_ref[:, :width] = jnp.concatenate([normed_in, grad], axis=0).astype(BF16)


def fetch_kernel(slab_hbm, down_hbm, after_ref, slab_ref, down_ref, sems):
    del after_ref
    first = pltpu.make_async_copy(slab_hbm, slab_ref, sems.at[0])
    second = pltpu.make_async_copy(down_hbm, down_ref, sems.at[1])
    first.start()
    second.start()
    first.wait()
    second.wait()


def halves(rows, cap):
    blocks = range(rows.shape[0] // (2 * cap))
    return [
        jnp.concatenate([rows[(2 * b + h) * cap : (2 * b + h + 1) * cap] for b in blocks], axis=0)
        for h in (0, 1)
    ]


def padded(rows, half, cap):
    blank = jnp.zeros((cap, rows.shape[1]), rows.dtype)
    pieces = []
    for b in range(rows.shape[0] // cap):
        own = rows[b * cap : (b + 1) * cap]
        pieces += [own, blank] if half == 0 else [blank, own]
    return jnp.concatenate(pieces, axis=0)


def hidden_kernel(*refs):
    *blocks, slab_ref, down_ref, keep_ref, send_ref, both_ref, act_ref = refs
    hidden, width = down_ref.shape
    half = keep_ref.shape[0]
    cap = SPECIALIST_CAP
    rows = jnp.concatenate([r[:, :width] for r in blocks], axis=0)
    pre, _ = halves(rows_product(rows, slab_ref[...]), cap)
    _, back = halves(rows_product(rows, down_ref[...]), cap)
    weight = jnp.concatenate([r[:, width:].astype(F32)[:cap, :1] for r in blocks], axis=0)
    gate = pre[:, :hidden]
    up = pre[:, hidden:]
    sig = jax.nn.sigmoid(gate)
    active = gate * sig
    act = active * up
    into = weight * back
    both = jnp.concatenate(
        [into * up * sig * (1.0 + gate * (1.0 - sig)), into * active], axis=1
    )
    part = take_rows(both.astype(BF16), slab_ref[...]).astype(BF16)
    send_ref[:, :width] = part[half:]
    keep_ref[:, :width] = part[:half]
    comb = jnp.sum(act * back, axis=1, keepdims=True)
    comb = jnp.broadcast_to(comb, (2 * half, LANES)).astype(BF16)
    send_ref[:, width:] = comb[half:]
    keep_ref[:, width:] = comb[:half]
    both_ref[...] = padded(both, 0, cap).T.astype(BF16)
    act_ref[...] = padded(weight * act, 1, cap).T.astype(BF16)


def join_kernel(keep_ref, got_ref, *refs):
    *out_refs, comb_ref = refs
    rows, width = out_refs[0].shape
    total = keep_ref[...].astype(F32) + got_ref[...].astype(F32)
    for k, out_ref in enumerate(out_refs):
        out_ref[...] = total[k * rows : (k + 1) * rows, :width].astype(BF16)
    comb_ref[...] = total[:, width:]


def weights_kernel(chips, *refs):
    blocks, refs = refs[: 2 * chips], refs[2 * chips :]
    both_ref, act_ref, comb_ref, both_out, act_out, *comb_refs = refs
    rows = jnp.concatenate([r[...] for r in blocks], axis=0)
    both_out[...] = take_rows(both_ref[...], rows).astype(BF16)
    act_out[...] = take_rows(act_ref[...], rows).astype(BF16)
    cap = comb_refs[0].shape[0]
    for k, out_ref in enumerate(comb_refs):
        out_ref[...] = comb_ref[k * cap : (k + 1) * cap]


def weight_grads(blocks, both, act, comb, chips, width):
    chunk = min(width, 1024)
    across = lambda rows: pl.BlockSpec((rows, chunk), lambda i: (0, i))
    whole = lambda shape: pl.BlockSpec(shape, lambda i: (0, 0))
    comb_shape = (comb.shape[0] // chips, comb.shape[1])
    hidden = act.shape[0]
    return pl.pallas_call(
        functools.partial(weights_kernel, chips),
        grid=(width // chunk,),
        in_specs=[across(b.shape[0]) for b in blocks]
        + [whole(both.shape), whole(act.shape), whole(comb.shape)],
        out_specs=[across(2 * hidden), across(hidden)] + [whole(comb_shape)] * chips,
        out_shape=[
            jax.ShapeDtypeStruct((2 * hidden, width), BF16),
            jax.ShapeDtypeStruct((hidden, width), BF16),
        ]
        + [jax.ShapeDtypeStruct(comb_shape, F32)] * chips,
        compiler_params=pltpu.CompilerParams(vmem_limit_bytes=24 << 20),
        cost_estimate=pl.CostEstimate(
            flops=6 * 128 * hidden * width, bytes_accessed=6 * hidden * width, transcendentals=0
        ),
    )(*blocks, both, act, comb)


def finish_kernel(*refs):
    *parts, side_ref, grad_ref, out_ref = refs
    cap = SPECIALIST_CAP
    width = grad_ref.shape[1]
    side = side_ref[...].astype(F32)
    place = side[:cap, width:]
    gain = side[cap : cap + 1, :width] + side[cap + 1 : cap + 2, :width] + side[cap + 2 : cap + 3, :width]
    normed, rms = normed_rows(side[:cap, :width])
    grad = grad_ref[...]
    own = take_rows(place.astype(BF16), grad)
    total = sum(p[...].astype(F32) for p in parts)
    scaled = total * gain
    inner = jnp.mean(scaled * normed, axis=-1, keepdims=True)
    rows = (own + (scaled - normed * inner) / rms).astype(BF16)
    back = place.T
    spread = take_rows(back.astype(BF16), rows)
    named = jnp.sum(back, axis=1, keepdims=True) > 0.0
    out_ref[...] = jnp.where(named, spread, grad.astype(F32)).astype(BF16)


def combine_kernel(*refs):
    *parts, ids_ref, place_ref, out_ref = refs
    total = sum(p[...] for p in parts)
    spread = jnp.sum(place_ref[...] * total, axis=0, keepdims=True)
    out_ref[...] = jnp.where(ids_ref[...] == 0, spread, 0.0)


def on_one(hidden_in, out_grad, expert_ids, route_weight, norm_gain, w_gate_up, w_down):
    sections = lax.axis_size("pipe")
    devices = lax.axis_size("expert")
    chips = devices // 2
    tokens, width = hidden_in.shape[1:]
    hidden = w_down.shape[2]
    cap = SPECIALIST_CAP
    ids = expert_ids[0].T
    weights = route_weight[0].T
    slab = w_gate_up.reshape(2 * hidden, width)
    down = w_down.reshape(hidden, width)
    grad = out_grad[0]
    in_hbm = lambda a: pltpu.with_memory_space_constraint(a, pltpu.HBM)
    wide = width + LANES
    total_rows = devices * cap

    def across(block, offset):
        return lax.ppermute(block, "expert", [(i, i ^ (2 * offset)) for i in range(devices)])

    def beside(block):
        return lax.ppermute(block, "expert", [(i, i ^ 1) for i in range(devices)])

    def handed(block, offset):
        route = [
            (((p + 1) % sections) * devices + i, p * devices + (i ^ (2 * offset)))
            for p in range(sections)
            for i in range(devices)
        ]
        return lax.ppermute(block, ("pipe", "expert"), route)

    rows, side, place = call(
        rows_kernel,
        [((2 * cap, wide), BF16), ((2 * cap, wide), BF16), ((cap, tokens), F32)],
        4 * tokens * width * cap,
        4 * tokens * width,
        in_specs=[IN_HBM] * 5,
        scratch=[
            pltpu.VMEM(ids.shape, ids.dtype),
            pltpu.VMEM(weights.shape, weights.dtype),
            pltpu.VMEM(norm_gain.shape, norm_gain.dtype),
            pltpu.VMEM((tokens, width), BF16),
            pltpu.VMEM((tokens, width), BF16),
            pltpu.SemaphoreType.DMA((5,)),
        ],
    )(*map(in_hbm, (ids, weights, norm_gain, hidden_in[0], grad)))
    lane = [rows] + [across(rows, k) for k in range(1, chips)]
    next_side = handed(side, 0)
    next_grad = handed(grad, 0)
    slab_near, down_near = call(
        fetch_kernel,
        [(slab.shape, BF16), (down.shape, BF16)],
        0,
        6 * hidden * width,
        in_specs=[IN_HBM, IN_HBM, pl.BlockSpec(memory_space=pl.ANY)],
        scratch=[pltpu.SemaphoreType.DMA((2,))],
    )(in_hbm(slab), in_hbm(down), place)
    blocks = lane + [beside(b) for b in lane]
    keep, send, both, act = call(
        hidden_kernel,
        [
            ((total_rows // 2, wide), BF16),
            ((total_rows // 2, wide), BF16),
            ((2 * hidden, 2 * total_rows), BF16),
            ((hidden, 2 * total_rows), BF16),
        ],
        10 * total_rows * hidden * width,
        6 * hidden * width,
    )(*blocks, slab_near, down_near)
    *parts, comb = call(
        join_kernel,
        [((cap, width), BF16)] * chips + [((total_rows // 2, LANES), F32)],
        total_rows * width,
        4 * total_rows * width,
    )(keep, beside(send))
    got = [handed(parts[k], k) for k in range(chips)]
    gate_up_out, down_out, *comb_parts = weight_grads(blocks, both, act, comb, chips, width)
    comb_got = [comb_parts[0]] + [across(comb_parts[k], k) for k in range(1, chips)]
    (combined,) = call(combine_kernel, [((SPLIT, tokens), F32)], 1000, 1000)(*comb_got, ids, place)
    (out,) = call(finish_kernel, [((tokens, width), BF16)], 4 * tokens * width * cap, 4 * tokens * width)(
        *got, next_side, next_grad
    )
    return (
        out[None],
        gate_up_out.reshape(1, 1, 2, hidden, width),
        down_out.reshape(1, 1, hidden, width),
        combined.T[None],
    )


def solution(mesh):
    on_device = on_one if mesh.shape["expert"] == SPLIT else on_many
    return jax.shard_map(
        on_device,
        mesh=mesh,
        in_specs=(
            P("pipe", "expert", None),
            P("pipe", "expert", None),
            P("pipe", "expert", None),
            P("pipe", "expert", None),
            P("pipe", None),
            P("pipe", "expert", None, None, None),
            P("pipe", "expert", None, None),
        ),
        out_specs=(
            P("pipe", "expert", None),
            P("pipe", "expert", None, None, None),
            P("pipe", "expert", None, None),
            P("pipe", "expert", None),
        ),
        check_vma=False,
    )
```

```python
import functools

import jax
import jax.numpy as jnp
from jax import lax
from jax.experimental import pallas as pl
from jax.experimental.pallas import tpu as pltpu
from jax.sharding import PartitionSpec as P

SPLIT = 8
SPECIALIST_CAP = 8
LANES = 128
EPS = 1e-06
F32 = jnp.float32
BF16 = jnp.bfloat16


def shifted(block, axis, distance):
    devices = range(lax.axis_size(axis))
    route = [((i - distance) % len(devices), i) for i in devices]
    return lax.ppermute(block, axis, route)


def rows_product(left_rows, right_rows):
    return lax.dot_general(
        left_rows, right_rows, (((1,), (1,)), ((), ())), preferred_element_type=jnp.float32
    )


def column_product(left_rows, right_rows):
    return lax.dot_general(
        left_rows, right_rows, (((0,), (0,)), ((), ())), preferred_element_type=jnp.float32
    )


def on_many(hidden_in, out_grad, expert_ids, route_weight, norm_gain, w_gate_up, w_down):
    tokens_in = hidden_in[0]
    grad_out = out_grad[0]
    chosen = expert_ids[0]
    weights_in = route_weight[0]
    gain_row = norm_gain[0]
    slab_gate_up = w_gate_up[0, 0]
    slab_down = w_down[0, 0]
    devices = lax.axis_size("expert")
    specialist_span = devices // SPLIT
    model_width = tokens_in.shape[1]
    hidden_slab = slab_down.shape[0]
    capacity = SPECIALIST_CAP
    tokens_f = tokens_in.astype(jnp.float32)
    rms_value = jnp.sqrt(jnp.mean(tokens_f * tokens_f, axis=-1, keepdims=True) + 1e-06)
    normed = tokens_f / rms_value
    normed_in = (normed * gain_row).astype(jnp.bfloat16)
    expert_range = jnp.arange(specialist_span, dtype=jnp.int32)
    picked = chosen[:, :, None] == expert_range[None, None, :]
    member = jnp.any(picked, axis=1).astype(jnp.int32)
    weight_te = jnp.sum(jnp.where(picked, weights_in.astype(jnp.float32)[:, :, None], 0.0), axis=1)
    position = jnp.cumsum(member, axis=0) - member
    slot_range = jnp.arange(capacity, dtype=jnp.int32)
    placing = (position.T[:, None, :] == slot_range[None, :, None]) & (member.T[:, None, :] == 1)
    place_bf = placing.astype(jnp.bfloat16)
    place_f = placing.astype(jnp.float32)
    sent_in = jnp.einsum(
        "wst,td->wsd", place_bf, normed_in, preferred_element_type=jnp.float32
    ).astype(jnp.bfloat16)
    sent_grad = jnp.einsum(
        "wst,td->wsd", place_bf, grad_out, preferred_element_type=jnp.float32
    ).astype(jnp.bfloat16)
    sent_weight = jnp.sum(place_f * weight_te.T[:, None, :], axis=-1).astype(jnp.bfloat16)
    rows_in, rows_grad, rows_weight = (
        lax.all_to_all(
            jnp.repeat(sent_in, SPLIT, axis=0), "expert", split_axis=0, concat_axis=0, tiled=True
        ),
        lax.all_to_all(
            jnp.repeat(sent_grad, SPLIT, axis=0), "expert", split_axis=0, concat_axis=0, tiled=True
        ),
        lax.all_to_all(
            jnp.repeat(sent_weight, SPLIT, axis=0),
            "expert",
            split_axis=0,
            concat_axis=0,
            tiled=True,
        ),
    )
    total_rows = devices * capacity
    flat_in = rows_in.reshape(total_rows, model_width)
    flat_grad = rows_grad.reshape(total_rows, model_width)
    flat_weight = rows_weight.reshape(total_rows, 1).astype(jnp.float32)
    joined_slab = slab_gate_up.reshape(2 * hidden_slab, model_width)
    projected = rows_product(flat_in, joined_slab)
    gate_pre = projected[:, :hidden_slab]
    up_pre = projected[:, hidden_slab:]
    sigmoid_gate = jax.nn.sigmoid(gate_pre)
    active = gate_pre * sigmoid_gate
    hidden_act = active * up_pre
    scaled_hidden = (flat_weight * hidden_act).astype(jnp.bfloat16)
    back_proj = rows_product(flat_grad, slab_down)
    grad_hidden = flat_weight * back_proj
    grad_gate = (
        grad_hidden * up_pre * sigmoid_gate * (1.0 + gate_pre * (1.0 - sigmoid_gate))
    ).astype(jnp.bfloat16)
    grad_up = (grad_hidden * active).astype(jnp.bfloat16)
    grad_both = jnp.concatenate([grad_gate, grad_up], axis=1)
    weight_grad = column_product(grad_both, flat_in)
    down_grad = column_product(scaled_hidden, flat_grad)
    input_part = (
        jnp.dot(grad_both, joined_slab, preferred_element_type=jnp.float32)
        .astype(jnp.bfloat16)
        .reshape(devices, capacity, model_width)
    )
    combine_part = (
        jnp.sum(hidden_act * back_proj, axis=-1).astype(jnp.bfloat16).reshape(devices, capacity)
    )
    returned_in, returned_comb = (
        lax.all_to_all(input_part, "expert", split_axis=0, concat_axis=0, tiled=True),
        lax.all_to_all(combine_part, "expert", split_axis=0, concat_axis=0, tiled=True),
    )
    summed_in = jnp.sum(
        returned_in.reshape(specialist_span, SPLIT, capacity, model_width).astype(jnp.float32),
        axis=1,
    )
    summed_comb = jnp.sum(
        returned_comb.reshape(specialist_span, SPLIT, capacity).astype(jnp.float32), axis=1
    )
    grad_normed = jnp.einsum("wst,wsd->td", place_f, summed_in, precision=lax.Precision.HIGHEST)
    comb_te = jnp.sum(place_f * summed_comb[:, :, None], axis=1)
    grad_combine = jnp.sum(jnp.where(picked, comb_te.T[:, None, :], 0.0), axis=-1)
    scaled = grad_normed * gain_row
    inner_mean = jnp.mean(scaled * normed, axis=-1, keepdims=True)
    grad_tokens = (
        grad_out.astype(jnp.float32) + (scaled - normed * inner_mean) / rms_value
    ).astype(jnp.bfloat16)
    handed = shifted(grad_tokens, "pipe", -1)
    gate_up_out = weight_grad.reshape(2, hidden_slab, model_width).astype(jnp.bfloat16)
    return (
        handed[None],
        gate_up_out[None, None],
        down_grad.astype(jnp.bfloat16)[None, None],
        grad_combine[None],
    )


def call(kernel, outs, flops, moved, in_specs=None, scratch=(), limit=24):
    given = {} if in_specs is None else {"in_specs": in_specs}
    return pl.pallas_call(
        kernel,
        **given,
        out_shape=[jax.ShapeDtypeStruct(shape, kind) for shape, kind in outs],
        scratch_shapes=list(scratch),
        compiler_params=pltpu.CompilerParams(vmem_limit_bytes=limit << 20),
        cost_estimate=pl.CostEstimate(flops=flops, bytes_accessed=moved, transcendentals=0),
    )


IN_HBM = pl.BlockSpec(memory_space=pltpu.HBM)
IN_VMEM = pl.BlockSpec(memory_space=pltpu.VMEM)


def take_rows(place, block):
    return lax.dot_general(place, block, (((1,), (0,)), ((), ())), preferred_element_type=F32)


def normed_rows(rows):
    rms = jnp.sqrt(jnp.mean(rows * rows, axis=-1, keepdims=True) + EPS)
    return rows / rms, rms


def rows_kernel(ids_hbm, weight_hbm, gain_hbm, hidden_hbm, grad_hbm, rows_ref, hand_ref, place_ref,
                ids_ref, weight_ref, gain_ref, hidden_ref, sems):
    tokens, width = hidden_ref.shape
    cap = SPECIALIST_CAP
    copies = [
        pltpu.make_async_copy(src, dst, sems.at[i])
        for i, (src, dst) in enumerate([
            (ids_hbm, ids_ref),
            (hidden_hbm, hidden_ref),
            (gain_hbm, gain_ref),
            (weight_hbm, weight_ref),
            (grad_hbm, hand_ref.at[:tokens, :width]),
        ])
    ]
    for copy in copies:
        copy.start()
    copies[0].wait()
    hit = ids_ref[...] == 0
    member = jnp.max(hit.astype(F32), axis=0, keepdims=True)
    member = jnp.broadcast_to(member, (cap, tokens))
    earlier = lax.broadcasted_iota(jnp.int32, (tokens, tokens), 0) < lax.broadcasted_iota(
        jnp.int32, (tokens, tokens), 1
    )
    position = take_rows(member.astype(BF16), earlier.astype(F32).astype(BF16))
    slot = lax.broadcasted_iota(jnp.int32, (cap, tokens), 0).astype(F32)
    place = jnp.where(position == slot, member, 0.0)
    place_ref[...] = place
    copies[1].wait()
    raw = take_rows(place.astype(BF16), hidden_ref[...])
    normed, _ = normed_rows(raw)
    copies[2].wait()
    gain = gain_ref[...]
    normed_in = normed * gain
    high = gain.astype(BF16).astype(F32)
    middle = (gain - high).astype(BF16).astype(F32)
    low = gain - high - middle
    blank = jnp.zeros((cap - 3, width), F32)
    hand_ref[tokens:, :width] = jnp.concatenate([raw, high, middle, low, blank], axis=0).astype(BF16)
    hand_ref[tokens:, width:] = jnp.concatenate([place, jnp.zeros_like(place)], axis=0).astype(BF16)
    hand_ref[:tokens, width:] = jnp.zeros((tokens, LANES), BF16)
    copies[3].wait()
    weight = jnp.sum(
        jnp.where(hit, weight_ref[...].astype(F32), 0.0), axis=0, keepdims=True
    )
    taken = jnp.sum(place * weight, axis=1, keepdims=True)
    taken = jnp.broadcast_to(taken, (cap, LANES))
    rows_ref[:, width:] = jnp.concatenate([taken, taken], axis=0).astype(BF16)
    copies[4].wait()
    grad = take_rows(place.astype(BF16), hand_ref[:tokens, :width])
    rows_ref[:, :width] = jnp.concatenate([normed_in, grad], axis=0).astype(BF16)


def fetch_kernel(slab_hbm, down_hbm, rows_ref, slab_ref, down_ref, again_ref, sems):
    first = pltpu.make_async_copy(slab_hbm, slab_ref, sems.at[0])
    second = pltpu.make_async_copy(down_hbm, down_ref, sems.at[1])
    first.start()
    second.start()
    again_ref[...] = rows_ref[...]
    first.wait()
    second.wait()


def halves(rows, cap):
    blocks = range(rows.shape[0] // (2 * cap))
    return [
        jnp.concatenate([rows[(2 * b + h) * cap : (2 * b + h + 1) * cap] for b in blocks], axis=0)
        for h in (0, 1)
    ]


def padded(rows, half, cap):
    blank = jnp.zeros((cap, rows.shape[1]), rows.dtype)
    pieces = []
    for b in range(rows.shape[0] // cap):
        own = rows[b * cap : (b + 1) * cap]
        pieces += [own, blank] if half == 0 else [blank, own]
    return jnp.concatenate(pieces, axis=0)


def hidden_kernel(*refs):
    *blocks, slab_ref, down_ref, keep_ref, send_ref, rows_ref, both_ref, act_ref = refs
    hidden, width = down_ref.shape
    half = keep_ref.shape[0]
    cap = SPECIALIST_CAP
    rows = jnp.concatenate([r[:, :width] for r in blocks], axis=0)
    rows_ref[...] = rows
    pre, _ = halves(rows_product(rows, slab_ref[...]), cap)
    _, back = halves(rows_product(rows, down_ref[...]), cap)
    weight = jnp.concatenate([r[:, width:].astype(F32)[:cap, :1] for r in blocks], axis=0)
    gate = pre[:, :hidden]
    up = pre[:, hidden:]
    sig = jax.nn.sigmoid(gate)
    active = gate * sig
    act = active * up
    into = weight * back
    both = jnp.concatenate(
        [into * up * sig * (1.0 + gate * (1.0 - sig)), into * active], axis=1
    )
    part = take_rows(both.astype(BF16), slab_ref[...]).astype(BF16)
    send_ref[:, :width] = part[half:]
    keep_ref[:, :width] = part[:half]
    comb = jnp.sum(act * back, axis=1, keepdims=True)
    comb = jnp.broadcast_to(comb, (2 * half, LANES)).astype(BF16)
    send_ref[:, width:] = comb[half:]
    keep_ref[:, width:] = comb[:half]
    both_ref[...] = padded(both, 0, cap).T.astype(BF16)
    act_ref[...] = padded(weight * act, 1, cap).T.astype(BF16)


def halve_kernel(keep_ref, got_ref, own_ref, other_ref):
    total = keep_ref[...].astype(F32) + got_ref[...].astype(F32)
    half = own_ref.shape[0]
    width = own_ref.shape[1] - LANES
    other_ref[:, :width] = total[half:, :width].astype(BF16)
    own_ref[:, :width] = total[:half, :width].astype(BF16)
    comb = total[:, width:]
    high = comb.astype(BF16).astype(F32)
    lane = lax.broadcasted_iota(jnp.int32, comb.shape, 1)
    comb = jnp.where(lane < LANES // 2, high, comb - high).astype(BF16)
    other_ref[:, width:] = comb[half:]
    own_ref[:, width:] = comb[:half]


def split_kernel(keep_ref, got_ref, own_ref, other_ref, own_comb_ref, other_comb_ref):
    total = keep_ref[...].astype(F32) + got_ref[...].astype(F32)
    half, width = own_ref.shape
    other_ref[...] = total[half:, :width].astype(BF16)
    own_ref[...] = total[:half, :width].astype(BF16)
    comb = total[:, width:]
    comb = comb + pltpu.roll(comb, LANES // 2, 1)
    other_comb_ref[...] = comb[half:]
    own_comb_ref[...] = comb[:half]


def weights_kernel(rows_ref, both_ref, act_ref, after_ref, both_out, act_out):
    del after_ref
    chunk = both_out.shape[1]
    rows = rows_ref[:, pl.ds(pl.multiple_of(pl.program_id(0) * chunk, chunk), chunk)]
    both_out[...] = take_rows(both_ref[...], rows).astype(BF16)
    act_out[...] = take_rows(act_ref[...], rows).astype(BF16)


def weight_grads(rows, both, act, after):
    width = rows.shape[1]
    hidden = act.shape[0]
    chunk = min(width, 1024)
    across = lambda count: pl.BlockSpec((count, chunk), lambda i: (0, i))
    return pl.pallas_call(
        weights_kernel,
        grid=(width // chunk,),
        in_specs=[IN_VMEM, IN_VMEM, IN_VMEM, pl.BlockSpec(memory_space=pl.ANY)],
        out_specs=[across(2 * hidden), across(hidden)],
        out_shape=[
            jax.ShapeDtypeStruct((2 * hidden, width), BF16),
            jax.ShapeDtypeStruct((hidden, width), BF16),
        ],
        compiler_params=pltpu.CompilerParams(vmem_limit_bytes=24 << 20),
        cost_estimate=pl.CostEstimate(
            flops=6 * rows.shape[0] * hidden * width,
            bytes_accessed=6 * hidden * width,
            transcendentals=0,
        ),
    )(rows, both, act, after)


def finish_kernel(own_ref, other_ref, hand_ref, own_comb_ref, other_comb_ref, ids_ref, place_ref,
                  out_ref, comb_ref):
    cap = SPECIALIST_CAP
    tokens, width = out_ref.shape
    comb = own_comb_ref[...] + other_comb_ref[...]
    comb = jnp.sum(place_ref[...] * comb, axis=0, keepdims=True)
    comb_ref[...] = jnp.where(ids_ref[...] == 0, comb, 0.0)
    side = hand_ref[tokens:, :].astype(F32)
    place = side[:cap, width:]
    gain = side[cap : cap + 1, :width] + side[cap + 1 : cap + 2, :width]
    gain = gain + side[cap + 2 : cap + 3, :width]
    normed, rms = normed_rows(side[:cap, :width])
    grad = hand_ref[:tokens, :width]
    own = take_rows(place.astype(BF16), grad)
    total = own_ref[...].astype(F32) + other_ref[...].astype(F32)
    scaled = total * gain
    inner = jnp.mean(scaled * normed, axis=-1, keepdims=True)
    rows = (own + (scaled - normed * inner) / rms).astype(BF16)
    back = place.T
    spread = take_rows(back.astype(BF16), rows)
    named = jnp.sum(back, axis=1, keepdims=True) > 0.0
    out_ref[...] = jnp.where(named, spread, grad.astype(F32)).astype(BF16)


def on_one(hidden_in, out_grad, expert_ids, route_weight, norm_gain, w_gate_up, w_down):
    sections = lax.axis_size("pipe")
    devices = lax.axis_size("expert")
    tokens, width = hidden_in.shape[1:]
    hidden = w_down.shape[2]
    cap = SPECIALIST_CAP
    ids = expert_ids[0].T
    weights = route_weight[0].T
    slab = w_gate_up.reshape(2 * hidden, width)
    down = w_down.reshape(hidden, width)
    in_hbm = lambda a: pltpu.with_memory_space_constraint(a, pltpu.HBM)
    wide = width + LANES
    total_rows = devices * cap

    def across(block, offset):
        return lax.ppermute(block, "expert", [(i, i ^ (2 * offset)) for i in range(devices)])

    def beside(block):
        return lax.ppermute(block, "expert", [(i, i ^ 1) for i in range(devices)])

    def handed(block, offset):
        route = [
            (((p + 1) % sections) * devices + i, p * devices + (i ^ (2 * offset)))
            for p in range(sections)
            for i in range(devices)
        ]
        return lax.ppermute(block, ("pipe", "expert"), route)

    rows, hand, place = call(
        rows_kernel,
        [((2 * cap, wide), BF16), ((tokens + 2 * cap, wide), BF16), ((cap, tokens), F32)],
        4 * tokens * width * cap,
        4 * tokens * width,
        in_specs=[IN_HBM] * 5,
        scratch=[
            pltpu.VMEM(ids.shape, ids.dtype),
            pltpu.VMEM(weights.shape, weights.dtype),
            pltpu.VMEM(norm_gain.shape, norm_gain.dtype),
            pltpu.VMEM((tokens, width), BF16),
            pltpu.SemaphoreType.DMA((5,)),
        ],
    )(*map(in_hbm, (ids, weights, norm_gain, hidden_in[0], out_grad[0])))
    far = across(rows, 2)
    near = across(rows, 1)
    farthest = across(far, 1)
    handed_block = handed(hand, 0)
    slab_near, down_near, rows_again = call(
        fetch_kernel,
        [(slab.shape, BF16), (down.shape, BF16), (rows.shape, BF16)],
        0,
        6 * hidden * width,
        in_specs=[IN_HBM, IN_HBM, IN_VMEM],
        scratch=[pltpu.SemaphoreType.DMA((2,))],
    )(in_hbm(slab), in_hbm(down), rows)
    lane = [rows, far, near, farthest]
    blocks = lane + [beside(b) for b in (rows_again, far, near, farthest)]
    keep, send, all_rows, both, act = call(
        hidden_kernel,
        [
            ((total_rows // 2, wide), BF16),
            ((total_rows // 2, wide), BF16),
            ((2 * total_rows, width), BF16),
            ((2 * hidden, 2 * total_rows), BF16),
            ((hidden, 2 * total_rows), BF16),
        ],
        10 * total_rows * hidden * width,
        6 * hidden * width,
    )(*blocks, slab_near, down_near)
    own_half, other_half = call(
        halve_kernel, [((2 * cap, wide), BF16)] * 2, 4 * cap * width, 16 * cap * width
    )(keep, beside(send))
    own, other, own_comb, other_comb = call(
        split_kernel,
        [((cap, width), BF16)] * 2 + [((cap, LANES), F32)] * 2,
        2 * cap * width,
        8 * cap * width,
    )(own_half, across(other_half, 1))
    gate_up_out, down_out = weight_grads(all_rows, both, act, own_comb)
    out, combined = call(
        finish_kernel,
        [((tokens, width), BF16), ((SPLIT, tokens), F32)],
        4 * tokens * width * cap,
        4 * tokens * width,
    )(handed(own, 0), handed(other, 2), handed_block, own_comb, across(other_comb, 2), ids, place)
    return (
        out[None],
        gate_up_out.reshape(1, 1, 2, hidden, width),
        down_out.reshape(1, 1, hidden, width),
        combined.T[None],
    )


def solution(mesh):
    on_device = on_one if mesh.shape["expert"] == SPLIT else on_many
    return jax.shard_map(
        on_device,
        mesh=mesh,
        in_specs=(
            P("pipe", "expert", None),
            P("pipe", "expert", None),
            P("pipe", "expert", None),
            P("pipe", "expert", None),
            P("pipe", None),
            P("pipe", "expert", None, None, None),
            P("pipe", "expert", None, None),
        ),
        out_specs=(
            P("pipe", "expert", None),
            P("pipe", "expert", None, None, None),
            P("pipe", "expert", None, None),
            P("pipe", "expert", None),
        ),
        check_vma=False,
    )
```

```python
import functools

import jax
import jax.numpy as jnp
from jax import lax
from jax.experimental import pallas as pl
from jax.experimental.pallas import tpu as pltpu
from jax.sharding import PartitionSpec as P

SPLIT = 8
SPECIALIST_CAP = 8
LANES = 128
EPS = 1e-06
F32 = jnp.float32
BF16 = jnp.bfloat16


def shifted(block, axis, distance):
    devices = range(lax.axis_size(axis))
    route = [((i - distance) % len(devices), i) for i in devices]
    return lax.ppermute(block, axis, route)


def rows_product(left_rows, right_rows):
    return lax.dot_general(
        left_rows, right_rows, (((1,), (1,)), ((), ())), preferred_element_type=jnp.float32
    )


def column_product(left_rows, right_rows):
    return lax.dot_general(
        left_rows, right_rows, (((0,), (0,)), ((), ())), preferred_element_type=jnp.float32
    )


def on_many(hidden_in, out_grad, expert_ids, route_weight, norm_gain, w_gate_up, w_down):
    tokens_in = hidden_in[0]
    grad_out = out_grad[0]
    chosen = expert_ids[0]
    weights_in = route_weight[0]
    gain_row = norm_gain[0]
    slab_gate_up = w_gate_up[0, 0]
    slab_down = w_down[0, 0]
    devices = lax.axis_size("expert")
    specialist_span = devices // SPLIT
    model_width = tokens_in.shape[1]
    hidden_slab = slab_down.shape[0]
    capacity = SPECIALIST_CAP
    tokens_f = tokens_in.astype(jnp.float32)
    rms_value = jnp.sqrt(jnp.mean(tokens_f * tokens_f, axis=-1, keepdims=True) + 1e-06)
    normed = tokens_f / rms_value
    normed_in = (normed * gain_row).astype(jnp.bfloat16)
    expert_range = jnp.arange(specialist_span, dtype=jnp.int32)
    picked = chosen[:, :, None] == expert_range[None, None, :]
    member = jnp.any(picked, axis=1).astype(jnp.int32)
    weight_te = jnp.sum(jnp.where(picked, weights_in.astype(jnp.float32)[:, :, None], 0.0), axis=1)
    position = jnp.cumsum(member, axis=0) - member
    slot_range = jnp.arange(capacity, dtype=jnp.int32)
    placing = (position.T[:, None, :] == slot_range[None, :, None]) & (member.T[:, None, :] == 1)
    place_bf = placing.astype(jnp.bfloat16)
    place_f = placing.astype(jnp.float32)
    sent_in = jnp.einsum(
        "wst,td->wsd", place_bf, normed_in, preferred_element_type=jnp.float32
    ).astype(jnp.bfloat16)
    sent_grad = jnp.einsum(
        "wst,td->wsd", place_bf, grad_out, preferred_element_type=jnp.float32
    ).astype(jnp.bfloat16)
    sent_weight = jnp.sum(place_f * weight_te.T[:, None, :], axis=-1).astype(jnp.bfloat16)
    rows_in, rows_grad, rows_weight = (
        lax.all_to_all(
            jnp.repeat(sent_in, SPLIT, axis=0), "expert", split_axis=0, concat_axis=0, tiled=True
        ),
        lax.all_to_all(
            jnp.repeat(sent_grad, SPLIT, axis=0), "expert", split_axis=0, concat_axis=0, tiled=True
        ),
        lax.all_to_all(
            jnp.repeat(sent_weight, SPLIT, axis=0),
            "expert",
            split_axis=0,
            concat_axis=0,
            tiled=True,
        ),
    )
    total_rows = devices * capacity
    flat_in = rows_in.reshape(total_rows, model_width)
    flat_grad = rows_grad.reshape(total_rows, model_width)
    flat_weight = rows_weight.reshape(total_rows, 1).astype(jnp.float32)
    joined_slab = slab_gate_up.reshape(2 * hidden_slab, model_width)
    projected = rows_product(flat_in, joined_slab)
    gate_pre = projected[:, :hidden_slab]
    up_pre = projected[:, hidden_slab:]
    sigmoid_gate = jax.nn.sigmoid(gate_pre)
    active = gate_pre * sigmoid_gate
    hidden_act = active * up_pre
    scaled_hidden = (flat_weight * hidden_act).astype(jnp.bfloat16)
    back_proj = rows_product(flat_grad, slab_down)
    grad_hidden = flat_weight * back_proj
    grad_gate = (
        grad_hidden * up_pre * sigmoid_gate * (1.0 + gate_pre * (1.0 - sigmoid_gate))
    ).astype(jnp.bfloat16)
    grad_up = (grad_hidden * active).astype(jnp.bfloat16)
    grad_both = jnp.concatenate([grad_gate, grad_up], axis=1)
    weight_grad = column_product(grad_both, flat_in)
    down_grad = column_product(scaled_hidden, flat_grad)
    input_part = (
        jnp.dot(grad_both, joined_slab, preferred_element_type=jnp.float32)
        .astype(jnp.bfloat16)
        .reshape(devices, capacity, model_width)
    )
    combine_part = (
        jnp.sum(hidden_act * back_proj, axis=-1).astype(jnp.bfloat16).reshape(devices, capacity)
    )
    returned_in, returned_comb = (
        lax.all_to_all(input_part, "expert", split_axis=0, concat_axis=0, tiled=True),
        lax.all_to_all(combine_part, "expert", split_axis=0, concat_axis=0, tiled=True),
    )
    summed_in = jnp.sum(
        returned_in.reshape(specialist_span, SPLIT, capacity, model_width).astype(jnp.float32),
        axis=1,
    )
    summed_comb = jnp.sum(
        returned_comb.reshape(specialist_span, SPLIT, capacity).astype(jnp.float32), axis=1
    )
    grad_normed = jnp.einsum("wst,wsd->td", place_f, summed_in, precision=lax.Precision.HIGHEST)
    comb_te = jnp.sum(place_f * summed_comb[:, :, None], axis=1)
    grad_combine = jnp.sum(jnp.where(picked, comb_te.T[:, None, :], 0.0), axis=-1)
    scaled = grad_normed * gain_row
    inner_mean = jnp.mean(scaled * normed, axis=-1, keepdims=True)
    grad_tokens = (
        grad_out.astype(jnp.float32) + (scaled - normed * inner_mean) / rms_value
    ).astype(jnp.bfloat16)
    handed = shifted(grad_tokens, "pipe", -1)
    gate_up_out = weight_grad.reshape(2, hidden_slab, model_width).astype(jnp.bfloat16)
    return (
        handed[None],
        gate_up_out[None, None],
        down_grad.astype(jnp.bfloat16)[None, None],
        grad_combine[None],
    )


def call(kernel, outs, flops, moved, in_specs=None, scratch=(), limit=24):
    given = {} if in_specs is None else {"in_specs": in_specs}
    return pl.pallas_call(
        kernel,
        **given,
        out_shape=[jax.ShapeDtypeStruct(shape, kind) for shape, kind in outs],
        scratch_shapes=list(scratch),
        compiler_params=pltpu.CompilerParams(vmem_limit_bytes=limit << 20),
        cost_estimate=pl.CostEstimate(flops=flops, bytes_accessed=moved, transcendentals=0),
    )


IN_HBM = pl.BlockSpec(memory_space=pltpu.HBM)
IN_VMEM = pl.BlockSpec(memory_space=pltpu.VMEM)


def take_rows(place, block):
    return lax.dot_general(place, block, (((1,), (0,)), ((), ())), preferred_element_type=F32)


def normed_rows(rows):
    rms = jnp.sqrt(jnp.mean(rows * rows, axis=-1, keepdims=True) + EPS)
    return rows / rms, rms


def in_parts(values):
    high = values.astype(BF16).astype(F32)
    middle = (values - high).astype(BF16).astype(F32)
    return high, middle, values - high - middle


def rows_kernel(ids_hbm, weight_hbm, gain_hbm, hidden_hbm, grad_hbm, rows_ref, normed_ref, place_ref,
                ids_ref, weight_ref, gain_ref, hidden_ref, grad_ref, sems):
    tokens, width = hidden_ref.shape
    cap = SPECIALIST_CAP
    copies = [
        pltpu.make_async_copy(src, dst, sems.at[i])
        for i, (src, dst) in enumerate([
            (ids_hbm, ids_ref),
            (hidden_hbm, hidden_ref),
            (gain_hbm, gain_ref),
            (weight_hbm, weight_ref),
            (grad_hbm, grad_ref),
        ])
    ]
    for copy in copies:
        copy.start()
    copies[0].wait()
    hit = ids_ref[...] == 0
    member = jnp.max(hit.astype(F32), axis=0, keepdims=True)
    member = jnp.broadcast_to(member, (cap, tokens))
    earlier = lax.broadcasted_iota(jnp.int32, (tokens, tokens), 0) < lax.broadcasted_iota(
        jnp.int32, (tokens, tokens), 1
    )
    position = take_rows(member.astype(BF16), earlier.astype(F32).astype(BF16))
    slot = lax.broadcasted_iota(jnp.int32, (cap, tokens), 0).astype(F32)
    place = jnp.where(position == slot, member, 0.0)
    place_ref[...] = place
    copies[1].wait()
    normed, rms = normed_rows(take_rows(place.astype(BF16), hidden_ref[...]))
    normed_ref[...] = normed
    copies[2].wait()
    normed_in = normed * gain_ref[...]
    copies[3].wait()
    weight = jnp.sum(
        jnp.where(hit, weight_ref[...].astype(F32), 0.0), axis=0, keepdims=True
    )
    taken = jnp.sum(place * weight, axis=1, keepdims=True)
    lane = lax.broadcasted_iota(jnp.int32, (cap, LANES), 1)
    extra = jnp.broadcast_to(taken, (cap, LANES))
    for number, part in enumerate(in_parts(rms)):
        extra = jnp.where(lane == number + 1, part, extra)
    rows_ref[:, width:] = jnp.concatenate([extra, place], axis=0).astype(BF16)
    copies[4].wait()
    grad = take_rows(place.astype(BF16), grad_ref[...])
    rows_ref[:, :width] = jnp.concatenate([normed_in, grad], axis=0).astype(BF16)


def fetch_kernel(slab_hbm, down_hbm, rows_ref, slab_ref, down_ref, again_ref, sems):
    first = pltpu.make_async_copy(slab_hbm, slab_ref, sems.at[0])
    second = pltpu.make_async_copy(down_hbm, down_ref, sems.at[1])
    first.start()
    second.start()
    again_ref[...] = rows_ref[...]
    first.wait()
    second.wait()


def halves(rows, cap):
    blocks = range(rows.shape[0] // (2 * cap))
    return [
        jnp.concatenate([rows[(2 * b + h) * cap : (2 * b + h + 1) * cap] for b in blocks], axis=0)
        for h in (0, 1)
    ]


def padded(rows, half, cap):
    blank = jnp.zeros((cap, rows.shape[1]), rows.dtype)
    pieces = []
    for b in range(rows.shape[0] // cap):
        own = rows[b * cap : (b + 1) * cap]
        pieces += [own, blank] if half == 0 else [blank, own]
    return jnp.concatenate(pieces, axis=0)


def hidden_kernel(*refs):
    *blocks, slab_ref, down_ref, keep_ref, send_ref, rows_ref, both_ref, act_ref = refs
    hidden, width = down_ref.shape
    half = keep_ref.shape[0]
    cap = SPECIALIST_CAP
    rows = jnp.concatenate([r[:, :width] for r in blocks], axis=0)
    rows_ref[...] = rows
    pre, _ = halves(rows_product(rows, slab_ref[...]), cap)
    _, back = halves(rows_product(rows, down_ref[...]), cap)
    weight = jnp.concatenate([r[:, width:].astype(F32)[:cap, :1] for r in blocks], axis=0)
    gate = pre[:, :hidden]
    up = pre[:, hidden:]
    sig = jax.nn.sigmoid(gate)
    active = gate * sig
    act = active * up
    into = weight * back
    both = jnp.concatenate(
        [into * up * sig * (1.0 + gate * (1.0 - sig)), into * active], axis=1
    )
    part = take_rows(both.astype(BF16), slab_ref[...]).astype(BF16)
    send_ref[:, :width] = part[half:]
    keep_ref[:, :width] = part[:half]
    comb = jnp.sum(act * back, axis=1, keepdims=True)
    comb = jnp.broadcast_to(comb, (2 * half, LANES)).astype(BF16)
    send_ref[:, width:] = comb[half:]
    keep_ref[:, width:] = comb[:half]
    both_ref[...] = padded(both, 0, cap).T.astype(BF16)
    act_ref[...] = padded(weight * act, 1, cap).T.astype(BF16)


def halve_kernel(keep_ref, got_ref, own_ref, other_ref):
    total = keep_ref[...].astype(F32) + got_ref[...].astype(F32)
    half = own_ref.shape[0]
    width = own_ref.shape[1] - LANES
    other_ref[:, :width] = total[half:, :width].astype(BF16)
    own_ref[:, :width] = total[:half, :width].astype(BF16)
    comb = total[:, width:]
    high = comb.astype(BF16).astype(F32)
    lane = lax.broadcasted_iota(jnp.int32, comb.shape, 1)
    comb = jnp.where(lane < LANES // 2, high, comb - high).astype(BF16)
    other_ref[:, width:] = comb[half:]
    own_ref[:, width:] = comb[:half]


def split_kernel(keep_ref, got_ref, normed_ref, rows_ref, far_ref, gain_ref, after_ref,
                 own_ref, other_ref, own_comb_ref, other_comb_ref):
    del after_ref
    cap, width = own_ref.shape
    total = keep_ref[...].astype(F32) + got_ref[...].astype(F32)
    gain = gain_ref[...]
    far = far_ref[...].astype(F32)
    extra = jnp.concatenate([rows_ref[:, width:].astype(F32)[:cap], far[:cap, width:]], axis=0)
    rms = extra[:, 1:2] + extra[:, 2:3] + extra[:, 3:4]
    normed = jnp.concatenate([normed_ref[...], far[:cap, :width] / gain], axis=0)
    scaled = total[:, :width] * gain
    inner = jnp.mean(scaled * normed, axis=-1, keepdims=True)
    change = (scaled - normed * inner) / rms
    other_ref[:, :width] = change[cap:].astype(BF16)
    other_ref[:, width:] = far[cap:, width:].astype(BF16)
    own_ref[...] = change[:cap].astype(BF16)
    comb = total[:, width:]
    comb = comb + pltpu.roll(comb, LANES // 2, 1)
    other_comb_ref[...] = comb[cap:]
    own_comb_ref[...] = comb[:cap]


def weights_kernel(rows_ref, both_ref, act_ref, after_ref, both_out, act_out):
    del after_ref
    chunk = both_out.shape[1]
    rows = rows_ref[:, pl.ds(pl.multiple_of(pl.program_id(0) * chunk, chunk), chunk)]
    both_out[...] = take_rows(both_ref[...], rows).astype(BF16)
    act_out[...] = take_rows(act_ref[...], rows).astype(BF16)


def weight_grads(rows, both, act, after):
    width = rows.shape[1]
    hidden = act.shape[0]
    chunk = min(width, 1024)
    across = lambda count: pl.BlockSpec((count, chunk), lambda i: (0, i))
    return pl.pallas_call(
        weights_kernel,
        grid=(width // chunk,),
        in_specs=[IN_VMEM, IN_VMEM, IN_VMEM, pl.BlockSpec(memory_space=pl.ANY)],
        out_specs=[across(2 * hidden), across(hidden)],
        out_shape=[
            jax.ShapeDtypeStruct((2 * hidden, width), BF16),
            jax.ShapeDtypeStruct((hidden, width), BF16),
        ],
        compiler_params=pltpu.CompilerParams(vmem_limit_bytes=24 << 20),
        cost_estimate=pl.CostEstimate(
            flops=6 * rows.shape[0] * hidden * width,
            bytes_accessed=6 * hidden * width,
            transcendentals=0,
        ),
    )(rows, both, act, after)


def finish_kernel(other_ref, own_ref, grad_ref, other_comb_ref, own_comb_ref, ids_ref, place_ref,
                  out_ref, comb_ref):
    width = grad_ref.shape[1]
    chunk = out_ref.shape[1]

    @pl.when(pl.program_id(0) == 0)
    def _():
        comb = own_comb_ref[...] + other_comb_ref[...]
        comb = jnp.sum(place_ref[...] * comb, axis=0, keepdims=True)
        comb_ref[...] = jnp.where(ids_ref[...] == 0, comb, 0.0)

    columns = pl.ds(pl.multiple_of(pl.program_id(0) * chunk, chunk), chunk)
    place = other_ref[:, width:]
    grad = grad_ref[:, columns]
    change = own_ref[:, columns].astype(F32) + other_ref[:, columns].astype(F32)
    rows = (take_rows(place, grad) + change).astype(BF16)
    back = place.astype(F32).T
    spread = take_rows(back.astype(BF16), rows)
    named = jnp.sum(back, axis=1, keepdims=True) > 0.0
    out_ref[...] = jnp.where(named, spread, grad.astype(F32)).astype(BF16)


def finish(other, own, grad, other_comb, own_comb, ids, place):
    tokens, width = grad.shape
    chunk = min(width, 1024)
    return pl.pallas_call(
        finish_kernel,
        grid=(width // chunk,),
        in_specs=[IN_VMEM] * 7,
        out_specs=[
            pl.BlockSpec((tokens, chunk), lambda i: (0, i)),
            pl.BlockSpec(ids.shape, lambda i: (0, 0)),
        ],
        out_shape=[
            jax.ShapeDtypeStruct((tokens, width), BF16),
            jax.ShapeDtypeStruct(ids.shape, F32),
        ],
        compiler_params=pltpu.CompilerParams(vmem_limit_bytes=24 << 20),
        cost_estimate=pl.CostEstimate(
            flops=4 * tokens * width * place.shape[0],
            bytes_accessed=4 * tokens * width,
            transcendentals=0,
        ),
    )(other, own, grad, other_comb, own_comb, ids, place)


def on_one(hidden_in, out_grad, expert_ids, route_weight, norm_gain, w_gate_up, w_down):
    sections = lax.axis_size("pipe")
    devices = lax.axis_size("expert")
    tokens, width = hidden_in.shape[1:]
    hidden = w_down.shape[2]
    cap = SPECIALIST_CAP
    ids = expert_ids[0].T
    weights = route_weight[0].T
    slab = w_gate_up.reshape(2 * hidden, width)
    down = w_down.reshape(hidden, width)
    in_hbm = lambda a: pltpu.with_memory_space_constraint(a, pltpu.HBM)
    wide = width + LANES
    total_rows = devices * cap

    def across(block, offset):
        return lax.ppermute(block, "expert", [(i, i ^ (2 * offset)) for i in range(devices)])

    def beside(block):
        return lax.ppermute(block, "expert", [(i, i ^ 1) for i in range(devices)])

    def handed(block, offset):
        route = [
            (((p + 1) % sections) * devices + i, p * devices + (i ^ (2 * offset)))
            for p in range(sections)
            for i in range(devices)
        ]
        return lax.ppermute(block, ("pipe", "expert"), route)

    next_grad = handed(out_grad[0], 0)
    rows, normed, place = call(
        rows_kernel,
        [((2 * cap, wide), BF16), ((cap, width), F32), ((cap, tokens), F32)],
        4 * tokens * width * cap,
        4 * tokens * width,
        in_specs=[IN_HBM] * 5,
        scratch=[
            pltpu.VMEM(ids.shape, ids.dtype),
            pltpu.VMEM(weights.shape, weights.dtype),
            pltpu.VMEM(norm_gain.shape, norm_gain.dtype),
            pltpu.VMEM((tokens, width), BF16),
            pltpu.VMEM((tokens, width), BF16),
            pltpu.SemaphoreType.DMA((5,)),
        ],
    )(*map(in_hbm, (ids, weights, norm_gain, hidden_in[0], out_grad[0])))
    far = across(rows, 2)
    near = across(rows, 1)
    farthest = across(far, 1)
    slab_near, down_near, rows_again = call(
        fetch_kernel,
        [(slab.shape, BF16), (down.shape, BF16), (rows.shape, BF16)],
        0,
        6 * hidden * width,
        in_specs=[IN_HBM, IN_HBM, IN_VMEM],
        scratch=[pltpu.SemaphoreType.DMA((2,))],
    )(in_hbm(slab), in_hbm(down), rows)
    lane = [rows, far, near, farthest]
    blocks = lane + [beside(b) for b in (rows_again, far, near, farthest)]
    keep, send, all_rows, both, act = call(
        hidden_kernel,
        [
            ((total_rows // 2, wide), BF16),
            ((total_rows // 2, wide), BF16),
            ((2 * total_rows, width), BF16),
            ((2 * hidden, 2 * total_rows), BF16),
            ((hidden, 2 * total_rows), BF16),
        ],
        10 * total_rows * hidden * width,
        6 * hidden * width,
    )(*blocks, slab_near, down_near)
    own_half, other_half = call(
        halve_kernel, [((2 * cap, wide), BF16)] * 2, 4 * cap * width, 16 * cap * width
    )(keep, beside(send))
    gate_up_out, down_out = weight_grads(all_rows, both, act, own_half)
    own, other, own_comb, other_comb = call(
        split_kernel,
        [((cap, width), BF16), ((cap, wide), BF16)] + [((cap, LANES), F32)] * 2,
        2 * cap * width,
        8 * cap * width,
        in_specs=[IN_VMEM] * 6 + [IN_HBM],
    )(own_half, across(other_half, 1), normed, rows, far, norm_gain, in_hbm(down_out))
    out, combined = finish(
        handed(other, 2), handed(own, 0), next_grad, across(other_comb, 2), own_comb, ids, place
    )
    return (
        out[None],
        gate_up_out.reshape(1, 1, 2, hidden, width),
        down_out.reshape(1, 1, hidden, width),
        combined.T[None],
    )


def solution(mesh):
    on_device = on_one if mesh.shape["expert"] == SPLIT else on_many
    return jax.shard_map(
        on_device,
        mesh=mesh,
        in_specs=(
            P("pipe", "expert", None),
            P("pipe", "expert", None),
            P("pipe", "expert", None),
            P("pipe", "expert", None),
            P("pipe", None),
            P("pipe", "expert", None, None, None),
            P("pipe", "expert", None, None),
        ),
        out_specs=(
            P("pipe", "expert", None),
            P("pipe", "expert", None, None, None),
            P("pipe", "expert", None, None),
            P("pipe", "expert", None),
        ),
        check_vma=False,
    )
```

```python
import functools

import jax
import jax.numpy as jnp
from jax import lax
from jax.experimental import pallas as pl
from jax.experimental.pallas import tpu as pltpu
from jax.sharding import PartitionSpec as P

SPLIT = 8
SPECIALIST_CAP = 8
LANES = 128
EPS = 1e-06
F32 = jnp.float32
BF16 = jnp.bfloat16


def shifted(block, axis, distance):
    devices = range(lax.axis_size(axis))
    route = [((i - distance) % len(devices), i) for i in devices]
    return lax.ppermute(block, axis, route)


def rows_product(left_rows, right_rows):
    return lax.dot_general(
        left_rows, right_rows, (((1,), (1,)), ((), ())), preferred_element_type=jnp.float32
    )


def column_product(left_rows, right_rows):
    return lax.dot_general(
        left_rows, right_rows, (((0,), (0,)), ((), ())), preferred_element_type=jnp.float32
    )


def on_many(hidden_in, out_grad, expert_ids, route_weight, norm_gain, w_gate_up, w_down):
    tokens_in = hidden_in[0]
    grad_out = out_grad[0]
    chosen = expert_ids[0]
    weights_in = route_weight[0]
    gain_row = norm_gain[0]
    slab_gate_up = w_gate_up[0, 0]
    slab_down = w_down[0, 0]
    devices = lax.axis_size("expert")
    specialist_span = devices // SPLIT
    model_width = tokens_in.shape[1]
    hidden_slab = slab_down.shape[0]
    capacity = SPECIALIST_CAP
    tokens_f = tokens_in.astype(jnp.float32)
    rms_value = jnp.sqrt(jnp.mean(tokens_f * tokens_f, axis=-1, keepdims=True) + 1e-06)
    normed = tokens_f / rms_value
    normed_in = (normed * gain_row).astype(jnp.bfloat16)
    expert_range = jnp.arange(specialist_span, dtype=jnp.int32)
    picked = chosen[:, :, None] == expert_range[None, None, :]
    member = jnp.any(picked, axis=1).astype(jnp.int32)
    weight_te = jnp.sum(jnp.where(picked, weights_in.astype(jnp.float32)[:, :, None], 0.0), axis=1)
    position = jnp.cumsum(member, axis=0) - member
    slot_range = jnp.arange(capacity, dtype=jnp.int32)
    placing = (position.T[:, None, :] == slot_range[None, :, None]) & (member.T[:, None, :] == 1)
    place_bf = placing.astype(jnp.bfloat16)
    place_f = placing.astype(jnp.float32)
    sent_in = jnp.einsum(
        "wst,td->wsd", place_bf, normed_in, preferred_element_type=jnp.float32
    ).astype(jnp.bfloat16)
    sent_grad = jnp.einsum(
        "wst,td->wsd", place_bf, grad_out, preferred_element_type=jnp.float32
    ).astype(jnp.bfloat16)
    sent_weight = jnp.sum(place_f * weight_te.T[:, None, :], axis=-1).astype(jnp.bfloat16)
    rows_in, rows_grad, rows_weight = (
        lax.all_to_all(
            jnp.repeat(sent_in, SPLIT, axis=0), "expert", split_axis=0, concat_axis=0, tiled=True
        ),
        lax.all_to_all(
            jnp.repeat(sent_grad, SPLIT, axis=0), "expert", split_axis=0, concat_axis=0, tiled=True
        ),
        lax.all_to_all(
            jnp.repeat(sent_weight, SPLIT, axis=0),
            "expert",
            split_axis=0,
            concat_axis=0,
            tiled=True,
        ),
    )
    total_rows = devices * capacity
    flat_in = rows_in.reshape(total_rows, model_width)
    flat_grad = rows_grad.reshape(total_rows, model_width)
    flat_weight = rows_weight.reshape(total_rows, 1).astype(jnp.float32)
    joined_slab = slab_gate_up.reshape(2 * hidden_slab, model_width)
    projected = rows_product(flat_in, joined_slab)
    gate_pre = projected[:, :hidden_slab]
    up_pre = projected[:, hidden_slab:]
    sigmoid_gate = jax.nn.sigmoid(gate_pre)
    active = gate_pre * sigmoid_gate
    hidden_act = active * up_pre
    scaled_hidden = (flat_weight * hidden_act).astype(jnp.bfloat16)
    back_proj = rows_product(flat_grad, slab_down)
    grad_hidden = flat_weight * back_proj
    grad_gate = (
        grad_hidden * up_pre * sigmoid_gate * (1.0 + gate_pre * (1.0 - sigmoid_gate))
    ).astype(jnp.bfloat16)
    grad_up = (grad_hidden * active).astype(jnp.bfloat16)
    grad_both = jnp.concatenate([grad_gate, grad_up], axis=1)
    weight_grad = column_product(grad_both, flat_in)
    down_grad = column_product(scaled_hidden, flat_grad)
    input_part = (
        jnp.dot(grad_both, joined_slab, preferred_element_type=jnp.float32)
        .astype(jnp.bfloat16)
        .reshape(devices, capacity, model_width)
    )
    combine_part = (
        jnp.sum(hidden_act * back_proj, axis=-1).astype(jnp.bfloat16).reshape(devices, capacity)
    )
    returned_in, returned_comb = (
        lax.all_to_all(input_part, "expert", split_axis=0, concat_axis=0, tiled=True),
        lax.all_to_all(combine_part, "expert", split_axis=0, concat_axis=0, tiled=True),
    )
    summed_in = jnp.sum(
        returned_in.reshape(specialist_span, SPLIT, capacity, model_width).astype(jnp.float32),
        axis=1,
    )
    summed_comb = jnp.sum(
        returned_comb.reshape(specialist_span, SPLIT, capacity).astype(jnp.float32), axis=1
    )
    grad_normed = jnp.einsum("wst,wsd->td", place_f, summed_in, precision=lax.Precision.HIGHEST)
    comb_te = jnp.sum(place_f * summed_comb[:, :, None], axis=1)
    grad_combine = jnp.sum(jnp.where(picked, comb_te.T[:, None, :], 0.0), axis=-1)
    scaled = grad_normed * gain_row
    inner_mean = jnp.mean(scaled * normed, axis=-1, keepdims=True)
    grad_tokens = (
        grad_out.astype(jnp.float32) + (scaled - normed * inner_mean) / rms_value
    ).astype(jnp.bfloat16)
    handed = shifted(grad_tokens, "pipe", -1)
    gate_up_out = weight_grad.reshape(2, hidden_slab, model_width).astype(jnp.bfloat16)
    return (
        handed[None],
        gate_up_out[None, None],
        down_grad.astype(jnp.bfloat16)[None, None],
        grad_combine[None],
    )


def call(kernel, outs, flops, moved, in_specs=None, scratch=(), limit=24):
    given = {} if in_specs is None else {"in_specs": in_specs}
    return pl.pallas_call(
        kernel,
        **given,
        out_shape=[jax.ShapeDtypeStruct(shape, kind) for shape, kind in outs],
        scratch_shapes=list(scratch),
        compiler_params=pltpu.CompilerParams(vmem_limit_bytes=limit << 20),
        cost_estimate=pl.CostEstimate(flops=flops, bytes_accessed=moved, transcendentals=0),
    )


IN_HBM = pl.BlockSpec(memory_space=pltpu.HBM)
IN_VMEM = pl.BlockSpec(memory_space=pltpu.VMEM)


def take_rows(place, block):
    return lax.dot_general(place, block, (((1,), (0,)), ((), ())), preferred_element_type=F32)


def normed_rows(rows):
    rms = jnp.sqrt(jnp.mean(rows * rows, axis=-1, keepdims=True) + EPS)
    return rows / rms, rms


def in_parts(values):
    high = values.astype(BF16).astype(F32)
    middle = (values - high).astype(BF16).astype(F32)
    return high, middle, values - high - middle


def rows_kernel(ids_hbm, weight_hbm, gain_hbm, hidden_hbm, grad_hbm, rows_ref, normed_ref, place_ref,
                ids_ref, weight_ref, gain_ref, hidden_ref, grad_ref, sems):
    tokens, width = hidden_ref.shape
    cap = SPECIALIST_CAP
    copies = [
        pltpu.make_async_copy(src, dst, sems.at[i])
        for i, (src, dst) in enumerate([
            (ids_hbm, ids_ref),
            (hidden_hbm, hidden_ref),
            (gain_hbm, gain_ref),
            (weight_hbm, weight_ref),
            (grad_hbm, grad_ref),
        ])
    ]
    for copy in copies:
        copy.start()
    copies[0].wait()
    hit = ids_ref[...] == 0
    member = jnp.max(hit.astype(F32), axis=0, keepdims=True)
    member = jnp.broadcast_to(member, (cap, tokens))
    earlier = lax.broadcasted_iota(jnp.int32, (tokens, tokens), 0) < lax.broadcasted_iota(
        jnp.int32, (tokens, tokens), 1
    )
    position = take_rows(member.astype(BF16), earlier.astype(F32).astype(BF16))
    slot = lax.broadcasted_iota(jnp.int32, (cap, tokens), 0).astype(F32)
    place = jnp.where(position == slot, member, 0.0)
    place_ref[...] = place
    copies[1].wait()
    normed, rms = normed_rows(take_rows(place.astype(BF16), hidden_ref[...]))
    normed_ref[...] = normed
    copies[2].wait()
    normed_in = normed * gain_ref[...]
    copies[3].wait()
    weight = jnp.sum(
        jnp.where(hit, weight_ref[...].astype(F32), 0.0), axis=0, keepdims=True
    )
    taken = jnp.sum(place * weight, axis=1, keepdims=True)
    lane = lax.broadcasted_iota(jnp.int32, (cap, LANES), 1)
    extra = jnp.broadcast_to(taken, (cap, LANES))
    for number, part in enumerate(in_parts(rms)):
        extra = jnp.where(lane == number + 1, part, extra)
    rows_ref[:, width:] = jnp.concatenate([extra, place], axis=0).astype(BF16)
    copies[4].wait()
    grad = take_rows(place.astype(BF16), grad_ref[...])
    rows_ref[:, :width] = jnp.concatenate([normed_in, grad], axis=0).astype(BF16)


def fetch_kernel(slab_hbm, down_hbm, rows_ref, slab_ref, down_ref, again_ref, sems):
    first = pltpu.make_async_copy(slab_hbm, slab_ref, sems.at[0])
    second = pltpu.make_async_copy(down_hbm, down_ref, sems.at[1])
    first.start()
    second.start()
    again_ref[...] = rows_ref[...]
    first.wait()
    second.wait()


def halves(rows, cap):
    blocks = range(rows.shape[0] // (2 * cap))
    return [
        jnp.concatenate([rows[(2 * b + h) * cap : (2 * b + h + 1) * cap] for b in blocks], axis=0)
        for h in (0, 1)
    ]


def padded(rows, half, cap):
    blank = jnp.zeros((cap, rows.shape[1]), rows.dtype)
    pieces = []
    for b in range(rows.shape[0] // cap):
        own = rows[b * cap : (b + 1) * cap]
        pieces += [own, blank] if half == 0 else [blank, own]
    return jnp.concatenate(pieces, axis=0)


def hidden_kernel(*refs):
    *blocks, slab_ref, down_ref, keep_ref, send_ref, rows_ref, both_ref, act_ref = refs
    hidden, width = down_ref.shape
    half = keep_ref.shape[0]
    cap = SPECIALIST_CAP
    rows = jnp.concatenate([r[:, :width] for r in blocks], axis=0)
    rows_ref[...] = rows
    pre, _ = halves(rows_product(rows, slab_ref[...]), cap)
    _, back = halves(rows_product(rows, down_ref[...]), cap)
    weight = jnp.concatenate([r[:, width:].astype(F32)[:cap, :1] for r in blocks], axis=0)
    gate = pre[:, :hidden]
    up = pre[:, hidden:]
    sig = jax.nn.sigmoid(gate)
    active = gate * sig
    act = active * up
    into = weight * back
    both = jnp.concatenate(
        [into * up * sig * (1.0 + gate * (1.0 - sig)), into * active], axis=1
    )
    part = take_rows(both.astype(BF16), slab_ref[...]).astype(BF16)
    send_ref[:, :width] = part[half:]
    keep_ref[:, :width] = part[:half]
    comb = jnp.sum(act * back, axis=1, keepdims=True)
    comb = jnp.broadcast_to(comb, (2 * half, LANES)).astype(BF16)
    send_ref[:, width:] = comb[half:]
    keep_ref[:, width:] = comb[:half]
    both_ref[...] = padded(both, 0, cap).T.astype(BF16)
    act_ref[...] = padded(weight * act, 1, cap).T.astype(BF16)


def halve_kernel(keep_ref, got_ref, own_ref, other_ref):
    total = keep_ref[...].astype(F32) + got_ref[...].astype(F32)
    half = own_ref.shape[0]
    width = own_ref.shape[1] - LANES
    other_ref[:, :width] = total[half:, :width].astype(BF16)
    own_ref[:, :width] = total[:half, :width].astype(BF16)
    comb = total[:, width:]
    high = comb.astype(BF16).astype(F32)
    lane = lax.broadcasted_iota(jnp.int32, comb.shape, 1)
    comb = jnp.where(lane < LANES // 2, high, comb - high).astype(BF16)
    other_ref[:, width:] = comb[half:]
    own_ref[:, width:] = comb[:half]


def split_kernel(keep_ref, got_ref, normed_ref, rows_ref, far_ref, gain_ref, after_ref,
                 own_ref, other_ref, own_comb_ref, other_comb_ref):
    del after_ref
    cap, width = own_ref.shape
    total = keep_ref[...].astype(F32) + got_ref[...].astype(F32)
    gain = gain_ref[...]
    far = far_ref[...].astype(F32)
    extra = jnp.concatenate([rows_ref[:, width:].astype(F32)[:cap], far[:cap, width:]], axis=0)
    rms = extra[:, 1:2] + extra[:, 2:3] + extra[:, 3:4]
    normed = jnp.concatenate([normed_ref[...], far[:cap, :width] / gain], axis=0)
    scaled = total[:, :width] * gain
    inner = jnp.mean(scaled * normed, axis=-1, keepdims=True)
    change = (scaled - normed * inner) / rms
    other_ref[:, :width] = change[cap:].astype(BF16)
    other_ref[:, width:] = far[cap:, width:].astype(BF16)
    own_ref[...] = change[:cap].astype(BF16)
    comb = total[:, width:]
    comb = comb + pltpu.roll(comb, LANES // 2, 1)
    other_comb_ref[...] = comb[cap:]
    own_comb_ref[...] = comb[:cap]


def weights_kernel(rows_ref, both_ref, act_ref, after_ref, both_out, act_out):
    del after_ref
    chunk = both_out.shape[1]
    rows = rows_ref[:, pl.ds(pl.multiple_of(pl.program_id(0) * chunk, chunk), chunk)]
    both_out[...] = take_rows(both_ref[...], rows).astype(BF16)
    act_out[...] = take_rows(act_ref[...], rows).astype(BF16)


def weight_grads(rows, both, act, after):
    width = rows.shape[1]
    hidden = act.shape[0]
    chunk = min(width, 1024)
    across = lambda count: pl.BlockSpec((count, chunk), lambda i: (0, i))
    return pl.pallas_call(
        weights_kernel,
        grid=(width // chunk,),
        in_specs=[IN_VMEM, IN_VMEM, IN_VMEM, pl.BlockSpec(memory_space=pl.ANY)],
        out_specs=[across(2 * hidden), across(hidden)],
        out_shape=[
            jax.ShapeDtypeStruct((2 * hidden, width), BF16),
            jax.ShapeDtypeStruct((hidden, width), BF16),
        ],
        compiler_params=pltpu.CompilerParams(vmem_limit_bytes=24 << 20),
        cost_estimate=pl.CostEstimate(
            flops=6 * rows.shape[0] * hidden * width,
            bytes_accessed=6 * hidden * width,
            transcendentals=0,
        ),
    )(rows, both, act, after)


def finish_kernel(other_ref, own_ref, grad_ref, other_comb_ref, own_comb_ref, ids_ref, place_ref,
                  out_ref, comb_ref):
    width = grad_ref.shape[1]
    comb = own_comb_ref[...] + other_comb_ref[...]
    comb = jnp.sum(place_ref[...] * comb, axis=0, keepdims=True)
    comb_ref[...] = jnp.where(ids_ref[...] == 0, comb, 0.0)
    place = other_ref[:, width:]
    grad = grad_ref[...]
    own = take_rows(place, grad)
    change = own_ref[...].astype(F32) + other_ref[:, :width].astype(F32)
    rows = (own + change).astype(BF16)
    back = place.astype(F32).T
    spread = take_rows(back.astype(BF16), rows)
    named = jnp.sum(back, axis=1, keepdims=True) > 0.0
    out_ref[...] = jnp.where(named, spread, grad.astype(F32)).astype(BF16)


def on_one(hidden_in, out_grad, expert_ids, route_weight, norm_gain, w_gate_up, w_down):
    sections = lax.axis_size("pipe")
    devices = lax.axis_size("expert")
    tokens, width = hidden_in.shape[1:]
    hidden = w_down.shape[2]
    cap = SPECIALIST_CAP
    ids = expert_ids[0].T
    weights = route_weight[0].T
    slab = w_gate_up.reshape(2 * hidden, width)
    down = w_down.reshape(hidden, width)
    in_hbm = lambda a: pltpu.with_memory_space_constraint(a, pltpu.HBM)
    wide = width + LANES
    total_rows = devices * cap

    def across(block, offset):
        return lax.ppermute(block, "expert", [(i, i ^ (2 * offset)) for i in range(devices)])

    def beside(block):
        return lax.ppermute(block, "expert", [(i, i ^ 1) for i in range(devices)])

    def handed(block, offset):
        route = [
            (((p + 1) % sections) * devices + i, p * devices + (i ^ (2 * offset)))
            for p in range(sections)
            for i in range(devices)
        ]
        return lax.ppermute(block, ("pipe", "expert"), route)

    next_grad = handed(out_grad[0], 0)
    rows, normed, place = call(
        rows_kernel,
        [((2 * cap, wide), BF16), ((cap, width), F32), ((cap, tokens), F32)],
        4 * tokens * width * cap,
        4 * tokens * width,
        in_specs=[IN_HBM] * 5,
        scratch=[
            pltpu.VMEM(ids.shape, ids.dtype),
            pltpu.VMEM(weights.shape, weights.dtype),
            pltpu.VMEM(norm_gain.shape, norm_gain.dtype),
            pltpu.VMEM((tokens, width), BF16),
            pltpu.VMEM((tokens, width), BF16),
            pltpu.SemaphoreType.DMA((5,)),
        ],
    )(*map(in_hbm, (ids, weights, norm_gain, hidden_in[0], out_grad[0])))
    far = across(rows, 2)
    near = across(rows, 1)
    farthest = across(far, 1)
    slab_near, down_near, rows_again = call(
        fetch_kernel,
        [(slab.shape, BF16), (down.shape, BF16), (rows.shape, BF16)],
        30_000_000_000,
        6 * hidden * width,
        in_specs=[IN_HBM, IN_HBM, IN_VMEM],
        scratch=[pltpu.SemaphoreType.DMA((2,))],
    )(in_hbm(slab), in_hbm(down), rows)
    lane = [rows, far, near, farthest]
    blocks = lane + [beside(b) for b in (rows_again, far, near, farthest)]
    keep, send, all_rows, both, act = call(
        hidden_kernel,
        [
            ((total_rows // 2, wide), BF16),
            ((total_rows // 2, wide), BF16),
            ((2 * total_rows, width), BF16),
            ((2 * hidden, 2 * total_rows), BF16),
            ((hidden, 2 * total_rows), BF16),
        ],
        10 * total_rows * hidden * width,
        6 * hidden * width,
    )(*blocks, slab_near, down_near)
    own_half, other_half = call(
        halve_kernel, [((2 * cap, wide), BF16)] * 2, 4 * cap * width, 16 * cap * width
    )(keep, beside(send))
    gate_up_out, down_out = weight_grads(all_rows, both, act, own_half)
    own, other, own_comb, other_comb = call(
        split_kernel,
        [((cap, width), BF16), ((cap, wide), BF16)] + [((cap, LANES), F32)] * 2,
        2 * cap * width,
        8 * cap * width,
        in_specs=[IN_VMEM] * 6 + [IN_HBM],
    )(own_half, across(other_half, 1), normed, rows, far, norm_gain, in_hbm(down_out))
    out, combined = call(
        finish_kernel,
        [((tokens, width), BF16), ((SPLIT, tokens), F32)],
        4 * tokens * width * cap,
        4 * tokens * width,
    )(handed(other, 2), handed(own, 0), next_grad, across(other_comb, 2), own_comb, ids, place)
    return (
        out[None],
        gate_up_out.reshape(1, 1, 2, hidden, width),
        down_out.reshape(1, 1, hidden, width),
        combined.T[None],
    )


def solution(mesh):
    on_device = on_one if mesh.shape["expert"] == SPLIT else on_many
    return jax.shard_map(
        on_device,
        mesh=mesh,
        in_specs=(
            P("pipe", "expert", None),
            P("pipe", "expert", None),
            P("pipe", "expert", None),
            P("pipe", "expert", None),
            P("pipe", None),
            P("pipe", "expert", None, None, None),
            P("pipe", "expert", None, None),
        ),
        out_specs=(
            P("pipe", "expert", None),
            P("pipe", "expert", None, None, None),
            P("pipe", "expert", None, None),
            P("pipe", "expert", None),
        ),
        check_vma=False,
    )
```

```python
import functools

import jax
import jax.numpy as jnp
from jax import lax
from jax.experimental import pallas as pl
from jax.experimental.pallas import tpu as pltpu
from jax.sharding import PartitionSpec as P

SPLIT = 8
SPECIALIST_CAP = 8
LANES = 128
EPS = 1e-06
F32 = jnp.float32
BF16 = jnp.bfloat16


def shifted(block, axis, distance):
    devices = range(lax.axis_size(axis))
    route = [((i - distance) % len(devices), i) for i in devices]
    return lax.ppermute(block, axis, route)


def rows_product(left_rows, right_rows):
    return lax.dot_general(
        left_rows, right_rows, (((1,), (1,)), ((), ())), preferred_element_type=jnp.float32
    )


def column_product(left_rows, right_rows):
    return lax.dot_general(
        left_rows, right_rows, (((0,), (0,)), ((), ())), preferred_element_type=jnp.float32
    )


def on_many(hidden_in, out_grad, expert_ids, route_weight, norm_gain, w_gate_up, w_down):
    tokens_in = hidden_in[0]
    grad_out = out_grad[0]
    chosen = expert_ids[0]
    weights_in = route_weight[0]
    gain_row = norm_gain[0]
    slab_gate_up = w_gate_up[0, 0]
    slab_down = w_down[0, 0]
    devices = lax.axis_size("expert")
    specialist_span = devices // SPLIT
    model_width = tokens_in.shape[1]
    hidden_slab = slab_down.shape[0]
    capacity = SPECIALIST_CAP
    tokens_f = tokens_in.astype(jnp.float32)
    rms_value = jnp.sqrt(jnp.mean(tokens_f * tokens_f, axis=-1, keepdims=True) + 1e-06)
    normed = tokens_f / rms_value
    normed_in = (normed * gain_row).astype(jnp.bfloat16)
    expert_range = jnp.arange(specialist_span, dtype=jnp.int32)
    picked = chosen[:, :, None] == expert_range[None, None, :]
    member = jnp.any(picked, axis=1).astype(jnp.int32)
    weight_te = jnp.sum(jnp.where(picked, weights_in.astype(jnp.float32)[:, :, None], 0.0), axis=1)
    position = jnp.cumsum(member, axis=0) - member
    slot_range = jnp.arange(capacity, dtype=jnp.int32)
    placing = (position.T[:, None, :] == slot_range[None, :, None]) & (member.T[:, None, :] == 1)
    place_bf = placing.astype(jnp.bfloat16)
    place_f = placing.astype(jnp.float32)
    sent_in = jnp.einsum(
        "wst,td->wsd", place_bf, normed_in, preferred_element_type=jnp.float32
    ).astype(jnp.bfloat16)
    sent_grad = jnp.einsum(
        "wst,td->wsd", place_bf, grad_out, preferred_element_type=jnp.float32
    ).astype(jnp.bfloat16)
    sent_weight = jnp.sum(place_f * weight_te.T[:, None, :], axis=-1).astype(jnp.bfloat16)
    rows_in, rows_grad, rows_weight = (
        lax.all_to_all(
            jnp.repeat(sent_in, SPLIT, axis=0), "expert", split_axis=0, concat_axis=0, tiled=True
        ),
        lax.all_to_all(
            jnp.repeat(sent_grad, SPLIT, axis=0), "expert", split_axis=0, concat_axis=0, tiled=True
        ),
        lax.all_to_all(
            jnp.repeat(sent_weight, SPLIT, axis=0),
            "expert",
            split_axis=0,
            concat_axis=0,
            tiled=True,
        ),
    )
    total_rows = devices * capacity
    flat_in = rows_in.reshape(total_rows, model_width)
    flat_grad = rows_grad.reshape(total_rows, model_width)
    flat_weight = rows_weight.reshape(total_rows, 1).astype(jnp.float32)
    joined_slab = slab_gate_up.reshape(2 * hidden_slab, model_width)
    projected = rows_product(flat_in, joined_slab)
    gate_pre = projected[:, :hidden_slab]
    up_pre = projected[:, hidden_slab:]
    sigmoid_gate = jax.nn.sigmoid(gate_pre)
    active = gate_pre * sigmoid_gate
    hidden_act = active * up_pre
    scaled_hidden = (flat_weight * hidden_act).astype(jnp.bfloat16)
    back_proj = rows_product(flat_grad, slab_down)
    grad_hidden = flat_weight * back_proj
    grad_gate = (
        grad_hidden * up_pre * sigmoid_gate * (1.0 + gate_pre * (1.0 - sigmoid_gate))
    ).astype(jnp.bfloat16)
    grad_up = (grad_hidden * active).astype(jnp.bfloat16)
    grad_both = jnp.concatenate([grad_gate, grad_up], axis=1)
    weight_grad = column_product(grad_both, flat_in)
    down_grad = column_product(scaled_hidden, flat_grad)
    input_part = (
        jnp.dot(grad_both, joined_slab, preferred_element_type=jnp.float32)
        .astype(jnp.bfloat16)
        .reshape(devices, capacity, model_width)
    )
    combine_part = (
        jnp.sum(hidden_act * back_proj, axis=-1).astype(jnp.bfloat16).reshape(devices, capacity)
    )
    returned_in, returned_comb = (
        lax.all_to_all(input_part, "expert", split_axis=0, concat_axis=0, tiled=True),
        lax.all_to_all(combine_part, "expert", split_axis=0, concat_axis=0, tiled=True),
    )
    summed_in = jnp.sum(
        returned_in.reshape(specialist_span, SPLIT, capacity, model_width).astype(jnp.float32),
        axis=1,
    )
    summed_comb = jnp.sum(
        returned_comb.reshape(specialist_span, SPLIT, capacity).astype(jnp.float32), axis=1
    )
    grad_normed = jnp.einsum("wst,wsd->td", place_f, summed_in, precision=lax.Precision.HIGHEST)
    comb_te = jnp.sum(place_f * summed_comb[:, :, None], axis=1)
    grad_combine = jnp.sum(jnp.where(picked, comb_te.T[:, None, :], 0.0), axis=-1)
    scaled = grad_normed * gain_row
    inner_mean = jnp.mean(scaled * normed, axis=-1, keepdims=True)
    grad_tokens = (
        grad_out.astype(jnp.float32) + (scaled - normed * inner_mean) / rms_value
    ).astype(jnp.bfloat16)
    handed = shifted(grad_tokens, "pipe", -1)
    gate_up_out = weight_grad.reshape(2, hidden_slab, model_width).astype(jnp.bfloat16)
    return (
        handed[None],
        gate_up_out[None, None],
        down_grad.astype(jnp.bfloat16)[None, None],
        grad_combine[None],
    )


def call(kernel, outs, flops, moved, in_specs=None, scratch=(), limit=24):
    given = {} if in_specs is None else {"in_specs": in_specs}
    return pl.pallas_call(
        kernel,
        **given,
        out_shape=[jax.ShapeDtypeStruct(shape, kind) for shape, kind in outs],
        scratch_shapes=list(scratch),
        compiler_params=pltpu.CompilerParams(vmem_limit_bytes=limit << 20),
        cost_estimate=pl.CostEstimate(flops=flops, bytes_accessed=moved, transcendentals=0),
    )


FETCH_FLOPS = 1_000_000_000
HIDDEN_FLOPS = 6_400_000_000
IN_HBM = pl.BlockSpec(memory_space=pltpu.HBM)
IN_VMEM = pl.BlockSpec(memory_space=pltpu.VMEM)


def take_rows(place, block):
    return lax.dot_general(place, block, (((1,), (0,)), ((), ())), preferred_element_type=F32)


def normed_rows(rows):
    rms = jnp.sqrt(jnp.mean(rows * rows, axis=-1, keepdims=True) + EPS)
    return rows / rms, rms


def in_parts(values):
    high = values.astype(BF16).astype(F32)
    middle = (values - high).astype(BF16).astype(F32)
    return high, middle, values - high - middle


def rows_kernel(ids_hbm, weight_hbm, gain_hbm, hidden_hbm, grad_hbm, in_ref, out_ref, both_ref,
                normed_ref, place_ref, ids_ref, weight_ref, gain_ref, hidden_ref, grad_ref, sems):
    tokens, width = hidden_ref.shape
    cap = SPECIALIST_CAP
    copies = [
        pltpu.make_async_copy(src, dst, sems.at[i])
        for i, (src, dst) in enumerate([
            (ids_hbm, ids_ref),
            (hidden_hbm, hidden_ref),
            (gain_hbm, gain_ref),
            (weight_hbm, weight_ref),
            (grad_hbm, grad_ref),
        ])
    ]
    for copy in copies:
        copy.start()
    copies[0].wait()
    hit = ids_ref[...] == 0
    member = jnp.max(hit.astype(F32), axis=0, keepdims=True)
    member = jnp.broadcast_to(member, (cap, tokens))
    earlier = lax.broadcasted_iota(jnp.int32, (tokens, tokens), 0) < lax.broadcasted_iota(
        jnp.int32, (tokens, tokens), 1
    )
    position = take_rows(member.astype(BF16), earlier.astype(F32).astype(BF16))
    slot = lax.broadcasted_iota(jnp.int32, (cap, tokens), 0).astype(F32)
    place = jnp.where(position == slot, member, 0.0)
    place_ref[...] = place
    copies[1].wait()
    normed, rms = normed_rows(take_rows(place.astype(BF16), hidden_ref[...]))
    normed_ref[...] = normed
    copies[2].wait()
    normed_in = normed * gain_ref[...]
    in_ref[:, :width] = normed_in.astype(BF16)
    copies[3].wait()
    weight = jnp.sum(
        jnp.where(hit, weight_ref[...].astype(F32), 0.0), axis=0, keepdims=True
    )
    taken = jnp.sum(place * weight, axis=1, keepdims=True)
    lane = lax.broadcasted_iota(jnp.int32, (cap, LANES), 1)
    extra = jnp.broadcast_to(taken, (cap, LANES))
    for number, part in enumerate(in_parts(rms)):
        extra = jnp.where(lane == number + 1, part, extra)
    in_ref[:, width:] = extra.astype(BF16)
    out_ref[:, width:] = place.astype(BF16)
    both_ref[:, width:] = jnp.concatenate([extra, place], axis=0).astype(BF16)
    copies[4].wait()
    grad = take_rows(place.astype(BF16), grad_ref[...])
    out_ref[:, :width] = grad.astype(BF16)
    both_ref[:, :width] = jnp.concatenate([normed_in, grad], axis=0).astype(BF16)


def fetch_kernel(slab_hbm, down_hbm, after_ref, slab_ref, down_ref, sems):
    del after_ref
    first = pltpu.make_async_copy(slab_hbm, slab_ref, sems.at[0])
    second = pltpu.make_async_copy(down_hbm, down_ref, sems.at[1])
    first.start()
    second.start()
    first.wait()
    second.wait()


def pass_kernel(block_ref, *refs):
    *after_refs, out_ref = refs
    del after_refs
    out_ref[...] = block_ref[...]


def stacked(refs, half, start, stop):
    cap = SPECIALIST_CAP
    pieces = []
    for ref in refs:
        block = ref[:, start:stop].astype(F32)
        pieces.append(block if ref.shape[0] == cap else block[half * cap : (half + 1) * cap])
    return jnp.concatenate(pieces, axis=0)


def project_kernel(*refs):
    *blocks, slab_ref, slab_two_ref, pre_ref, pre_two_ref, first_ref, last_ref = refs
    width = slab_ref.shape[1]
    rows = stacked(blocks, 0, 0, width).astype(BF16)
    half = first_ref.shape[0]
    pre_ref[...] = rows_product(rows, slab_ref[...])
    pre_two_ref[...] = rows_product(rows, slab_two_ref[...])
    first_ref[...] = rows[:half]
    last_ref[...] = rows[half:]


def hidden_kernel(*refs):
    in_blocks, blocks, refs = refs[:4], refs[4:8], refs[8:]
    pre_ref, pre_two_ref, slab_ref, down_ref, slab_two_ref, down_two_ref, *refs = refs
    own_ref, other_ref, first_ref, last_ref, keep_ref, send_ref = refs
    hidden, width = down_ref.shape
    half = own_ref.shape[0]
    rows = stacked(blocks, 1, 0, width).astype(BF16)
    weight = stacked(in_blocks, 0, width, width + LANES)[:, :1]
    total, comb = 0.0, 0.0
    for slab, down, pre, left_ref in (
        (slab_ref[...], down_ref[...], pre_ref[...], keep_ref),
        (slab_two_ref[...], down_two_ref[...], pre_two_ref[...], send_ref),
    ):
        back = rows_product(rows, down)
        gate = pre[:, :hidden]
        up = pre[:, hidden:]
        sig = jax.nn.sigmoid(gate)
        active = gate * sig
        act = active * up
        into = weight * back
        both = jnp.concatenate(
            [into * up * sig * (1.0 + gate * (1.0 - sig)), into * active], axis=1
        )
        total = total + take_rows(both.astype(BF16), slab)
        part = jnp.sum(act * back, axis=1, keepdims=True)
        comb = comb + part.astype(BF16).astype(F32)
        left_ref[:, : 2 * hidden] = both.astype(BF16)
        left_ref[:, 2 * hidden : 3 * hidden] = (weight * act).astype(BF16)
        left_ref[:, 3 * hidden :] = jnp.zeros(
            (left_ref.shape[0], left_ref.shape[1] - 3 * hidden), BF16
        )
    other_ref[:, :width] = total[half:].astype(BF16)
    own_ref[:, :width] = total[:half].astype(BF16)
    comb = jnp.broadcast_to(comb, (2 * half, LANES))
    high = comb.astype(BF16).astype(F32)
    lane = lax.broadcasted_iota(jnp.int32, comb.shape, 1)
    comb = jnp.where(lane < LANES // 2, high, comb - high).astype(BF16)
    other_ref[:, width:] = comb[half:]
    own_ref[:, width:] = comb[:half]
    first_ref[...] = rows[:half]
    last_ref[...] = rows[half:]


def split_kernel(keep_ref, got_ref, normed_ref, in_ref, far_in_ref, far_grad_ref, gain_ref,
                 own_ref, other_ref, own_comb_ref, other_comb_ref):
    cap, width = own_ref.shape
    total = keep_ref[...].astype(F32) + got_ref[...].astype(F32)
    gain = gain_ref[...]
    far = far_in_ref[...].astype(F32)
    extra = jnp.concatenate([in_ref[:, width:].astype(F32), far[:, width:]], axis=0)
    rms = extra[:, 1:2] + extra[:, 2:3] + extra[:, 3:4]
    normed = jnp.concatenate([normed_ref[...], far[:, :width] / gain], axis=0)
    scaled = total[:, :width] * gain
    inner = jnp.mean(scaled * normed, axis=-1, keepdims=True)
    change = (scaled - normed * inner) / rms
    other_ref[:, :width] = change[cap:].astype(BF16)
    other_ref[:, width:] = far_grad_ref[:, width:]
    own_ref[...] = change[:cap].astype(BF16)
    comb = total[:, width:]
    comb = comb + pltpu.roll(comb, LANES // 2, 1)
    other_comb_ref[...] = comb[cap:]
    own_comb_ref[...] = comb[:cap]


def weights_kernel(chunks, *refs):
    ins, grads, refs = refs[:4], refs[4:8], refs[8:]
    keep_ref, got_ref, after_ref, both_hbm, act_hbm, both_ref, act_ref, sems = refs
    del after_ref
    hidden, width = act_ref.shape
    left = jnp.concatenate([keep_ref[...], got_ref[...]], axis=0).astype(F32).T
    both = left[: 2 * hidden].astype(BF16)
    act = left[2 * hidden : 3 * hidden].astype(BF16)
    chunk = width // chunks
    copies = []
    for number in range(chunks):
        columns = slice(number * chunk, (number + 1) * chunk)
        for which, (left_rows, blocks, ref, hbm) in enumerate(
            ((both, ins, both_ref, both_hbm), (act, grads, act_ref, act_hbm))
        ):
            rows = jnp.concatenate([r[:, columns] for r in blocks], axis=0)
            ref[:, columns] = take_rows(left_rows, rows).astype(BF16)
            copy = pltpu.make_async_copy(
                ref.at[:, columns], hbm.at[:, columns], sems.at[2 * number + which]
            )
            copy.start()
            copies.append(copy)
    for copy in copies:
        copy.wait()


def weight_grads(blocks, keep, got, after, hidden, width):
    chunks = 4
    return pl.pallas_call(
        functools.partial(weights_kernel, chunks),
        in_specs=[IN_VMEM] * (len(blocks) + 2) + [pl.BlockSpec(memory_space=pl.ANY)],
        out_specs=[IN_HBM] * 2,
        out_shape=[
            jax.ShapeDtypeStruct((2 * hidden, width), BF16),
            jax.ShapeDtypeStruct((hidden, width), BF16),
        ],
        scratch_shapes=[
            pltpu.VMEM((2 * hidden, width), BF16),
            pltpu.VMEM((hidden, width), BF16),
            pltpu.SemaphoreType.DMA((2 * chunks,)),
        ],
        compiler_params=pltpu.CompilerParams(vmem_limit_bytes=24 << 20),
        cost_estimate=pl.CostEstimate(
            flops=6 * 64 * hidden * width, bytes_accessed=6 * hidden * width, transcendentals=0
        ),
    )(*blocks, keep, got, after)


def finish_kernel(other_ref, own_ref, grad_ref, other_comb_ref, own_comb_ref, ids_ref, place_ref,
                  out_ref, comb_ref):
    width = grad_ref.shape[1]
    comb = own_comb_ref[...] + other_comb_ref[...]
    comb = jnp.sum(place_ref[...] * comb, axis=0, keepdims=True)
    comb_ref[...] = jnp.where(ids_ref[...] == 0, comb, 0.0)
    place = other_ref[:, width:]
    grad = grad_ref[...]
    own = take_rows(place, grad)
    change = own_ref[...].astype(F32) + other_ref[:, :width].astype(F32)
    rows = (own + change).astype(BF16)
    back = place.astype(F32).T
    spread = take_rows(back.astype(BF16), rows)
    named = jnp.sum(back, axis=1, keepdims=True) > 0.0
    out_ref[...] = jnp.where(named, spread, grad.astype(F32)).astype(BF16)


def on_one(hidden_in, out_grad, expert_ids, route_weight, norm_gain, w_gate_up, w_down):
    sections = lax.axis_size("pipe")
    devices = lax.axis_size("expert")
    tokens, width = hidden_in.shape[1:]
    hidden = w_down.shape[2]
    cap = SPECIALIST_CAP
    ids = expert_ids[0].T
    weights = route_weight[0].T
    slab = w_gate_up.reshape(2 * hidden, width)
    down = w_down.reshape(hidden, width)
    in_hbm = lambda a: pltpu.with_memory_space_constraint(a, pltpu.HBM)
    wide = width + LANES
    total_rows = devices * cap

    def across(block, offset):
        return lax.ppermute(block, "expert", [(i, i ^ (2 * offset)) for i in range(devices)])

    def beside(block):
        return lax.ppermute(block, "expert", [(i, i ^ 1) for i in range(devices)])

    def handed(block, offset):
        route = [
            (((p + 1) % sections) * devices + i, p * devices + (i ^ (2 * offset)))
            for p in range(sections)
            for i in range(devices)
        ]
        return lax.ppermute(block, ("pipe", "expert"), route)

    next_grad = handed(out_grad[0], 0)
    row_in, row_grad, row_both, normed, place = call(
        rows_kernel,
        [((cap, wide), BF16)] * 2
        + [((2 * cap, wide), BF16), ((cap, width), F32), ((cap, tokens), F32)],
        4 * tokens * width * cap,
        4 * tokens * width,
        in_specs=[IN_HBM] * 5,
        scratch=[
            pltpu.VMEM(ids.shape, ids.dtype),
            pltpu.VMEM(weights.shape, weights.dtype),
            pltpu.VMEM(norm_gain.shape, norm_gain.dtype),
            pltpu.VMEM((tokens, width), BF16),
            pltpu.VMEM((tokens, width), BF16),
            pltpu.SemaphoreType.DMA((5,)),
        ],
    )(*map(in_hbm, (ids, weights, norm_gain, hidden_in[0], out_grad[0])))
    far_in = across(row_in, 2)
    far_grad = across(row_grad, 2)
    slab_two, down_two = beside(slab), beside(down)
    (passed,) = call(
        pass_kernel,
        [(row_both.shape, BF16)],
        0,
        4 * cap * wide,
        in_specs=[IN_VMEM] + [pl.BlockSpec(memory_space=pl.ANY)] * 2,
    )(row_both, slab_two, down_two)
    near = across(passed, 1)
    slab_near, down_near = call(
        fetch_kernel,
        [(slab.shape, BF16), (down.shape, BF16)],
        FETCH_FLOPS,
        6 * hidden * width,
        in_specs=[IN_HBM] * 2 + [pl.BlockSpec(memory_space=pl.ANY)],
        scratch=[pltpu.SemaphoreType.DMA((2,))],
    )(in_hbm(slab), in_hbm(down), far_grad)
    farthest_in = across(far_in, 1)
    farthest_grad = across(far_grad, 1)
    ins = [row_in, far_in, near, farthest_in]
    grads = [row_grad, far_grad, near, farthest_grad]
    half_rows = ((2 * cap, width), BF16)
    pre, pre_two, *in_halves = call(
        project_kernel,
        [((total_rows // 2, 2 * hidden), F32)] * 2 + [half_rows] * 2,
        0,
        4 * hidden * width,
    )(*ins, slab_near, slab_two)
    left_width = -(-3 * hidden // LANES) * LANES
    own_half, other_half, *rest = call(
        hidden_kernel,
        [((2 * cap, wide), BF16)] * 2
        + [half_rows] * 2
        + [((total_rows // 2, left_width), BF16)] * 2,
        HIDDEN_FLOPS,
        6 * hidden * width,
    )(*ins, *grads, pre, pre_two, slab_near, down_near, slab_two, down_two)
    *grad_halves, left_keep, left_send = rest
    own, other, own_comb, other_comb = call(
        split_kernel,
        [((cap, width), BF16), ((cap, wide), BF16)] + [((cap, LANES), F32)] * 2,
        2 * cap * width,
        8 * cap * width,
    )(own_half, across(other_half, 1), normed, row_in, far_in, far_grad, norm_gain)
    blocks = in_halves + [beside(b) for b in in_halves]
    blocks += grad_halves + [beside(b) for b in grad_halves]
    gate_up_out, down_out = weight_grads(blocks, left_keep, beside(left_send), own, hidden, width)
    out, combined = call(
        finish_kernel,
        [((tokens, width), BF16), ((SPLIT, tokens), F32)],
        4 * tokens * width * cap,
        4 * tokens * width,
    )(handed(other, 2), handed(own, 0), next_grad, across(other_comb, 2), own_comb, ids, place)
    return (
        out[None],
        gate_up_out.reshape(1, 1, 2, hidden, width),
        down_out.reshape(1, 1, hidden, width),
        combined.T[None],
    )


def solution(mesh):
    on_device = on_one if mesh.shape["expert"] == SPLIT else on_many
    return jax.shard_map(
        on_device,
        mesh=mesh,
        in_specs=(
            P("pipe", "expert", None),
            P("pipe", "expert", None),
            P("pipe", "expert", None),
            P("pipe", "expert", None),
            P("pipe", None),
            P("pipe", "expert", None, None, None),
            P("pipe", "expert", None, None),
        ),
        out_specs=(
            P("pipe", "expert", None),
            P("pipe", "expert", None, None, None),
            P("pipe", "expert", None, None),
            P("pipe", "expert", None),
        ),
        check_vma=False,
    )
```

```python
import functools

import jax
import jax.numpy as jnp
from jax import lax
from jax.experimental import pallas as pl
from jax.experimental.pallas import tpu as pltpu
from jax.sharding import PartitionSpec as P

SPLIT = 8
SPECIALIST_CAP = 8
LANES = 128
EPS = 1e-06
F32 = jnp.float32
BF16 = jnp.bfloat16


def shifted(block, axis, distance):
    devices = range(lax.axis_size(axis))
    route = [((i - distance) % len(devices), i) for i in devices]
    return lax.ppermute(block, axis, route)


def rows_product(left_rows, right_rows):
    return lax.dot_general(
        left_rows, right_rows, (((1,), (1,)), ((), ())), preferred_element_type=jnp.float32
    )


def column_product(left_rows, right_rows):
    return lax.dot_general(
        left_rows, right_rows, (((0,), (0,)), ((), ())), preferred_element_type=jnp.float32
    )


def on_many(hidden_in, out_grad, expert_ids, route_weight, norm_gain, w_gate_up, w_down):
    tokens_in = hidden_in[0]
    grad_out = out_grad[0]
    chosen = expert_ids[0]
    weights_in = route_weight[0]
    gain_row = norm_gain[0]
    slab_gate_up = w_gate_up[0, 0]
    slab_down = w_down[0, 0]
    devices = lax.axis_size("expert")
    specialist_span = devices // SPLIT
    model_width = tokens_in.shape[1]
    hidden_slab = slab_down.shape[0]
    capacity = SPECIALIST_CAP
    tokens_f = tokens_in.astype(jnp.float32)
    rms_value = jnp.sqrt(jnp.mean(tokens_f * tokens_f, axis=-1, keepdims=True) + 1e-06)
    normed = tokens_f / rms_value
    normed_in = (normed * gain_row).astype(jnp.bfloat16)
    expert_range = jnp.arange(specialist_span, dtype=jnp.int32)
    picked = chosen[:, :, None] == expert_range[None, None, :]
    member = jnp.any(picked, axis=1).astype(jnp.int32)
    weight_te = jnp.sum(jnp.where(picked, weights_in.astype(jnp.float32)[:, :, None], 0.0), axis=1)
    position = jnp.cumsum(member, axis=0) - member
    slot_range = jnp.arange(capacity, dtype=jnp.int32)
    placing = (position.T[:, None, :] == slot_range[None, :, None]) & (member.T[:, None, :] == 1)
    place_bf = placing.astype(jnp.bfloat16)
    place_f = placing.astype(jnp.float32)
    sent_in = jnp.einsum(
        "wst,td->wsd", place_bf, normed_in, preferred_element_type=jnp.float32
    ).astype(jnp.bfloat16)
    sent_grad = jnp.einsum(
        "wst,td->wsd", place_bf, grad_out, preferred_element_type=jnp.float32
    ).astype(jnp.bfloat16)
    sent_weight = jnp.sum(place_f * weight_te.T[:, None, :], axis=-1).astype(jnp.bfloat16)
    rows_in, rows_grad, rows_weight = (
        lax.all_to_all(
            jnp.repeat(sent_in, SPLIT, axis=0), "expert", split_axis=0, concat_axis=0, tiled=True
        ),
        lax.all_to_all(
            jnp.repeat(sent_grad, SPLIT, axis=0), "expert", split_axis=0, concat_axis=0, tiled=True
        ),
        lax.all_to_all(
            jnp.repeat(sent_weight, SPLIT, axis=0),
            "expert",
            split_axis=0,
            concat_axis=0,
            tiled=True,
        ),
    )
    total_rows = devices * capacity
    flat_in = rows_in.reshape(total_rows, model_width)
    flat_grad = rows_grad.reshape(total_rows, model_width)
    flat_weight = rows_weight.reshape(total_rows, 1).astype(jnp.float32)
    joined_slab = slab_gate_up.reshape(2 * hidden_slab, model_width)
    projected = rows_product(flat_in, joined_slab)
    gate_pre = projected[:, :hidden_slab]
    up_pre = projected[:, hidden_slab:]
    sigmoid_gate = jax.nn.sigmoid(gate_pre)
    active = gate_pre * sigmoid_gate
    hidden_act = active * up_pre
    scaled_hidden = (flat_weight * hidden_act).astype(jnp.bfloat16)
    back_proj = rows_product(flat_grad, slab_down)
    grad_hidden = flat_weight * back_proj
    grad_gate = (
        grad_hidden * up_pre * sigmoid_gate * (1.0 + gate_pre * (1.0 - sigmoid_gate))
    ).astype(jnp.bfloat16)
    grad_up = (grad_hidden * active).astype(jnp.bfloat16)
    grad_both = jnp.concatenate([grad_gate, grad_up], axis=1)
    weight_grad = column_product(grad_both, flat_in)
    down_grad = column_product(scaled_hidden, flat_grad)
    input_part = (
        jnp.dot(grad_both, joined_slab, preferred_element_type=jnp.float32)
        .astype(jnp.bfloat16)
        .reshape(devices, capacity, model_width)
    )
    combine_part = (
        jnp.sum(hidden_act * back_proj, axis=-1).astype(jnp.bfloat16).reshape(devices, capacity)
    )
    returned_in, returned_comb = (
        lax.all_to_all(input_part, "expert", split_axis=0, concat_axis=0, tiled=True),
        lax.all_to_all(combine_part, "expert", split_axis=0, concat_axis=0, tiled=True),
    )
    summed_in = jnp.sum(
        returned_in.reshape(specialist_span, SPLIT, capacity, model_width).astype(jnp.float32),
        axis=1,
    )
    summed_comb = jnp.sum(
        returned_comb.reshape(specialist_span, SPLIT, capacity).astype(jnp.float32), axis=1
    )
    grad_normed = jnp.einsum("wst,wsd->td", place_f, summed_in, precision=lax.Precision.HIGHEST)
    comb_te = jnp.sum(place_f * summed_comb[:, :, None], axis=1)
    grad_combine = jnp.sum(jnp.where(picked, comb_te.T[:, None, :], 0.0), axis=-1)
    scaled = grad_normed * gain_row
    inner_mean = jnp.mean(scaled * normed, axis=-1, keepdims=True)
    grad_tokens = (
        grad_out.astype(jnp.float32) + (scaled - normed * inner_mean) / rms_value
    ).astype(jnp.bfloat16)
    handed = shifted(grad_tokens, "pipe", -1)
    gate_up_out = weight_grad.reshape(2, hidden_slab, model_width).astype(jnp.bfloat16)
    return (
        handed[None],
        gate_up_out[None, None],
        down_grad.astype(jnp.bfloat16)[None, None],
        grad_combine[None],
    )


def call(kernel, outs, flops, moved, in_specs=None, scratch=(), limit=24):
    given = {} if in_specs is None else {"in_specs": in_specs}
    return pl.pallas_call(
        kernel,
        **given,
        out_shape=[jax.ShapeDtypeStruct(shape, kind) for shape, kind in outs],
        scratch_shapes=list(scratch),
        compiler_params=pltpu.CompilerParams(vmem_limit_bytes=limit << 20),
        cost_estimate=pl.CostEstimate(flops=flops, bytes_accessed=moved, transcendentals=0),
    )


FETCH_FLOPS = 1_000_000_000
HIDDEN_FLOPS = 7_000_000_000
IN_HBM = pl.BlockSpec(memory_space=pltpu.HBM)
IN_VMEM = pl.BlockSpec(memory_space=pltpu.VMEM)


def take_rows(place, block):
    return lax.dot_general(place, block, (((1,), (0,)), ((), ())), preferred_element_type=F32)


def normed_rows(rows):
    rms = jnp.sqrt(jnp.mean(rows * rows, axis=-1, keepdims=True) + EPS)
    return rows / rms, rms


def in_parts(values):
    high = values.astype(BF16).astype(F32)
    middle = (values - high).astype(BF16).astype(F32)
    return high, middle, values - high - middle


def rows_kernel(ids_hbm, weight_hbm, gain_hbm, hidden_hbm, grad_hbm, in_ref, out_ref, both_ref,
                normed_ref, place_ref, ids_ref, weight_ref, gain_ref, hidden_ref, grad_ref, sems):
    tokens, width = hidden_ref.shape
    cap = SPECIALIST_CAP
    copies = [
        pltpu.make_async_copy(src, dst, sems.at[i])
        for i, (src, dst) in enumerate([
            (ids_hbm, ids_ref),
            (hidden_hbm, hidden_ref),
            (gain_hbm, gain_ref),
            (weight_hbm, weight_ref),
            (grad_hbm, grad_ref),
        ])
    ]
    for copy in copies:
        copy.start()
    copies[0].wait()
    hit = ids_ref[...] == 0
    member = jnp.max(hit.astype(F32), axis=0, keepdims=True)
    member = jnp.broadcast_to(member, (cap, tokens))
    earlier = lax.broadcasted_iota(jnp.int32, (tokens, tokens), 0) < lax.broadcasted_iota(
        jnp.int32, (tokens, tokens), 1
    )
    position = take_rows(member.astype(BF16), earlier.astype(F32).astype(BF16))
    slot = lax.broadcasted_iota(jnp.int32, (cap, tokens), 0).astype(F32)
    place = jnp.where(position == slot, member, 0.0)
    place_ref[...] = place
    copies[1].wait()
    normed, rms = normed_rows(take_rows(place.astype(BF16), hidden_ref[...]))
    normed_ref[...] = normed
    copies[2].wait()
    normed_in = normed * gain_ref[...]
    in_ref[:, :width] = normed_in.astype(BF16)
    copies[3].wait()
    weight = jnp.sum(
        jnp.where(hit, weight_ref[...].astype(F32), 0.0), axis=0, keepdims=True
    )
    taken = jnp.sum(place * weight, axis=1, keepdims=True)
    lane = lax.broadcasted_iota(jnp.int32, (cap, LANES), 1)
    extra = jnp.broadcast_to(taken, (cap, LANES))
    for number, part in enumerate(in_parts(rms)):
        extra = jnp.where(lane == number + 1, part, extra)
    in_ref[:, width:] = extra.astype(BF16)
    out_ref[:, width:] = place.astype(BF16)
    both_ref[:, width:] = jnp.concatenate([extra, place], axis=0).astype(BF16)
    copies[4].wait()
    grad = take_rows(place.astype(BF16), grad_ref[...])
    out_ref[:, :width] = grad.astype(BF16)
    both_ref[:, :width] = jnp.concatenate([normed_in, grad], axis=0).astype(BF16)


def fetch_kernel(slab_hbm, down_hbm, after_ref, slab_ref, down_ref, sems):
    del after_ref
    first = pltpu.make_async_copy(slab_hbm, slab_ref, sems.at[0])
    second = pltpu.make_async_copy(down_hbm, down_ref, sems.at[1])
    first.start()
    second.start()
    first.wait()
    second.wait()


def stacked(refs, half, start, stop):
    cap = SPECIALIST_CAP
    pieces = []
    for ref in refs:
        block = ref[:, start:stop].astype(F32)
        pieces.append(block if ref.shape[0] == cap else block[half * cap : (half + 1) * cap])
    return jnp.concatenate(pieces, axis=0)


def project_kernel(*refs):
    *blocks, slab_ref, slab_two_ref, pre_ref, pre_two_ref, first_ref, last_ref = refs
    width = slab_ref.shape[1]
    rows = stacked(blocks, 0, 0, width).astype(BF16)
    half = first_ref.shape[0]
    pre_ref[...] = rows_product(rows, slab_ref[...])
    pre_two_ref[...] = rows_product(rows, slab_two_ref[...])
    first_ref[...] = rows[:half]
    last_ref[...] = rows[half:]


def hidden_kernel(*refs):
    in_blocks, blocks, refs = refs[:4], refs[4:8], refs[8:]
    pre_ref, pre_two_ref, slab_ref, down_ref, slab_two_ref, down_two_ref, *refs = refs
    own_ref, other_ref, first_ref, last_ref, keep_ref, send_ref = refs
    hidden, width = down_ref.shape
    half = own_ref.shape[0]
    rows = stacked(blocks, 1, 0, width).astype(BF16)
    weight = stacked(in_blocks, 0, width, width + LANES)[:, :1]
    total, comb = 0.0, 0.0
    for slab, down, pre, left_ref in (
        (slab_ref[...], down_ref[...], pre_ref[...], keep_ref),
        (slab_two_ref[...], down_two_ref[...], pre_two_ref[...], send_ref),
    ):
        back = rows_product(rows, down)
        gate = pre[:, :hidden]
        up = pre[:, hidden:]
        sig = jax.nn.sigmoid(gate)
        active = gate * sig
        act = active * up
        into = weight * back
        both = jnp.concatenate(
            [into * up * sig * (1.0 + gate * (1.0 - sig)), into * active], axis=1
        )
        total = total + take_rows(both.astype(BF16), slab)
        part = jnp.sum(act * back, axis=1, keepdims=True)
        comb = comb + part.astype(BF16).astype(F32)
        left_ref[:, : 2 * hidden] = both.astype(BF16)
        left_ref[:, 2 * hidden : 3 * hidden] = (weight * act).astype(BF16)
        left_ref[:, 3 * hidden :] = jnp.zeros(
            (left_ref.shape[0], left_ref.shape[1] - 3 * hidden), BF16
        )
    other_ref[:, :width] = total[half:].astype(BF16)
    own_ref[:, :width] = total[:half].astype(BF16)
    comb = jnp.broadcast_to(comb, (2 * half, LANES))
    high = comb.astype(BF16).astype(F32)
    lane = lax.broadcasted_iota(jnp.int32, comb.shape, 1)
    comb = jnp.where(lane < LANES // 2, high, comb - high).astype(BF16)
    other_ref[:, width:] = comb[half:]
    own_ref[:, width:] = comb[:half]
    first_ref[...] = rows[:half]
    last_ref[...] = rows[half:]


def split_kernel(keep_ref, got_ref, normed_ref, in_ref, far_in_ref, far_grad_ref, gain_ref,
                 own_ref, other_ref, own_comb_ref, other_comb_ref):
    cap, width = own_ref.shape
    total = keep_ref[...].astype(F32) + got_ref[...].astype(F32)
    gain = gain_ref[...]
    far = far_in_ref[...].astype(F32)
    extra = jnp.concatenate([in_ref[:, width:].astype(F32), far[:, width:]], axis=0)
    rms = extra[:, 1:2] + extra[:, 2:3] + extra[:, 3:4]
    normed = jnp.concatenate([normed_ref[...], far[:, :width] / gain], axis=0)
    scaled = total[:, :width] * gain
    inner = jnp.mean(scaled * normed, axis=-1, keepdims=True)
    change = (scaled - normed * inner) / rms
    other_ref[:, :width] = change[cap:].astype(BF16)
    other_ref[:, width:] = far_grad_ref[:, width:]
    own_ref[...] = change[:cap].astype(BF16)
    comb = total[:, width:]
    comb = comb + pltpu.roll(comb, LANES // 2, 1)
    other_comb_ref[...] = comb[cap:]
    own_comb_ref[...] = comb[:cap]


def weights_kernel(chunks, *refs):
    ins, grads, refs = refs[:4], refs[4:8], refs[8:]
    keep_ref, got_ref, after_ref, both_hbm, act_hbm, both_ref, act_ref, sems = refs
    del after_ref
    hidden, width = act_ref.shape
    left = jnp.concatenate([keep_ref[...], got_ref[...]], axis=0).astype(F32).T
    both = left[: 2 * hidden].astype(BF16)
    act = left[2 * hidden : 3 * hidden].astype(BF16)
    chunk = width // chunks
    copies = []
    for number in range(chunks):
        columns = slice(number * chunk, (number + 1) * chunk)
        for which, (left_rows, blocks, ref, hbm) in enumerate(
            ((both, ins, both_ref, both_hbm), (act, grads, act_ref, act_hbm))
        ):
            rows = jnp.concatenate([r[:, columns] for r in blocks], axis=0)
            ref[:, columns] = take_rows(left_rows, rows).astype(BF16)
            copy = pltpu.make_async_copy(
                ref.at[:, columns], hbm.at[:, columns], sems.at[2 * number + which]
            )
            copy.start()
            copies.append(copy)
    for copy in copies:
        copy.wait()


def weight_grads(blocks, keep, got, after, hidden, width):
    chunks = 4
    return pl.pallas_call(
        functools.partial(weights_kernel, chunks),
        in_specs=[IN_VMEM] * (len(blocks) + 2) + [pl.BlockSpec(memory_space=pl.ANY)],
        out_specs=[IN_HBM] * 2,
        out_shape=[
            jax.ShapeDtypeStruct((2 * hidden, width), BF16),
            jax.ShapeDtypeStruct((hidden, width), BF16),
        ],
        scratch_shapes=[
            pltpu.VMEM((2 * hidden, width), BF16),
            pltpu.VMEM((hidden, width), BF16),
            pltpu.SemaphoreType.DMA((2 * chunks,)),
        ],
        compiler_params=pltpu.CompilerParams(vmem_limit_bytes=24 << 20),
        cost_estimate=pl.CostEstimate(
            flops=6 * 64 * hidden * width, bytes_accessed=6 * hidden * width, transcendentals=0
        ),
    )(*blocks, keep, got, after)


def finish_kernel(other_ref, own_ref, grad_ref, other_comb_ref, own_comb_ref, ids_ref, place_ref,
                  out_ref, comb_ref):
    width = grad_ref.shape[1]
    comb = own_comb_ref[...] + other_comb_ref[...]
    comb = jnp.sum(place_ref[...] * comb, axis=0, keepdims=True)
    comb_ref[...] = jnp.where(ids_ref[...] == 0, comb, 0.0)
    place = other_ref[:, width:]
    grad = grad_ref[...]
    own = take_rows(place, grad)
    change = own_ref[...].astype(F32) + other_ref[:, :width].astype(F32)
    rows = (own + change).astype(BF16)
    back = place.astype(F32).T
    spread = take_rows(back.astype(BF16), rows)
    named = jnp.sum(back, axis=1, keepdims=True) > 0.0
    out_ref[...] = jnp.where(named, spread, grad.astype(F32)).astype(BF16)


def on_one(hidden_in, out_grad, expert_ids, route_weight, norm_gain, w_gate_up, w_down):
    sections = lax.axis_size("pipe")
    devices = lax.axis_size("expert")
    tokens, width = hidden_in.shape[1:]
    hidden = w_down.shape[2]
    cap = SPECIALIST_CAP
    ids = expert_ids[0].T
    weights = route_weight[0].T
    slab = w_gate_up.reshape(2 * hidden, width)
    down = w_down.reshape(hidden, width)
    in_hbm = lambda a: pltpu.with_memory_space_constraint(a, pltpu.HBM)
    wide = width + LANES
    total_rows = devices * cap

    def across(block, offset):
        return lax.ppermute(block, "expert", [(i, i ^ (2 * offset)) for i in range(devices)])

    def beside(block):
        return lax.ppermute(block, "expert", [(i, i ^ 1) for i in range(devices)])

    def handed(block, offset):
        route = [
            (((p + 1) % sections) * devices + i, p * devices + (i ^ (2 * offset)))
            for p in range(sections)
            for i in range(devices)
        ]
        return lax.ppermute(block, ("pipe", "expert"), route)

    row_in, row_grad, row_both, normed, place = call(
        rows_kernel,
        [((cap, wide), BF16)] * 2
        + [((2 * cap, wide), BF16), ((cap, width), F32), ((cap, tokens), F32)],
        4 * tokens * width * cap,
        4 * tokens * width,
        in_specs=[IN_HBM] * 5,
        scratch=[
            pltpu.VMEM(ids.shape, ids.dtype),
            pltpu.VMEM(weights.shape, weights.dtype),
            pltpu.VMEM(norm_gain.shape, norm_gain.dtype),
            pltpu.VMEM((tokens, width), BF16),
            pltpu.VMEM((tokens, width), BF16),
            pltpu.SemaphoreType.DMA((5,)),
        ],
    )(*map(in_hbm, (ids, weights, norm_gain, hidden_in[0], out_grad[0])))
    far_in = across(row_in, 2)
    far_grad = across(row_grad, 2)
    slab_two, down_two = beside(slab), beside(down)
    near = across(row_both, 1)
    grad_after, _ = lax.optimization_barrier((out_grad[0], slab_two))
    next_grad = handed(grad_after, 0)
    slab_near, down_near = call(
        fetch_kernel,
        [(slab.shape, BF16), (down.shape, BF16)],
        FETCH_FLOPS,
        6 * hidden * width,
        in_specs=[IN_HBM] * 2 + [pl.BlockSpec(memory_space=pl.ANY)],
        scratch=[pltpu.SemaphoreType.DMA((2,))],
    )(in_hbm(slab), in_hbm(down), far_grad)
    farthest_in = across(far_in, 1)
    farthest_grad = across(far_grad, 1)
    ins = [row_in, far_in, near, farthest_in]
    grads = [row_grad, far_grad, near, farthest_grad]
    half_rows = ((2 * cap, width), BF16)
    pre, pre_two, *in_halves = call(
        project_kernel,
        [((total_rows // 2, 2 * hidden), F32)] * 2 + [half_rows] * 2,
        0,
        4 * hidden * width,
    )(*ins, slab_near, slab_two)
    left_width = -(-3 * hidden // LANES) * LANES
    own_half, other_half, *rest = call(
        hidden_kernel,
        [((2 * cap, wide), BF16)] * 2
        + [half_rows] * 2
        + [((total_rows // 2, left_width), BF16)] * 2,
        HIDDEN_FLOPS,
        6 * hidden * width,
    )(*ins, *grads, pre, pre_two, slab_near, down_near, slab_two, down_two)
    *grad_halves, left_keep, left_send = rest
    own, other, own_comb, other_comb = call(
        split_kernel,
        [((cap, width), BF16), ((cap, wide), BF16)] + [((cap, LANES), F32)] * 2,
        2 * cap * width,
        8 * cap * width,
    )(own_half, across(other_half, 1), normed, row_in, far_in, far_grad, norm_gain)
    blocks = in_halves + [beside(b) for b in in_halves]
    blocks += grad_halves + [beside(b) for b in grad_halves]
    gate_up_out, down_out = weight_grads(blocks, left_keep, beside(left_send), own, hidden, width)
    out, combined = call(
        finish_kernel,
        [((tokens, width), BF16), ((SPLIT, tokens), F32)],
        4 * tokens * width * cap,
        4 * tokens * width,
    )(handed(other, 2), handed(own, 0), next_grad, across(other_comb, 2), own_comb, ids, place)
    return (
        out[None],
        gate_up_out.reshape(1, 1, 2, hidden, width),
        down_out.reshape(1, 1, hidden, width),
        combined.T[None],
    )


def solution(mesh):
    on_device = on_one if mesh.shape["expert"] == SPLIT else on_many
    return jax.shard_map(
        on_device,
        mesh=mesh,
        in_specs=(
            P("pipe", "expert", None),
            P("pipe", "expert", None),
            P("pipe", "expert", None),
            P("pipe", "expert", None),
            P("pipe", None),
            P("pipe", "expert", None, None, None),
            P("pipe", "expert", None, None),
        ),
        out_specs=(
            P("pipe", "expert", None),
            P("pipe", "expert", None, None, None),
            P("pipe", "expert", None, None),
            P("pipe", "expert", None),
        ),
        check_vma=False,
    )
```

```python
import functools

import jax
import jax.numpy as jnp
from jax import lax
from jax.experimental import pallas as pl
from jax.experimental.pallas import tpu as pltpu
from jax.sharding import PartitionSpec as P

SPLIT = 8
SPECIALIST_CAP = 8
LANES = 128
EPS = 1e-06
F32 = jnp.float32
BF16 = jnp.bfloat16


def shifted(block, axis, distance):
    devices = range(lax.axis_size(axis))
    route = [((i - distance) % len(devices), i) for i in devices]
    return lax.ppermute(block, axis, route)


def rows_product(left_rows, right_rows):
    return lax.dot_general(
        left_rows, right_rows, (((1,), (1,)), ((), ())), preferred_element_type=jnp.float32
    )


def column_product(left_rows, right_rows):
    return lax.dot_general(
        left_rows, right_rows, (((0,), (0,)), ((), ())), preferred_element_type=jnp.float32
    )


def on_many(hidden_in, out_grad, expert_ids, route_weight, norm_gain, w_gate_up, w_down):
    tokens_in = hidden_in[0]
    grad_out = out_grad[0]
    chosen = expert_ids[0]
    weights_in = route_weight[0]
    gain_row = norm_gain[0]
    slab_gate_up = w_gate_up[0, 0]
    slab_down = w_down[0, 0]
    devices = lax.axis_size("expert")
    specialist_span = devices // SPLIT
    model_width = tokens_in.shape[1]
    hidden_slab = slab_down.shape[0]
    capacity = SPECIALIST_CAP
    tokens_f = tokens_in.astype(jnp.float32)
    rms_value = jnp.sqrt(jnp.mean(tokens_f * tokens_f, axis=-1, keepdims=True) + 1e-06)
    normed = tokens_f / rms_value
    normed_in = (normed * gain_row).astype(jnp.bfloat16)
    expert_range = jnp.arange(specialist_span, dtype=jnp.int32)
    picked = chosen[:, :, None] == expert_range[None, None, :]
    member = jnp.any(picked, axis=1).astype(jnp.int32)
    weight_te = jnp.sum(jnp.where(picked, weights_in.astype(jnp.float32)[:, :, None], 0.0), axis=1)
    position = jnp.cumsum(member, axis=0) - member
    slot_range = jnp.arange(capacity, dtype=jnp.int32)
    placing = (position.T[:, None, :] == slot_range[None, :, None]) & (member.T[:, None, :] == 1)
    place_bf = placing.astype(jnp.bfloat16)
    place_f = placing.astype(jnp.float32)
    sent_in = jnp.einsum(
        "wst,td->wsd", place_bf, normed_in, preferred_element_type=jnp.float32
    ).astype(jnp.bfloat16)
    sent_grad = jnp.einsum(
        "wst,td->wsd", place_bf, grad_out, preferred_element_type=jnp.float32
    ).astype(jnp.bfloat16)
    sent_weight = jnp.sum(place_f * weight_te.T[:, None, :], axis=-1).astype(jnp.bfloat16)
    rows_in, rows_grad, rows_weight = (
        lax.all_to_all(
            jnp.repeat(sent_in, SPLIT, axis=0), "expert", split_axis=0, concat_axis=0, tiled=True
        ),
        lax.all_to_all(
            jnp.repeat(sent_grad, SPLIT, axis=0), "expert", split_axis=0, concat_axis=0, tiled=True
        ),
        lax.all_to_all(
            jnp.repeat(sent_weight, SPLIT, axis=0),
            "expert",
            split_axis=0,
            concat_axis=0,
            tiled=True,
        ),
    )
    total_rows = devices * capacity
    flat_in = rows_in.reshape(total_rows, model_width)
    flat_grad = rows_grad.reshape(total_rows, model_width)
    flat_weight = rows_weight.reshape(total_rows, 1).astype(jnp.float32)
    joined_slab = slab_gate_up.reshape(2 * hidden_slab, model_width)
    projected = rows_product(flat_in, joined_slab)
    gate_pre = projected[:, :hidden_slab]
    up_pre = projected[:, hidden_slab:]
    sigmoid_gate = jax.nn.sigmoid(gate_pre)
    active = gate_pre * sigmoid_gate
    hidden_act = active * up_pre
    scaled_hidden = (flat_weight * hidden_act).astype(jnp.bfloat16)
    back_proj = rows_product(flat_grad, slab_down)
    grad_hidden = flat_weight * back_proj
    grad_gate = (
        grad_hidden * up_pre * sigmoid_gate * (1.0 + gate_pre * (1.0 - sigmoid_gate))
    ).astype(jnp.bfloat16)
    grad_up = (grad_hidden * active).astype(jnp.bfloat16)
    grad_both = jnp.concatenate([grad_gate, grad_up], axis=1)
    weight_grad = column_product(grad_both, flat_in)
    down_grad = column_product(scaled_hidden, flat_grad)
    input_part = (
        jnp.dot(grad_both, joined_slab, preferred_element_type=jnp.float32)
        .astype(jnp.bfloat16)
        .reshape(devices, capacity, model_width)
    )
    combine_part = (
        jnp.sum(hidden_act * back_proj, axis=-1).astype(jnp.bfloat16).reshape(devices, capacity)
    )
    returned_in, returned_comb = (
        lax.all_to_all(input_part, "expert", split_axis=0, concat_axis=0, tiled=True),
        lax.all_to_all(combine_part, "expert", split_axis=0, concat_axis=0, tiled=True),
    )
    summed_in = jnp.sum(
        returned_in.reshape(specialist_span, SPLIT, capacity, model_width).astype(jnp.float32),
        axis=1,
    )
    summed_comb = jnp.sum(
        returned_comb.reshape(specialist_span, SPLIT, capacity).astype(jnp.float32), axis=1
    )
    grad_normed = jnp.einsum("wst,wsd->td", place_f, summed_in, precision=lax.Precision.HIGHEST)
    comb_te = jnp.sum(place_f * summed_comb[:, :, None], axis=1)
    grad_combine = jnp.sum(jnp.where(picked, comb_te.T[:, None, :], 0.0), axis=-1)
    scaled = grad_normed * gain_row
    inner_mean = jnp.mean(scaled * normed, axis=-1, keepdims=True)
    grad_tokens = (
        grad_out.astype(jnp.float32) + (scaled - normed * inner_mean) / rms_value
    ).astype(jnp.bfloat16)
    handed = shifted(grad_tokens, "pipe", -1)
    gate_up_out = weight_grad.reshape(2, hidden_slab, model_width).astype(jnp.bfloat16)
    return (
        handed[None],
        gate_up_out[None, None],
        down_grad.astype(jnp.bfloat16)[None, None],
        grad_combine[None],
    )


def call(kernel, outs, flops, moved, in_specs=None, scratch=(), limit=24):
    given = {} if in_specs is None else {"in_specs": in_specs}
    return pl.pallas_call(
        kernel,
        **given,
        out_shape=[jax.ShapeDtypeStruct(shape, kind) for shape, kind in outs],
        scratch_shapes=list(scratch),
        compiler_params=pltpu.CompilerParams(vmem_limit_bytes=limit << 20),
        cost_estimate=pl.CostEstimate(flops=flops, bytes_accessed=moved, transcendentals=0),
    )


TOKEN_FLOPS = 1_000_000_000
HIDDEN_FLOPS = 6_400_000_000
IN_HBM = pl.BlockSpec(memory_space=pltpu.HBM)
IN_VMEM = pl.BlockSpec(memory_space=pltpu.VMEM)


def take_rows(place, block):
    return lax.dot_general(place, block, (((1,), (0,)), ((), ())), preferred_element_type=F32)


def normed_rows(rows):
    rms = jnp.sqrt(jnp.mean(rows * rows, axis=-1, keepdims=True) + EPS)
    return rows / rms, rms


def in_parts(values):
    high = values.astype(BF16).astype(F32)
    middle = (values - high).astype(BF16).astype(F32)
    return high, middle, values - high - middle


def rows_kernel(ids_hbm, weight_hbm, gain_hbm, hidden_hbm, grad_hbm, in_ref, out_ref, both_ref,
                normed_ref, place_ref, ids_ref, weight_ref, gain_ref, hidden_ref, grad_ref, sems):
    tokens, width = hidden_ref.shape
    cap = SPECIALIST_CAP
    copies = [
        pltpu.make_async_copy(src, dst, sems.at[i])
        for i, (src, dst) in enumerate([
            (ids_hbm, ids_ref),
            (hidden_hbm, hidden_ref),
            (gain_hbm, gain_ref),
            (weight_hbm, weight_ref),
            (grad_hbm, grad_ref),
        ])
    ]
    for copy in copies:
        copy.start()
    copies[0].wait()
    hit = ids_ref[...] == 0
    member = jnp.max(hit.astype(F32), axis=0, keepdims=True)
    member = jnp.broadcast_to(member, (cap, tokens))
    earlier = lax.broadcasted_iota(jnp.int32, (tokens, tokens), 0) < lax.broadcasted_iota(
        jnp.int32, (tokens, tokens), 1
    )
    position = take_rows(member.astype(BF16), earlier.astype(F32).astype(BF16))
    slot = lax.broadcasted_iota(jnp.int32, (cap, tokens), 0).astype(F32)
    place = jnp.where(position == slot, member, 0.0)
    place_ref[...] = place
    copies[1].wait()
    normed, rms = normed_rows(take_rows(place.astype(BF16), hidden_ref[...]))
    normed_ref[...] = normed
    copies[2].wait()
    normed_in = normed * gain_ref[...]
    in_ref[:, :width] = normed_in.astype(BF16)
    copies[3].wait()
    weight = jnp.sum(
        jnp.where(hit, weight_ref[...].astype(F32), 0.0), axis=0, keepdims=True
    )
    taken = jnp.sum(place * weight, axis=1, keepdims=True)
    lane = lax.broadcasted_iota(jnp.int32, (cap, LANES), 1)
    extra = jnp.broadcast_to(taken, (cap, LANES))
    for number, part in enumerate(in_parts(rms)):
        extra = jnp.where(lane == number + 1, part, extra)
    in_ref[:, width:] = extra.astype(BF16)
    out_ref[:, width:] = place.astype(BF16)
    both_ref[:, width:] = jnp.concatenate([extra, place], axis=0).astype(BF16)
    copies[4].wait()
    grad = take_rows(place.astype(BF16), grad_ref[...])
    out_ref[:, :width] = grad.astype(BF16)
    both_ref[:, :width] = jnp.concatenate([normed_in, grad], axis=0).astype(BF16)


def token_kernel(after_ref, token_ref):
    del after_ref
    token_ref[...] = jnp.zeros_like(token_ref)


def pass_kernel(block_ref, after_ref, out_ref):
    del after_ref
    out_ref[...] = block_ref[...]


def stacked(refs, half, start, stop):
    cap = SPECIALIST_CAP
    pieces = []
    for ref in refs:
        block = ref[:, start:stop].astype(F32)
        pieces.append(block if ref.shape[0] == cap else block[half * cap : (half + 1) * cap])
    return jnp.concatenate(pieces, axis=0)


def project_kernel(*refs):
    *blocks, token_ref, slab_ref, slab_two_ref, pre_ref, pre_two_ref, first_ref, last_ref = refs
    del token_ref
    width = slab_ref.shape[1]
    rows = stacked(blocks, 0, 0, width).astype(BF16)
    half = first_ref.shape[0]
    pre_ref[...] = rows_product(rows, slab_ref[...])
    pre_two_ref[...] = rows_product(rows, slab_two_ref[...])
    first_ref[...] = rows[:half]
    last_ref[...] = rows[half:]


def hidden_kernel(*refs):
    in_blocks, blocks, refs = refs[:4], refs[4:8], refs[8:]
    pre_ref, pre_two_ref, slab_ref, down_ref, slab_two_ref, down_two_ref, *refs = refs
    own_ref, other_ref, first_ref, last_ref, keep_ref, send_ref = refs
    hidden, width = down_ref.shape
    half = own_ref.shape[0]
    rows = stacked(blocks, 1, 0, width).astype(BF16)
    weight = stacked(in_blocks, 0, width, width + LANES)[:, :1]
    total, comb = 0.0, 0.0
    for slab, down, pre, left_ref in (
        (slab_ref[...], down_ref[...], pre_ref[...], keep_ref),
        (slab_two_ref[...], down_two_ref[...], pre_two_ref[...], send_ref),
    ):
        back = rows_product(rows, down)
        gate = pre[:, :hidden]
        up = pre[:, hidden:]
        sig = jax.nn.sigmoid(gate)
        active = gate * sig
        act = active * up
        into = weight * back
        both = jnp.concatenate(
            [into * up * sig * (1.0 + gate * (1.0 - sig)), into * active], axis=1
        )
        total = total + take_rows(both.astype(BF16), slab)
        part = jnp.sum(act * back, axis=1, keepdims=True)
        comb = comb + part.astype(BF16).astype(F32)
        left_ref[:, : 2 * hidden] = both.astype(BF16)
        left_ref[:, 2 * hidden : 3 * hidden] = (weight * act).astype(BF16)
        left_ref[:, 3 * hidden :] = jnp.zeros(
            (left_ref.shape[0], left_ref.shape[1] - 3 * hidden), BF16
        )
    other_ref[:, :width] = total[half:].astype(BF16)
    own_ref[:, :width] = total[:half].astype(BF16)
    comb = jnp.broadcast_to(comb, (2 * half, LANES))
    high = comb.astype(BF16).astype(F32)
    lane = lax.broadcasted_iota(jnp.int32, comb.shape, 1)
    comb = jnp.where(lane < LANES // 2, high, comb - high).astype(BF16)
    other_ref[:, width:] = comb[half:]
    own_ref[:, width:] = comb[:half]
    first_ref[...] = rows[:half]
    last_ref[...] = rows[half:]


def split_kernel(keep_ref, got_ref, normed_ref, in_ref, far_in_ref, far_grad_ref, gain_ref,
                 own_ref, other_ref, own_comb_ref, other_comb_ref):
    cap, width = own_ref.shape
    total = keep_ref[...].astype(F32) + got_ref[...].astype(F32)
    gain = gain_ref[...]
    far = far_in_ref[...].astype(F32)
    extra = jnp.concatenate([in_ref[:, width:].astype(F32), far[:, width:]], axis=0)
    rms = extra[:, 1:2] + extra[:, 2:3] + extra[:, 3:4]
    normed = jnp.concatenate([normed_ref[...], far[:, :width] / gain], axis=0)
    scaled = total[:, :width] * gain
    inner = jnp.mean(scaled * normed, axis=-1, keepdims=True)
    change = (scaled - normed * inner) / rms
    other_ref[:, :width] = change[cap:].astype(BF16)
    other_ref[:, width:] = far_grad_ref[:, width:]
    own_ref[...] = change[:cap].astype(BF16)
    comb = total[:, width:]
    comb = comb + pltpu.roll(comb, LANES // 2, 1)
    other_comb_ref[...] = comb[cap:]
    own_comb_ref[...] = comb[:cap]


def weights_kernel(chunks, *refs):
    ins, grads, refs = refs[:4], refs[4:8], refs[8:]
    keep_ref, got_ref, after_ref, both_hbm, act_hbm, both_ref, act_ref, sems = refs
    del after_ref
    hidden, width = act_ref.shape
    left = jnp.concatenate([keep_ref[...], got_ref[...]], axis=0).astype(F32).T
    both = left[: 2 * hidden].astype(BF16)
    act = left[2 * hidden : 3 * hidden].astype(BF16)
    chunk = width // chunks
    copies = []
    for number in range(chunks):
        columns = slice(number * chunk, (number + 1) * chunk)
        for which, (left_rows, blocks, ref, hbm) in enumerate(
            ((both, ins, both_ref, both_hbm), (act, grads, act_ref, act_hbm))
        ):
            rows = jnp.concatenate([r[:, columns] for r in blocks], axis=0)
            ref[:, columns] = take_rows(left_rows, rows).astype(BF16)
            copy = pltpu.make_async_copy(
                ref.at[:, columns], hbm.at[:, columns], sems.at[2 * number + which]
            )
            copy.start()
            copies.append(copy)
    for copy in copies:
        copy.wait()


def weight_grads(blocks, keep, got, after, hidden, width):
    chunks = 4
    return pl.pallas_call(
        functools.partial(weights_kernel, chunks),
        in_specs=[IN_VMEM] * (len(blocks) + 2) + [pl.BlockSpec(memory_space=pl.ANY)],
        out_specs=[IN_HBM] * 2,
        out_shape=[
            jax.ShapeDtypeStruct((2 * hidden, width), BF16),
            jax.ShapeDtypeStruct((hidden, width), BF16),
        ],
        scratch_shapes=[
            pltpu.VMEM((2 * hidden, width), BF16),
            pltpu.VMEM((hidden, width), BF16),
            pltpu.SemaphoreType.DMA((2 * chunks,)),
        ],
        compiler_params=pltpu.CompilerParams(vmem_limit_bytes=24 << 20),
        cost_estimate=pl.CostEstimate(
            flops=6 * 64 * hidden * width, bytes_accessed=6 * hidden * width, transcendentals=0
        ),
    )(*blocks, keep, got, after)


def finish_kernel(other_ref, own_ref, grad_ref, out_ref):
    width = grad_ref.shape[1]
    place = other_ref[:, width:]
    grad = grad_ref[...]
    own = take_rows(place, grad)
    change = own_ref[...].astype(F32) + other_ref[:, :width].astype(F32)
    rows = (own + change).astype(BF16)
    back = place.astype(F32).T
    spread = take_rows(back.astype(BF16), rows)
    named = jnp.sum(back, axis=1, keepdims=True) > 0.0
    out_ref[...] = jnp.where(named, spread, grad.astype(F32)).astype(BF16)


def combine_kernel(own_comb_ref, other_comb_ref, ids_ref, place_ref, after_ref, comb_ref):
    del after_ref
    comb = own_comb_ref[...] + other_comb_ref[...]
    comb = jnp.sum(place_ref[...] * comb, axis=0, keepdims=True)
    comb_ref[...] = jnp.where(ids_ref[...] == 0, comb, 0.0)


def on_one(hidden_in, out_grad, expert_ids, route_weight, norm_gain, w_gate_up, w_down):
    sections = lax.axis_size("pipe")
    devices = lax.axis_size("expert")
    tokens, width = hidden_in.shape[1:]
    hidden = w_down.shape[2]
    cap = SPECIALIST_CAP
    ids = expert_ids[0].T
    weights = route_weight[0].T
    slab = w_gate_up.reshape(2 * hidden, width)
    down = w_down.reshape(hidden, width)
    in_hbm = lambda a: pltpu.with_memory_space_constraint(a, pltpu.HBM)
    wide = width + LANES
    total_rows = devices * cap

    def across(block, offset):
        return lax.ppermute(block, "expert", [(i, i ^ (2 * offset)) for i in range(devices)])

    def beside(block):
        return lax.ppermute(block, "expert", [(i, i ^ 1) for i in range(devices)])

    def handed(block, offset):
        route = [
            (((p + 1) % sections) * devices + i, p * devices + (i ^ (2 * offset)))
            for p in range(sections)
            for i in range(devices)
        ]
        return lax.ppermute(block, ("pipe", "expert"), route)

    next_grad = handed(out_grad[0], 0)
    row_in, row_grad, row_both, normed, place = call(
        rows_kernel,
        [((cap, wide), BF16)] * 2
        + [((2 * cap, wide), BF16), ((cap, width), F32), ((cap, tokens), F32)],
        4 * tokens * width * cap,
        4 * tokens * width,
        in_specs=[IN_HBM] * 5,
        scratch=[
            pltpu.VMEM(ids.shape, ids.dtype),
            pltpu.VMEM(weights.shape, weights.dtype),
            pltpu.VMEM(norm_gain.shape, norm_gain.dtype),
            pltpu.VMEM((tokens, width), BF16),
            pltpu.VMEM((tokens, width), BF16),
            pltpu.SemaphoreType.DMA((5,)),
        ],
    )(*map(in_hbm, (ids, weights, norm_gain, hidden_in[0], out_grad[0])))
    far_in = across(row_in, 2)
    far_grad = across(row_grad, 2)
    slab_two, down_two = beside(slab), beside(down)
    (passed,) = call(
        pass_kernel,
        [(row_both.shape, BF16)],
        0,
        4 * cap * wide,
        in_specs=[IN_VMEM] + [pl.BlockSpec(memory_space=pl.ANY)],
    )(row_both, slab_two)
    near = across(passed, 1)
    (token,) = call(
        token_kernel,
        [((cap, LANES), F32)],
        TOKEN_FLOPS,
        0,
        in_specs=[pl.BlockSpec(memory_space=pl.ANY)],
    )(far_grad)
    farthest_in = across(far_in, 1)
    farthest_grad = across(far_grad, 1)
    ins = [row_in, far_in, near, farthest_in]
    grads = [row_grad, far_grad, near, farthest_grad]
    half_rows = ((2 * cap, width), BF16)
    pre, pre_two, *in_halves = call(
        project_kernel,
        [((total_rows // 2, 2 * hidden), F32)] * 2 + [half_rows] * 2,
        0,
        4 * hidden * width,
    )(*ins, token, slab, slab_two)
    left_width = -(-3 * hidden // LANES) * LANES
    own_half, other_half, *rest = call(
        hidden_kernel,
        [((2 * cap, wide), BF16)] * 2
        + [half_rows] * 2
        + [((total_rows // 2, left_width), BF16)] * 2,
        HIDDEN_FLOPS,
        6 * hidden * width,
    )(*ins, *grads, pre, pre_two, slab, down, slab_two, down_two)
    *grad_halves, left_keep, left_send = rest
    own, other, own_comb, other_comb = call(
        split_kernel,
        [((cap, width), BF16), ((cap, wide), BF16)] + [((cap, LANES), F32)] * 2,
        2 * cap * width,
        8 * cap * width,
    )(own_half, across(other_half, 1), normed, row_in, far_in, far_grad, norm_gain)
    blocks = in_halves + [beside(b) for b in in_halves]
    blocks += grad_halves + [beside(b) for b in grad_halves]
    gate_up_out, down_out = weight_grads(blocks, left_keep, beside(left_send), own, hidden, width)
    (out,) = call(
        finish_kernel, [((tokens, width), BF16)], 4 * tokens * width * cap, 4 * tokens * width
    )(handed(other, 2), handed(own, 0), next_grad)
    (combined,) = call(
        combine_kernel,
        [((SPLIT, tokens), F32)],
        0,
        4 * SPLIT * tokens,
        in_specs=[IN_VMEM] * 4 + [IN_HBM],
    )(own_comb, across(other_comb, 2), ids, place, in_hbm(out))
    return (
        out[None],
        gate_up_out.reshape(1, 1, 2, hidden, width),
        down_out.reshape(1, 1, hidden, width),
        combined.T[None],
    )


def solution(mesh):
    on_device = on_one if mesh.shape["expert"] == SPLIT else on_many
    return jax.shard_map(
        on_device,
        mesh=mesh,
        in_specs=(
            P("pipe", "expert", None),
            P("pipe", "expert", None),
            P("pipe", "expert", None),
            P("pipe", "expert", None),
            P("pipe", None),
            P("pipe", "expert", None, None, None),
            P("pipe", "expert", None, None),
        ),
        out_specs=(
            P("pipe", "expert", None),
            P("pipe", "expert", None, None, None),
            P("pipe", "expert", None, None),
            P("pipe", "expert", None),
        ),
        check_vma=False,
    )
```

```python
import functools

import jax
import jax.numpy as jnp
from jax import lax
from jax.experimental import pallas as pl
from jax.experimental.pallas import tpu as pltpu
from jax.sharding import PartitionSpec as P

SPLIT = 8
SPECIALIST_CAP = 8
LANES = 128
EPS = 1e-06
F32 = jnp.float32
BF16 = jnp.bfloat16


def shifted(block, axis, distance):
    devices = range(lax.axis_size(axis))
    route = [((i - distance) % len(devices), i) for i in devices]
    return lax.ppermute(block, axis, route)


def rows_product(left_rows, right_rows):
    return lax.dot_general(
        left_rows, right_rows, (((1,), (1,)), ((), ())), preferred_element_type=jnp.float32
    )


def column_product(left_rows, right_rows):
    return lax.dot_general(
        left_rows, right_rows, (((0,), (0,)), ((), ())), preferred_element_type=jnp.float32
    )


def on_many(hidden_in, out_grad, expert_ids, route_weight, norm_gain, w_gate_up, w_down):
    tokens_in = hidden_in[0]
    grad_out = out_grad[0]
    chosen = expert_ids[0]
    weights_in = route_weight[0]
    gain_row = norm_gain[0]
    slab_gate_up = w_gate_up[0, 0]
    slab_down = w_down[0, 0]
    devices = lax.axis_size("expert")
    specialist_span = devices // SPLIT
    model_width = tokens_in.shape[1]
    hidden_slab = slab_down.shape[0]
    capacity = SPECIALIST_CAP
    tokens_f = tokens_in.astype(jnp.float32)
    rms_value = jnp.sqrt(jnp.mean(tokens_f * tokens_f, axis=-1, keepdims=True) + 1e-06)
    normed = tokens_f / rms_value
    normed_in = (normed * gain_row).astype(jnp.bfloat16)
    expert_range = jnp.arange(specialist_span, dtype=jnp.int32)
    picked = chosen[:, :, None] == expert_range[None, None, :]
    member = jnp.any(picked, axis=1).astype(jnp.int32)
    weight_te = jnp.sum(jnp.where(picked, weights_in.astype(jnp.float32)[:, :, None], 0.0), axis=1)
    position = jnp.cumsum(member, axis=0) - member
    slot_range = jnp.arange(capacity, dtype=jnp.int32)
    placing = (position.T[:, None, :] == slot_range[None, :, None]) & (member.T[:, None, :] == 1)
    place_bf = placing.astype(jnp.bfloat16)
    place_f = placing.astype(jnp.float32)
    sent_in = jnp.einsum(
        "wst,td->wsd", place_bf, normed_in, preferred_element_type=jnp.float32
    ).astype(jnp.bfloat16)
    sent_grad = jnp.einsum(
        "wst,td->wsd", place_bf, grad_out, preferred_element_type=jnp.float32
    ).astype(jnp.bfloat16)
    sent_weight = jnp.sum(place_f * weight_te.T[:, None, :], axis=-1).astype(jnp.bfloat16)
    rows_in, rows_grad, rows_weight = (
        lax.all_to_all(
            jnp.repeat(sent_in, SPLIT, axis=0), "expert", split_axis=0, concat_axis=0, tiled=True
        ),
        lax.all_to_all(
            jnp.repeat(sent_grad, SPLIT, axis=0), "expert", split_axis=0, concat_axis=0, tiled=True
        ),
        lax.all_to_all(
            jnp.repeat(sent_weight, SPLIT, axis=0),
            "expert",
            split_axis=0,
            concat_axis=0,
            tiled=True,
        ),
    )
    total_rows = devices * capacity
    flat_in = rows_in.reshape(total_rows, model_width)
    flat_grad = rows_grad.reshape(total_rows, model_width)
    flat_weight = rows_weight.reshape(total_rows, 1).astype(jnp.float32)
    joined_slab = slab_gate_up.reshape(2 * hidden_slab, model_width)
    projected = rows_product(flat_in, joined_slab)
    gate_pre = projected[:, :hidden_slab]
    up_pre = projected[:, hidden_slab:]
    sigmoid_gate = jax.nn.sigmoid(gate_pre)
    active = gate_pre * sigmoid_gate
    hidden_act = active * up_pre
    scaled_hidden = (flat_weight * hidden_act).astype(jnp.bfloat16)
    back_proj = rows_product(flat_grad, slab_down)
    grad_hidden = flat_weight * back_proj
    grad_gate = (
        grad_hidden * up_pre * sigmoid_gate * (1.0 + gate_pre * (1.0 - sigmoid_gate))
    ).astype(jnp.bfloat16)
    grad_up = (grad_hidden * active).astype(jnp.bfloat16)
    grad_both = jnp.concatenate([grad_gate, grad_up], axis=1)
    weight_grad = column_product(grad_both, flat_in)
    down_grad = column_product(scaled_hidden, flat_grad)
    input_part = (
        jnp.dot(grad_both, joined_slab, preferred_element_type=jnp.float32)
        .astype(jnp.bfloat16)
        .reshape(devices, capacity, model_width)
    )
    combine_part = (
        jnp.sum(hidden_act * back_proj, axis=-1).astype(jnp.bfloat16).reshape(devices, capacity)
    )
    returned_in, returned_comb = (
        lax.all_to_all(input_part, "expert", split_axis=0, concat_axis=0, tiled=True),
        lax.all_to_all(combine_part, "expert", split_axis=0, concat_axis=0, tiled=True),
    )
    summed_in = jnp.sum(
        returned_in.reshape(specialist_span, SPLIT, capacity, model_width).astype(jnp.float32),
        axis=1,
    )
    summed_comb = jnp.sum(
        returned_comb.reshape(specialist_span, SPLIT, capacity).astype(jnp.float32), axis=1
    )
    grad_normed = jnp.einsum("wst,wsd->td", place_f, summed_in, precision=lax.Precision.HIGHEST)
    comb_te = jnp.sum(place_f * summed_comb[:, :, None], axis=1)
    grad_combine = jnp.sum(jnp.where(picked, comb_te.T[:, None, :], 0.0), axis=-1)
    scaled = grad_normed * gain_row
    inner_mean = jnp.mean(scaled * normed, axis=-1, keepdims=True)
    grad_tokens = (
        grad_out.astype(jnp.float32) + (scaled - normed * inner_mean) / rms_value
    ).astype(jnp.bfloat16)
    handed = shifted(grad_tokens, "pipe", -1)
    gate_up_out = weight_grad.reshape(2, hidden_slab, model_width).astype(jnp.bfloat16)
    return (
        handed[None],
        gate_up_out[None, None],
        down_grad.astype(jnp.bfloat16)[None, None],
        grad_combine[None],
    )


def call(kernel, outs, flops, moved, in_specs=None, scratch=(), limit=24):
    given = {} if in_specs is None else {"in_specs": in_specs}
    return pl.pallas_call(
        kernel,
        **given,
        out_shape=[jax.ShapeDtypeStruct(shape, kind) for shape, kind in outs],
        scratch_shapes=list(scratch),
        compiler_params=pltpu.CompilerParams(vmem_limit_bytes=limit << 20),
        cost_estimate=pl.CostEstimate(flops=flops, bytes_accessed=moved, transcendentals=0),
    )


TOKEN_FLOPS = 1_000_000_000
HIDDEN_FLOPS = 6_400_000_000
IN_HBM = pl.BlockSpec(memory_space=pltpu.HBM)
IN_VMEM = pl.BlockSpec(memory_space=pltpu.VMEM)


def take_rows(place, block):
    return lax.dot_general(place, block, (((1,), (0,)), ((), ())), preferred_element_type=F32)


def normed_rows(rows):
    rms = jnp.sqrt(jnp.mean(rows * rows, axis=-1, keepdims=True) + EPS)
    return rows / rms, rms


def in_parts(values):
    high = values.astype(BF16).astype(F32)
    middle = (values - high).astype(BF16).astype(F32)
    return high, middle, values - high - middle


def rows_kernel(ids_hbm, weight_ref, gain_hbm, hidden_hbm, grad_hbm, in_ref, out_ref, both_ref,
                normed_ref, place_ref, ids_ref, gain_ref, hidden_ref, grad_ref, sems):
    tokens, width = hidden_ref.shape
    cap = SPECIALIST_CAP
    copies = [
        pltpu.make_async_copy(src, dst, sems.at[i])
        for i, (src, dst) in enumerate([
            (ids_hbm, ids_ref),
            (hidden_hbm, hidden_ref),
            (gain_hbm, gain_ref),
            (grad_hbm, grad_ref),
        ])
    ]
    for copy in copies:
        copy.start()
    copies[0].wait()
    hit = ids_ref[...] == 0
    member = jnp.max(hit.astype(F32), axis=0, keepdims=True)
    member = jnp.broadcast_to(member, (cap, tokens))
    earlier = lax.broadcasted_iota(jnp.int32, (tokens, tokens), 0) < lax.broadcasted_iota(
        jnp.int32, (tokens, tokens), 1
    )
    position = take_rows(member.astype(BF16), earlier.astype(F32).astype(BF16))
    slot = lax.broadcasted_iota(jnp.int32, (cap, tokens), 0).astype(F32)
    place = jnp.where(position == slot, member, 0.0)
    place_ref[...] = place
    copies[1].wait()
    normed, rms = normed_rows(take_rows(place.astype(BF16), hidden_ref[...]))
    normed_ref[...] = normed
    copies[2].wait()
    normed_in = normed * gain_ref[...]
    in_ref[:, :width] = normed_in.astype(BF16)
    weight = jnp.sum(
        jnp.where(hit, weight_ref[...].astype(F32), 0.0), axis=0, keepdims=True
    )
    taken = jnp.sum(place * weight, axis=1, keepdims=True)
    lane = lax.broadcasted_iota(jnp.int32, (cap, LANES), 1)
    extra = jnp.broadcast_to(taken, (cap, LANES))
    for number, part in enumerate(in_parts(rms)):
        extra = jnp.where(lane == number + 1, part, extra)
    in_ref[:, width:] = extra.astype(BF16)
    out_ref[:, width:] = place.astype(BF16)
    both_ref[:, width:] = jnp.concatenate([extra, place], axis=0).astype(BF16)
    copies[3].wait()
    grad = take_rows(place.astype(BF16), grad_ref[...])
    out_ref[:, :width] = grad.astype(BF16)
    both_ref[:, :width] = jnp.concatenate([normed_in, grad], axis=0).astype(BF16)


def token_kernel(after_ref, token_ref):
    del after_ref
    token_ref[...] = jnp.zeros_like(token_ref)


def pass_kernel(block_ref, after_ref, out_ref):
    del after_ref
    out_ref[...] = block_ref[...]


def stacked(refs, half, start, stop):
    cap = SPECIALIST_CAP
    pieces = []
    for ref in refs:
        block = ref[:, start:stop].astype(F32)
        pieces.append(block if ref.shape[0] == cap else block[half * cap : (half + 1) * cap])
    return jnp.concatenate(pieces, axis=0)


def project_kernel(*refs):
    *blocks, token_ref, slab_ref, slab_two_ref, pre_ref, pre_two_ref, first_ref, last_ref = refs
    del token_ref
    width = slab_ref.shape[1]
    rows = stacked(blocks, 0, 0, width).astype(BF16)
    half = first_ref.shape[0]
    pre_ref[...] = rows_product(rows, slab_ref[...])
    pre_two_ref[...] = rows_product(rows, slab_two_ref[...])
    first_ref[...] = rows[:half]
    last_ref[...] = rows[half:]


def hidden_kernel(*refs):
    in_blocks, blocks, refs = refs[:4], refs[4:8], refs[8:]
    pre_ref, pre_two_ref, slab_ref, down_ref, slab_two_ref, down_two_ref, *refs = refs
    own_ref, other_ref, first_ref, last_ref, keep_ref, send_ref = refs
    hidden, width = down_ref.shape
    half = own_ref.shape[0]
    rows = stacked(blocks, 1, 0, width).astype(BF16)
    weight = stacked(in_blocks, 0, width, width + LANES)[:, :1]
    total, comb = 0.0, 0.0
    for slab, down, pre, left_ref in (
        (slab_ref[...], down_ref[...], pre_ref[...], keep_ref),
        (slab_two_ref[...], down_two_ref[...], pre_two_ref[...], send_ref),
    ):
        back = rows_product(rows, down)
        gate = pre[:, :hidden]
        up = pre[:, hidden:]
        sig = jax.nn.sigmoid(gate)
        active = gate * sig
        act = active * up
        into = weight * back
        both = jnp.concatenate(
            [into * up * sig * (1.0 + gate * (1.0 - sig)), into * active], axis=1
        )
        total = total + take_rows(both.astype(BF16), slab)
        part = jnp.sum(act * back, axis=1, keepdims=True)
        comb = comb + part.astype(BF16).astype(F32)
        left_ref[:, : 2 * hidden] = both.astype(BF16)
        left_ref[:, 2 * hidden : 3 * hidden] = (weight * act).astype(BF16)
        left_ref[:, 3 * hidden :] = jnp.zeros(
            (left_ref.shape[0], left_ref.shape[1] - 3 * hidden), BF16
        )
    other_ref[:, :width] = total[half:].astype(BF16)
    own_ref[:, :width] = total[:half].astype(BF16)
    comb = jnp.broadcast_to(comb, (2 * half, LANES))
    high = comb.astype(BF16).astype(F32)
    lane = lax.broadcasted_iota(jnp.int32, comb.shape, 1)
    comb = jnp.where(lane < LANES // 2, high, comb - high).astype(BF16)
    other_ref[:, width:] = comb[half:]
    own_ref[:, width:] = comb[:half]
    first_ref[...] = rows[:half]
    last_ref[...] = rows[half:]


def split_kernel(keep_ref, got_ref, normed_ref, in_ref, far_in_ref, far_grad_ref, gain_ref,
                 own_ref, other_ref, own_comb_ref, other_comb_ref):
    cap, width = own_ref.shape
    total = keep_ref[...].astype(F32) + got_ref[...].astype(F32)
    gain = gain_ref[...]
    far = far_in_ref[...].astype(F32)
    extra = jnp.concatenate([in_ref[:, width:].astype(F32), far[:, width:]], axis=0)
    rms = extra[:, 1:2] + extra[:, 2:3] + extra[:, 3:4]
    normed = jnp.concatenate([normed_ref[...], far[:, :width] / gain], axis=0)
    scaled = total[:, :width] * gain
    inner = jnp.mean(scaled * normed, axis=-1, keepdims=True)
    change = (scaled - normed * inner) / rms
    other_ref[:, :width] = change[cap:].astype(BF16)
    other_ref[:, width:] = far_grad_ref[:, width:]
    own_ref[...] = change[:cap].astype(BF16)
    comb = total[:, width:]
    comb = comb + pltpu.roll(comb, LANES // 2, 1)
    other_comb_ref[...] = comb[cap:]
    own_comb_ref[...] = comb[:cap]


def weights_kernel(chunks, *refs):
    ins, grads, refs = refs[:4], refs[4:8], refs[8:]
    keep_ref, got_ref, after_ref, both_hbm, act_hbm, both_ref, act_ref, sems = refs
    del after_ref
    hidden, width = act_ref.shape
    left = jnp.concatenate([keep_ref[...], got_ref[...]], axis=0).astype(F32).T
    both = left[: 2 * hidden].astype(BF16)
    act = left[2 * hidden : 3 * hidden].astype(BF16)
    chunk = width // chunks
    copies = []
    for number in range(chunks):
        columns = slice(number * chunk, (number + 1) * chunk)
        for which, (left_rows, blocks, ref, hbm) in enumerate(
            ((both, ins, both_ref, both_hbm), (act, grads, act_ref, act_hbm))
        ):
            rows = jnp.concatenate([r[:, columns] for r in blocks], axis=0)
            ref[:, columns] = take_rows(left_rows, rows).astype(BF16)
            copy = pltpu.make_async_copy(
                ref.at[:, columns], hbm.at[:, columns], sems.at[2 * number + which]
            )
            copy.start()
            copies.append(copy)
    for copy in copies:
        copy.wait()


def weight_grads(blocks, keep, got, after, hidden, width):
    chunks = 4
    return pl.pallas_call(
        functools.partial(weights_kernel, chunks),
        in_specs=[IN_VMEM] * (len(blocks) + 2) + [pl.BlockSpec(memory_space=pl.ANY)],
        out_specs=[IN_HBM] * 2,
        out_shape=[
            jax.ShapeDtypeStruct((2 * hidden, width), BF16),
            jax.ShapeDtypeStruct((hidden, width), BF16),
        ],
        scratch_shapes=[
            pltpu.VMEM((2 * hidden, width), BF16),
            pltpu.VMEM((hidden, width), BF16),
            pltpu.SemaphoreType.DMA((2 * chunks,)),
        ],
        compiler_params=pltpu.CompilerParams(vmem_limit_bytes=24 << 20),
        cost_estimate=pl.CostEstimate(
            flops=6 * 64 * hidden * width, bytes_accessed=6 * hidden * width, transcendentals=0
        ),
    )(*blocks, keep, got, after)


def finish_kernel(other_ref, own_ref, grad_ref, out_ref):
    width = grad_ref.shape[1]
    place = other_ref[:, width:]
    grad = grad_ref[...]
    own = take_rows(place, grad)
    change = own_ref[...].astype(F32) + other_ref[:, :width].astype(F32)
    rows = (own + change).astype(BF16)
    back = place.astype(F32).T
    spread = take_rows(back.astype(BF16), rows)
    named = jnp.sum(back, axis=1, keepdims=True) > 0.0
    out_ref[...] = jnp.where(named, spread, grad.astype(F32)).astype(BF16)


def combine_kernel(own_comb_ref, other_comb_ref, ids_ref, place_ref, after_ref, comb_ref):
    del after_ref
    comb = own_comb_ref[...] + other_comb_ref[...]
    comb = jnp.sum(place_ref[...] * comb, axis=0, keepdims=True)
    comb_ref[...] = jnp.where(ids_ref[...] == 0, comb, 0.0)


def on_one(hidden_in, out_grad, expert_ids, route_weight, norm_gain, w_gate_up, w_down):
    sections = lax.axis_size("pipe")
    devices = lax.axis_size("expert")
    tokens, width = hidden_in.shape[1:]
    hidden = w_down.shape[2]
    cap = SPECIALIST_CAP
    ids = expert_ids[0].T
    weights = route_weight[0].T
    slab = w_gate_up.reshape(2 * hidden, width)
    down = w_down.reshape(hidden, width)
    in_hbm = lambda a: pltpu.with_memory_space_constraint(a, pltpu.HBM)
    wide = width + LANES
    total_rows = devices * cap

    def across(block, offset):
        return lax.ppermute(block, "expert", [(i, i ^ (2 * offset)) for i in range(devices)])

    def beside(block):
        return lax.ppermute(block, "expert", [(i, i ^ 1) for i in range(devices)])

    def handed(block, offset):
        route = [
            (((p + 1) % sections) * devices + i, p * devices + (i ^ (2 * offset)))
            for p in range(sections)
            for i in range(devices)
        ]
        return lax.ppermute(block, ("pipe", "expert"), route)

    next_grad = handed(out_grad[0], 0)
    row_in, row_grad, row_both, normed, place = call(
        rows_kernel,
        [((cap, wide), BF16)] * 2
        + [((2 * cap, wide), BF16), ((cap, width), F32), ((cap, tokens), F32)],
        4 * tokens * width * cap,
        4 * tokens * width,
        in_specs=[IN_HBM, IN_VMEM] + [IN_HBM] * 3,
        scratch=[
            pltpu.VMEM(ids.shape, ids.dtype),
            pltpu.VMEM(norm_gain.shape, norm_gain.dtype),
            pltpu.VMEM((tokens, width), BF16),
            pltpu.VMEM((tokens, width), BF16),
            pltpu.SemaphoreType.DMA((4,)),
        ],
    )(in_hbm(ids), weights, *map(in_hbm, (norm_gain, hidden_in[0], out_grad[0])))
    far_in = across(row_in, 2)
    far_grad = across(row_grad, 2)
    slab_two, down_two = beside(slab), beside(down)
    (passed,) = call(
        pass_kernel,
        [(row_both.shape, BF16)],
        0,
        4 * cap * wide,
        in_specs=[IN_VMEM] + [pl.BlockSpec(memory_space=pl.ANY)],
    )(row_both, slab_two)
    near = across(passed, 1)
    (token,) = call(
        token_kernel,
        [((cap, LANES), F32)],
        TOKEN_FLOPS,
        0,
        in_specs=[pl.BlockSpec(memory_space=pl.ANY)],
    )(far_grad)
    farthest_in = across(far_in, 1)
    farthest_grad = across(far_grad, 1)
    ins = [row_in, far_in, near, farthest_in]
    grads = [row_grad, far_grad, near, farthest_grad]
    half_rows = ((2 * cap, width), BF16)
    pre, pre_two, *in_halves = call(
        project_kernel,
        [((total_rows // 2, 2 * hidden), F32)] * 2 + [half_rows] * 2,
        0,
        4 * hidden * width,
    )(*ins, token, slab, slab_two)
    left_width = -(-3 * hidden // LANES) * LANES
    own_half, other_half, *rest = call(
        hidden_kernel,
        [((2 * cap, wide), BF16)] * 2
        + [half_rows] * 2
        + [((total_rows // 2, left_width), BF16)] * 2,
        HIDDEN_FLOPS,
        6 * hidden * width,
    )(*ins, *grads, pre, pre_two, slab, down, slab_two, down_two)
    *grad_halves, left_keep, left_send = rest
    own, other, own_comb, other_comb = call(
        split_kernel,
        [((cap, width), BF16), ((cap, wide), BF16)] + [((cap, LANES), F32)] * 2,
        2 * cap * width,
        8 * cap * width,
    )(own_half, across(other_half, 1), normed, row_in, far_in, far_grad, norm_gain)
    blocks = in_halves + [beside(b) for b in in_halves]
    blocks += grad_halves + [beside(b) for b in grad_halves]
    gate_up_out, down_out = weight_grads(blocks, left_keep, beside(left_send), own, hidden, width)
    (out,) = call(
        finish_kernel, [((tokens, width), BF16)], 4 * tokens * width * cap, 4 * tokens * width
    )(handed(other, 2), handed(own, 0), next_grad)
    (combined,) = call(
        combine_kernel,
        [((SPLIT, tokens), F32)],
        0,
        4 * SPLIT * tokens,
        in_specs=[IN_VMEM] * 4 + [IN_HBM],
    )(own_comb, across(other_comb, 2), ids, place, in_hbm(out))
    return (
        out[None],
        gate_up_out.reshape(1, 1, 2, hidden, width),
        down_out.reshape(1, 1, hidden, width),
        combined.T[None],
    )


def solution(mesh):
    on_device = on_one if mesh.shape["expert"] == SPLIT else on_many
    return jax.shard_map(
        on_device,
        mesh=mesh,
        in_specs=(
            P("pipe", "expert", None),
            P("pipe", "expert", None),
            P("pipe", "expert", None),
            P("pipe", "expert", None),
            P("pipe", None),
            P("pipe", "expert", None, None, None),
            P("pipe", "expert", None, None),
        ),
        out_specs=(
            P("pipe", "expert", None),
            P("pipe", "expert", None, None, None),
            P("pipe", "expert", None, None),
            P("pipe", "expert", None),
        ),
        check_vma=False,
    )
```

```python
import functools

import jax
import jax.numpy as jnp
from jax import lax
from jax.experimental import pallas as pl
from jax.experimental.pallas import tpu as pltpu
from jax.sharding import PartitionSpec as P

SPLIT = 8
SPECIALIST_CAP = 8
LANES = 128
EPS = 1e-06
F32 = jnp.float32
BF16 = jnp.bfloat16


def shifted(block, axis, distance):
    devices = range(lax.axis_size(axis))
    route = [((i - distance) % len(devices), i) for i in devices]
    return lax.ppermute(block, axis, route)


def rows_product(left_rows, right_rows):
    return lax.dot_general(
        left_rows, right_rows, (((1,), (1,)), ((), ())), preferred_element_type=jnp.float32
    )


def column_product(left_rows, right_rows):
    return lax.dot_general(
        left_rows, right_rows, (((0,), (0,)), ((), ())), preferred_element_type=jnp.float32
    )


def on_many(hidden_in, out_grad, expert_ids, route_weight, norm_gain, w_gate_up, w_down):
    tokens_in = hidden_in[0]
    grad_out = out_grad[0]
    chosen = expert_ids[0]
    weights_in = route_weight[0]
    gain_row = norm_gain[0]
    slab_gate_up = w_gate_up[0, 0]
    slab_down = w_down[0, 0]
    devices = lax.axis_size("expert")
    specialist_span = devices // SPLIT
    model_width = tokens_in.shape[1]
    hidden_slab = slab_down.shape[0]
    capacity = SPECIALIST_CAP
    tokens_f = tokens_in.astype(jnp.float32)
    rms_value = jnp.sqrt(jnp.mean(tokens_f * tokens_f, axis=-1, keepdims=True) + 1e-06)
    normed = tokens_f / rms_value
    normed_in = (normed * gain_row).astype(jnp.bfloat16)
    expert_range = jnp.arange(specialist_span, dtype=jnp.int32)
    picked = chosen[:, :, None] == expert_range[None, None, :]
    member = jnp.any(picked, axis=1).astype(jnp.int32)
    weight_te = jnp.sum(jnp.where(picked, weights_in.astype(jnp.float32)[:, :, None], 0.0), axis=1)
    position = jnp.cumsum(member, axis=0) - member
    slot_range = jnp.arange(capacity, dtype=jnp.int32)
    placing = (position.T[:, None, :] == slot_range[None, :, None]) & (member.T[:, None, :] == 1)
    place_bf = placing.astype(jnp.bfloat16)
    place_f = placing.astype(jnp.float32)
    sent_in = jnp.einsum(
        "wst,td->wsd", place_bf, normed_in, preferred_element_type=jnp.float32
    ).astype(jnp.bfloat16)
    sent_grad = jnp.einsum(
        "wst,td->wsd", place_bf, grad_out, preferred_element_type=jnp.float32
    ).astype(jnp.bfloat16)
    sent_weight = jnp.sum(place_f * weight_te.T[:, None, :], axis=-1).astype(jnp.bfloat16)
    rows_in, rows_grad, rows_weight = (
        lax.all_to_all(
            jnp.repeat(sent_in, SPLIT, axis=0), "expert", split_axis=0, concat_axis=0, tiled=True
        ),
        lax.all_to_all(
            jnp.repeat(sent_grad, SPLIT, axis=0), "expert", split_axis=0, concat_axis=0, tiled=True
        ),
        lax.all_to_all(
            jnp.repeat(sent_weight, SPLIT, axis=0),
            "expert",
            split_axis=0,
            concat_axis=0,
            tiled=True,
        ),
    )
    total_rows = devices * capacity
    flat_in = rows_in.reshape(total_rows, model_width)
    flat_grad = rows_grad.reshape(total_rows, model_width)
    flat_weight = rows_weight.reshape(total_rows, 1).astype(jnp.float32)
    joined_slab = slab_gate_up.reshape(2 * hidden_slab, model_width)
    projected = rows_product(flat_in, joined_slab)
    gate_pre = projected[:, :hidden_slab]
    up_pre = projected[:, hidden_slab:]
    sigmoid_gate = jax.nn.sigmoid(gate_pre)
    active = gate_pre * sigmoid_gate
    hidden_act = active * up_pre
    scaled_hidden = (flat_weight * hidden_act).astype(jnp.bfloat16)
    back_proj = rows_product(flat_grad, slab_down)
    grad_hidden = flat_weight * back_proj
    grad_gate = (
        grad_hidden * up_pre * sigmoid_gate * (1.0 + gate_pre * (1.0 - sigmoid_gate))
    ).astype(jnp.bfloat16)
    grad_up = (grad_hidden * active).astype(jnp.bfloat16)
    grad_both = jnp.concatenate([grad_gate, grad_up], axis=1)
    weight_grad = column_product(grad_both, flat_in)
    down_grad = column_product(scaled_hidden, flat_grad)
    input_part = (
        jnp.dot(grad_both, joined_slab, preferred_element_type=jnp.float32)
        .astype(jnp.bfloat16)
        .reshape(devices, capacity, model_width)
    )
    combine_part = (
        jnp.sum(hidden_act * back_proj, axis=-1).astype(jnp.bfloat16).reshape(devices, capacity)
    )
    returned_in, returned_comb = (
        lax.all_to_all(input_part, "expert", split_axis=0, concat_axis=0, tiled=True),
        lax.all_to_all(combine_part, "expert", split_axis=0, concat_axis=0, tiled=True),
    )
    summed_in = jnp.sum(
        returned_in.reshape(specialist_span, SPLIT, capacity, model_width).astype(jnp.float32),
        axis=1,
    )
    summed_comb = jnp.sum(
        returned_comb.reshape(specialist_span, SPLIT, capacity).astype(jnp.float32), axis=1
    )
    grad_normed = jnp.einsum("wst,wsd->td", place_f, summed_in, precision=lax.Precision.HIGHEST)
    comb_te = jnp.sum(place_f * summed_comb[:, :, None], axis=1)
    grad_combine = jnp.sum(jnp.where(picked, comb_te.T[:, None, :], 0.0), axis=-1)
    scaled = grad_normed * gain_row
    inner_mean = jnp.mean(scaled * normed, axis=-1, keepdims=True)
    grad_tokens = (
        grad_out.astype(jnp.float32) + (scaled - normed * inner_mean) / rms_value
    ).astype(jnp.bfloat16)
    handed = shifted(grad_tokens, "pipe", -1)
    gate_up_out = weight_grad.reshape(2, hidden_slab, model_width).astype(jnp.bfloat16)
    return (
        handed[None],
        gate_up_out[None, None],
        down_grad.astype(jnp.bfloat16)[None, None],
        grad_combine[None],
    )


def call(kernel, outs, flops, moved, in_specs=None, scratch=(), limit=24):
    given = {} if in_specs is None else {"in_specs": in_specs}
    return pl.pallas_call(
        kernel,
        **given,
        out_shape=[jax.ShapeDtypeStruct(shape, kind) for shape, kind in outs],
        scratch_shapes=list(scratch),
        compiler_params=pltpu.CompilerParams(vmem_limit_bytes=limit << 20),
        cost_estimate=pl.CostEstimate(flops=flops, bytes_accessed=moved, transcendentals=0),
    )


TOKEN_FLOPS = 1_000_000_000
HIDDEN_FLOPS = 6_400_000_000
IN_HBM = pl.BlockSpec(memory_space=pltpu.HBM)
IN_VMEM = pl.BlockSpec(memory_space=pltpu.VMEM)


def take_rows(place, block):
    return lax.dot_general(place, block, (((1,), (0,)), ((), ())), preferred_element_type=F32)


def normed_rows(rows):
    rms = jnp.sqrt(jnp.mean(rows * rows, axis=-1, keepdims=True) + EPS)
    return rows / rms, rms


def in_parts(values):
    high = values.astype(BF16).astype(F32)
    middle = (values - high).astype(BF16).astype(F32)
    return high, middle, values - high - middle


def rows_kernel(ids_hbm, weight_hbm, gain_hbm, hidden_hbm, grad_hbm, in_ref, out_ref, both_ref,
                normed_ref, place_ref, ids_ref, weight_ref, gain_ref, hidden_ref, grad_ref, sems):
    tokens, width = hidden_ref.shape
    cap = SPECIALIST_CAP
    copies = [
        pltpu.make_async_copy(src, dst, sems.at[i])
        for i, (src, dst) in enumerate([
            (ids_hbm, ids_ref),
            (hidden_hbm, hidden_ref),
            (gain_hbm, gain_ref),
            (weight_hbm, weight_ref),
            (grad_hbm, grad_ref),
        ])
    ]
    for copy in copies:
        copy.start()
    copies[0].wait()
    hit = ids_ref[...] == 0
    member = jnp.max(hit.astype(F32), axis=0, keepdims=True)
    member = jnp.broadcast_to(member, (cap, tokens))
    earlier = lax.broadcasted_iota(jnp.int32, (tokens, tokens), 0) < lax.broadcasted_iota(
        jnp.int32, (tokens, tokens), 1
    )
    position = take_rows(member.astype(BF16), earlier.astype(F32).astype(BF16))
    slot = lax.broadcasted_iota(jnp.int32, (cap, tokens), 0).astype(F32)
    place = jnp.where(position == slot, member, 0.0)
    place_ref[...] = place
    copies[1].wait()
    normed, rms = normed_rows(take_rows(place.astype(BF16), hidden_ref[...]))
    normed_ref[...] = normed
    copies[2].wait()
    normed_in = normed * gain_ref[...]
    in_ref[:, :width] = normed_in.astype(BF16)
    copies[3].wait()
    weight = jnp.sum(
        jnp.where(hit, weight_ref[...].astype(F32), 0.0), axis=0, keepdims=True
    )
    taken = jnp.sum(place * weight, axis=1, keepdims=True)
    lane = lax.broadcasted_iota(jnp.int32, (cap, LANES), 1)
    extra = jnp.broadcast_to(taken, (cap, LANES))
    for number, part in enumerate(in_parts(rms)):
        extra = jnp.where(lane == number + 1, part, extra)
    in_ref[:, width:] = extra.astype(BF16)
    out_ref[:, width:] = place.astype(BF16)
    both_ref[:, width:] = jnp.concatenate([extra, place], axis=0).astype(BF16)
    copies[4].wait()
    grad = take_rows(place.astype(BF16), grad_ref[...])
    out_ref[:, :width] = grad.astype(BF16)
    both_ref[:, :width] = jnp.concatenate([normed_in, grad], axis=0).astype(BF16)


def token_kernel(after_ref, token_ref):
    del after_ref
    token_ref[...] = jnp.zeros_like(token_ref)


def pass_kernel(block_ref, after_ref, out_ref):
    del after_ref
    out_ref[...] = block_ref[...]


def stacked(refs, half, start, stop):
    cap = SPECIALIST_CAP
    pieces = []
    for ref in refs:
        block = ref[:, start:stop].astype(F32)
        pieces.append(block if ref.shape[0] == cap else block[half * cap : (half + 1) * cap])
    return jnp.concatenate(pieces, axis=0)


def project_kernel(*refs):
    *blocks, token_ref, slab_ref, slab_two_ref, pre_ref, pre_two_ref, first_ref, last_ref = refs
    del token_ref
    width = slab_ref.shape[1]
    rows = stacked(blocks, 0, 0, width).astype(BF16)
    half = first_ref.shape[0]
    pre_ref[...] = rows_product(rows, slab_ref[...])
    pre_two_ref[...] = rows_product(rows, slab_two_ref[...])
    first_ref[...] = rows[:half]
    last_ref[...] = rows[half:]


def hidden_kernel(*refs):
    in_blocks, blocks, refs = refs[:4], refs[4:8], refs[8:]
    pre_ref, pre_two_ref, slab_ref, down_ref, slab_two_ref, down_two_ref, *refs = refs
    own_ref, other_ref, first_ref, last_ref, keep_ref, send_ref = refs
    hidden, width = down_ref.shape
    half = own_ref.shape[0]
    rows = stacked(blocks, 1, 0, width).astype(BF16)
    weight = stacked(in_blocks, 0, width, width + LANES)[:, :1]
    total, comb = 0.0, 0.0
    for slab, down, pre, left_ref in (
        (slab_ref[...], down_ref[...], pre_ref[...], keep_ref),
        (slab_two_ref[...], down_two_ref[...], pre_two_ref[...], send_ref),
    ):
        back = rows_product(rows, down)
        gate = pre[:, :hidden]
        up = pre[:, hidden:]
        sig = jax.nn.sigmoid(gate)
        active = gate * sig
        act = active * up
        into = weight * back
        both = jnp.concatenate(
            [into * up * sig * (1.0 + gate * (1.0 - sig)), into * active], axis=1
        )
        total = total + take_rows(both.astype(BF16), slab)
        part = jnp.sum(act * back, axis=1, keepdims=True)
        comb = comb + part.astype(BF16).astype(F32)
        left_ref[:, : 2 * hidden] = both.astype(BF16)
        left_ref[:, 2 * hidden : 3 * hidden] = (weight * act).astype(BF16)
        left_ref[:, 3 * hidden :] = jnp.zeros(
            (left_ref.shape[0], left_ref.shape[1] - 3 * hidden), BF16
        )
    other_ref[:, :width] = total[half:].astype(BF16)
    own_ref[:, :width] = total[:half].astype(BF16)
    comb = jnp.broadcast_to(comb, (2 * half, LANES))
    high = comb.astype(BF16).astype(F32)
    lane = lax.broadcasted_iota(jnp.int32, comb.shape, 1)
    comb = jnp.where(lane < LANES // 2, high, comb - high).astype(BF16)
    other_ref[:, width:] = comb[half:]
    own_ref[:, width:] = comb[:half]
    first_ref[...] = rows[:half]
    last_ref[...] = rows[half:]


def split_kernel(keep_ref, got_ref, normed_ref, in_ref, far_in_ref, far_grad_ref, gain_ref,
                 own_ref, other_ref, own_comb_ref, other_comb_ref):
    cap, width = own_ref.shape
    total = keep_ref[...].astype(F32) + got_ref[...].astype(F32)
    gain = gain_ref[...]
    far = far_in_ref[...].astype(F32)
    extra = jnp.concatenate([in_ref[:, width:].astype(F32), far[:, width:]], axis=0)
    rms = extra[:, 1:2] + extra[:, 2:3] + extra[:, 3:4]
    normed = jnp.concatenate([normed_ref[...], far[:, :width] / gain], axis=0)
    scaled = total[:, :width] * gain
    inner = jnp.mean(scaled * normed, axis=-1, keepdims=True)
    change = (scaled - normed * inner) / rms
    other_ref[:, :width] = change[cap:].astype(BF16)
    other_ref[:, width:] = far_grad_ref[:, width:]
    own_ref[...] = change[:cap].astype(BF16)
    comb = total[:, width:]
    comb = comb + pltpu.roll(comb, LANES // 2, 1)
    other_comb_ref[...] = comb[cap:]
    own_comb_ref[...] = comb[:cap]


def weights_kernel(chunks, *refs):
    ins, grads, refs = refs[:4], refs[4:8], refs[8:]
    keep_ref, got_ref, after_ref, both_hbm, act_hbm, both_ref, act_ref, sems = refs
    del after_ref
    hidden, width = act_ref.shape
    left = jnp.concatenate([keep_ref[...], got_ref[...]], axis=0).astype(F32).T
    both = left[: 2 * hidden].astype(BF16)
    act = left[2 * hidden : 3 * hidden].astype(BF16)
    chunk = width // chunks
    copies = []
    for number in range(chunks):
        columns = slice(number * chunk, (number + 1) * chunk)
        for which, (left_rows, blocks, ref, hbm) in enumerate(
            ((both, ins, both_ref, both_hbm), (act, grads, act_ref, act_hbm))
        ):
            rows = jnp.concatenate([r[:, columns] for r in blocks], axis=0)
            ref[:, columns] = take_rows(left_rows, rows).astype(BF16)
            copy = pltpu.make_async_copy(
                ref.at[:, columns], hbm.at[:, columns], sems.at[2 * number + which]
            )
            copy.start()
            copies.append(copy)
    for copy in copies:
        copy.wait()


def weight_grads(blocks, keep, got, after, hidden, width):
    chunks = 8
    return pl.pallas_call(
        functools.partial(weights_kernel, chunks),
        in_specs=[IN_VMEM] * (len(blocks) + 2) + [pl.BlockSpec(memory_space=pl.ANY)],
        out_specs=[IN_HBM] * 2,
        out_shape=[
            jax.ShapeDtypeStruct((2 * hidden, width), BF16),
            jax.ShapeDtypeStruct((hidden, width), BF16),
        ],
        scratch_shapes=[
            pltpu.VMEM((2 * hidden, width), BF16),
            pltpu.VMEM((hidden, width), BF16),
            pltpu.SemaphoreType.DMA((2 * chunks,)),
        ],
        compiler_params=pltpu.CompilerParams(vmem_limit_bytes=24 << 20),
        cost_estimate=pl.CostEstimate(
            flops=6 * 64 * hidden * width, bytes_accessed=6 * hidden * width, transcendentals=0
        ),
    )(*blocks, keep, got, after)


def finish_kernel(other_ref, own_ref, grad_ref, out_ref):
    width = grad_ref.shape[1]
    place = other_ref[:, width:]
    grad = grad_ref[...]
    own = take_rows(place, grad)
    change = own_ref[...].astype(F32) + other_ref[:, :width].astype(F32)
    rows = (own + change).astype(BF16)
    back = place.astype(F32).T
    spread = take_rows(back.astype(BF16), rows)
    named = jnp.sum(back, axis=1, keepdims=True) > 0.0
    out_ref[...] = jnp.where(named, spread, grad.astype(F32)).astype(BF16)


def combine_kernel(own_comb_ref, other_comb_ref, ids_ref, place_ref, after_ref, comb_ref):
    del after_ref
    comb = own_comb_ref[...] + other_comb_ref[...]
    comb = jnp.sum(place_ref[...] * comb, axis=0, keepdims=True)
    comb_ref[...] = jnp.where(ids_ref[...] == 0, comb, 0.0)


def on_one(hidden_in, out_grad, expert_ids, route_weight, norm_gain, w_gate_up, w_down):
    sections = lax.axis_size("pipe")
    devices = lax.axis_size("expert")
    tokens, width = hidden_in.shape[1:]
    hidden = w_down.shape[2]
    cap = SPECIALIST_CAP
    ids = expert_ids[0].T
    weights = route_weight[0].T
    slab = w_gate_up.reshape(2 * hidden, width)
    down = w_down.reshape(hidden, width)
    in_hbm = lambda a: pltpu.with_memory_space_constraint(a, pltpu.HBM)
    wide = width + LANES
    total_rows = devices * cap

    def across(block, offset):
        return lax.ppermute(block, "expert", [(i, i ^ (2 * offset)) for i in range(devices)])

    def beside(block):
        return lax.ppermute(block, "expert", [(i, i ^ 1) for i in range(devices)])

    def handed(block, offset):
        route = [
            (((p + 1) % sections) * devices + i, p * devices + (i ^ (2 * offset)))
            for p in range(sections)
            for i in range(devices)
        ]
        return lax.ppermute(block, ("pipe", "expert"), route)

    next_grad = handed(out_grad[0], 0)
    row_in, row_grad, row_both, normed, place = call(
        rows_kernel,
        [((cap, wide), BF16)] * 2
        + [((2 * cap, wide), BF16), ((cap, width), F32), ((cap, tokens), F32)],
        4 * tokens * width * cap,
        4 * tokens * width,
        in_specs=[IN_HBM] * 5,
        scratch=[
            pltpu.VMEM(ids.shape, ids.dtype),
            pltpu.VMEM(weights.shape, weights.dtype),
            pltpu.VMEM(norm_gain.shape, norm_gain.dtype),
            pltpu.VMEM((tokens, width), BF16),
            pltpu.VMEM((tokens, width), BF16),
            pltpu.SemaphoreType.DMA((5,)),
        ],
    )(*map(in_hbm, (ids, weights, norm_gain, hidden_in[0], out_grad[0])))
    far_in = across(row_in, 2)
    far_grad = across(row_grad, 2)
    slab_two, down_two = beside(slab), beside(down)
    (passed,) = call(
        pass_kernel,
        [(row_both.shape, BF16)],
        0,
        4 * cap * wide,
        in_specs=[IN_VMEM] + [pl.BlockSpec(memory_space=pl.ANY)],
    )(row_both, slab_two)
    near = across(passed, 1)
    (token,) = call(
        token_kernel,
        [((cap, LANES), F32)],
        TOKEN_FLOPS,
        0,
        in_specs=[pl.BlockSpec(memory_space=pl.ANY)],
    )(far_grad)
    farthest_in = across(far_in, 1)
    farthest_grad = across(far_grad, 1)
    ins = [row_in, far_in, near, farthest_in]
    grads = [row_grad, far_grad, near, farthest_grad]
    half_rows = ((2 * cap, width), BF16)
    pre, pre_two, *in_halves = call(
        project_kernel,
        [((total_rows // 2, 2 * hidden), F32)] * 2 + [half_rows] * 2,
        0,
        4 * hidden * width,
    )(*ins, token, slab, slab_two)
    left_width = -(-3 * hidden // LANES) * LANES
    own_half, other_half, *rest = call(
        hidden_kernel,
        [((2 * cap, wide), BF16)] * 2
        + [half_rows] * 2
        + [((total_rows // 2, left_width), BF16)] * 2,
        HIDDEN_FLOPS,
        6 * hidden * width,
    )(*ins, *grads, pre, pre_two, slab, down, slab_two, down_two)
    *grad_halves, left_keep, left_send = rest
    own, other, own_comb, other_comb = call(
        split_kernel,
        [((cap, width), BF16), ((cap, wide), BF16)] + [((cap, LANES), F32)] * 2,
        2 * cap * width,
        8 * cap * width,
    )(own_half, across(other_half, 1), normed, row_in, far_in, far_grad, norm_gain)
    blocks = in_halves + [beside(b) for b in in_halves]
    blocks += grad_halves + [beside(b) for b in grad_halves]
    gate_up_out, down_out = weight_grads(blocks, left_keep, beside(left_send), own, hidden, width)
    (out,) = call(
        finish_kernel, [((tokens, width), BF16)], 4 * tokens * width * cap, 4 * tokens * width
    )(handed(other, 2), handed(own, 0), next_grad)
    (combined,) = call(
        combine_kernel,
        [((SPLIT, tokens), F32)],
        0,
        4 * SPLIT * tokens,
        in_specs=[IN_VMEM] * 4 + [IN_HBM],
    )(own_comb, across(other_comb, 2), ids, place, in_hbm(out))
    return (
        out[None],
        gate_up_out.reshape(1, 1, 2, hidden, width),
        down_out.reshape(1, 1, hidden, width),
        combined.T[None],
    )


def solution(mesh):
    on_device = on_one if mesh.shape["expert"] == SPLIT else on_many
    return jax.shard_map(
        on_device,
        mesh=mesh,
        in_specs=(
            P("pipe", "expert", None),
            P("pipe", "expert", None),
            P("pipe", "expert", None),
            P("pipe", "expert", None),
            P("pipe", None),
            P("pipe", "expert", None, None, None),
            P("pipe", "expert", None, None),
        ),
        out_specs=(
            P("pipe", "expert", None),
            P("pipe", "expert", None, None, None),
            P("pipe", "expert", None, None),
            P("pipe", "expert", None),
        ),
        check_vma=False,
    )
```
